32 devices in a mesh: dp: 4 (over y, x), hid: 4 (over z), mod: 2 (over core).
Axes of the slice: x: 2, y: 2, z: 4, core: 2. Of those that a mesh axis runs over, the one named last changes fastest.
Arguments:
- tokens: bfloat16 [32768, 768], P(('dp', 'hid', 'mod')), may hold values from -6 to 6
- clusters: int32 [32768, 12], P(('dp', 'hid', 'mod')), may hold values from 0 to 99
- key_mask: int32 [32768], P(('dp', 'hid', 'mod')), may hold values from 0 to 1, as said below
- query_key_value_weight: bfloat16 [768, 2304], replicated, may hold values from -0.5 to 0.5
- attention_output_weight: bfloat16 [768, 768], replicated, may hold values from -0.4375 to 0.4375
- up_weight: bfloat16 [768, 3072], P('mod', 'hid'), may hold values from -0.21875 to 0.21875
- down_weight: bfloat16 [3072, 768], P('hid', 'mod'), may hold values from -0.109375 to 0.109375
- gain_one: float32 [768], replicated, may hold values from 0.1 to 1.9
- shift_one: float32 [768], replicated, may hold values from -3 to 3
- gain_two: float32 [768], replicated, may hold values from 0.1 to 1.9
- shift_two: float32 [768], replicated, may hold values from -3 to 3
- cotangent: bfloat16 [32768, 768], P(('dp', 'hid', 'mod')), may hold values from -6 to 6
Outputs:
- output: bfloat16 [32768, 768], P(('dp', 'hid', 'mod'))
- input_grad: bfloat16 [32768, 768], P(('dp', 'hid', 'mod'))
- grad_qkv: float32 [768, 2304], replicated
- grad_out: float32 [768, 768], replicated
- grad_in: float32 [768, 3072], P('mod', 'hid')
- grad_back: float32 [3072, 768], P('hid', 'mod')
- grad_gain_one: float32 [768], replicated
- grad_shift_one: float32 [768], replicated
- grad_gain_two: float32 [768], replicated
- grad_shift_two: float32 [768], replicated
The draws below stay inside these ranges and needn't reach their ends.
Inputs may be any that keep to these rules, and one draw needn't show every extreme that they name: `key_mask`: the first position of each sequence of 1024 tokens is always 1.
All inputs are finite; a program needn't handle non-finite values.
Results may differ from the reference program's by a relative error of at most 0.019.
Values may be sent and summed in bfloat16 or wider, within the bound.
No kernel may reach another device: no remote copies, remote signals or barrier semaphores. Data moves between devices by JAX's collectives and lax.ppermute only.
A program may use at most 192 MiB of HBM per device.

```python
import math
import jax
import jax.numpy as jnp
from jax import lax

D = 768
H = 12
DH = 64
FF = 3072
C = 100
LEN = 1024
TOKENS = 32768


def draw_key_mask(key, part):
    key = jax.random.fold_in(key, 11)
    first_key, second_key = jax.random.split(key)
    total_seqs = TOKENS // LEN
    rates = jax.random.randint(first_key, (total_seqs, 1), 5, 26)
    rolls = jax.random.randint(second_key, (total_seqs, LEN), 0, 100)
    kept = (rolls >= rates).astype(jnp.int32)
    leading = (jnp.arange(LEN, dtype=jnp.int32) == 0)[None, :]
    return jnp.where(leading, 1, kept).reshape(TOKENS).astype(jnp.int32)


def with_ends(entries, own_key, smallest, top_value):
    longest = entries.shape.index(max(entries.shape))
    spots = []
    for shift in (0, 1):
        where = [jax.random.randint(jax.random.fold_in(own_key, axis), (), 0, length) for axis, length in enumerate(entries.shape)]
        where[longest] = (where[longest] + shift) % entries.shape[longest]
        spots.append(tuple(where))
    return entries.at[spots[0]].set(smallest).at[spots[1]].set(top_value)


def shard_levels(own_key, extent, pieces, low, high):
    def one(axis_at, shards_of):
        steps = jax.random.uniform(jax.random.fold_in(jax.random.fold_in(own_key, 6), axis_at), (shards_of,), jnp.float32, low / len(pieces), high / len(pieces))
        return jnp.repeat(jnp.exp(steps), extent[axis_at] // shards_of).reshape((-1,) + (1,) * (len(extent) - axis_at - 1))

    loudness = one(*pieces[0])
    for cut in pieces[1:]:
        loudness = loudness * one(*cut)
    return loudness


def normal_values(key, shape, deviation, bound, pieces=(), kind=jnp.bfloat16):
    drawn = jax.random.normal(key, shape, jnp.float32) * deviation
    if len(pieces) > 0:
        drawn = shard_levels(key, shape, pieces, -0.22, 0.18) * drawn
    return jnp.clip(drawn, min=-bound, max=bound).astype(kind)


def setup_inputs(seed: int = 0) -> dict:
    seeds = jax.random.split(jax.random.key(seed), 13)
    tokens = normal_values(seeds[0], (TOKENS, D), 1.0, 6.0, ((0, 32),))
    clusters = with_ends(jax.random.randint(seeds[1], (TOKENS, H), 0, C), jax.random.fold_in(seeds[1], 1), 0, C - 1).astype(jnp.int32)
    key_mask = draw_key_mask(jax.random.fold_in(seeds[12], 71), 0)
    query_key_value_weight = normal_values(seeds[3], (D, 3 * D), (D // 6) ** -0.5, 0.5)
    attention_output_weight = normal_values(seeds[4], (D, D), (D // 4) ** -0.5, 0.4375)
    up_weight = normal_values(seeds[5], (D, FF), D ** -0.5, 0.21875, ((0, 2), (1, 4)))
    down_weight = normal_values(seeds[6], (FF, D), FF ** -0.5, 0.109375, ((0, 4), (1, 2)))
    gain_one = jnp.clip(1.0 + 0.18 * jax.random.normal(seeds[7], (D,), jnp.float32), 0.1, 1.9)
    shift_one = normal_values(seeds[8], (D,), 0.3, 3.0, (), jnp.float32)
    gain_two = jnp.clip(1.0 + 0.18 * jax.random.normal(seeds[9], (D,), jnp.float32), 0.1, 1.9)
    shift_two = normal_values(seeds[10], (D,), 0.3, 3.0, (), jnp.float32)
    cotangent = normal_values(seeds[11], (TOKENS, D), 1.0, 6.0, ((0, 32),))
    return dict(tokens=tokens, clusters=clusters, key_mask=key_mask, query_key_value_weight=query_key_value_weight, attention_output_weight=attention_output_weight, up_weight=up_weight, down_weight=down_weight, gain_one=gain_one, shift_one=shift_one, gain_two=gain_two, shift_two=shift_two, cotangent=cotangent)


EPSILON = 1e-05
NEGATIVE = -1e+30
FULL_PRECISION = lax.Precision.HIGHEST

@jax.custom_vjp
def low(v):
    return lax.optimization_barrier(v.astype(jnp.bfloat16)).astype(jnp.float32)

@jax.custom_vjp
def reduced_precision_backward(v):
    return v

def low_keep(v):
    return (low(v), None)

def low_pass(kept, grad):
    return (grad,)

def back_keep(v):
    return (v, None)

def back_low(kept, grad):
    return (low(grad),)
low.defvjp(low_keep, low_pass)
reduced_precision_backward.defvjp(back_keep, back_low)

def normalize(inputs, gain_vec, shift_vec):
    row_mean = lax.optimization_barrier(jnp.mean(inputs, axis=-1, keepdims=True))
    centered = inputs - row_mean
    row_var = lax.optimization_barrier(jnp.mean(centered * centered, axis=-1, keepdims=True))
    return centered * lax.rsqrt(row_var + EPSILON) * gain_vec + shift_vec

def forward_pass(inputs, query_key_value_weight, attention_output_weight, up_weight, down_weight, gain_one, shift_one, gain_two, shift_two, member, keep_mask):
    group_seqs = inputs.shape[0]
    first_normalized_input = low(normalize(inputs, gain_one, shift_one))
    output_projected = jnp.einsum('zmr,rj->zmj', first_normalized_input, query_key_value_weight, precision=FULL_PRECISION)
    output_projected = reduced_precision_backward(low(output_projected)).reshape(group_seqs, LEN, 3, H, DH)
    query = output_projected[:, :, 0]
    key_part = output_projected[:, :, 1]
    value_part = output_projected[:, :, 2]
    counts = jnp.maximum(lax.optimization_barrier(jnp.sum(member, axis=1)), 1.0)
    summed = jnp.einsum('slhc,slhd->shcd', member, query, precision=FULL_PRECISION)
    centre = reduced_precision_backward(low(summed / counts[..., None]))
    raw_scores = jnp.einsum('shcd,slhd->shcl', centre, key_part, precision=FULL_PRECISION) * DH ** (-0.5)
    raw_scores = reduced_precision_backward(raw_scores)
    scores = jnp.where(keep_mask[:, None, None, :], raw_scores, NEGATIVE)
    top_score = lax.optimization_barrier(jnp.max(scores, axis=-1, keepdims=True))
    powered = jnp.exp(scores - top_score)
    probability = powered / lax.optimization_barrier(jnp.sum(powered, axis=-1, keepdims=True))
    centre_out = jnp.einsum('shcl,slhd->shcd', low(probability), value_part, precision=FULL_PRECISION)
    centre_out = reduced_precision_backward(low(centre_out))
    attention_mixture = jnp.einsum('slhc,shcd->slhd', member, centre_out, precision=FULL_PRECISION)
    attention_mixture = reduced_precision_backward(attention_mixture).reshape(group_seqs, LEN, H * DH)
    attention_result = reduced_precision_backward(jnp.einsum('zmr,rj->zmj', attention_mixture, attention_output_weight, precision=FULL_PRECISION))
    residual_stream = inputs + attention_result
    second_normalized_input = low(normalize(residual_stream, gain_two, shift_two))
    hidden_before_activation = reduced_precision_backward(jnp.einsum('kpj,jh->kph', second_normalized_input, up_weight, precision=FULL_PRECISION))
    hidden_activation = low(jax.nn.gelu(hidden_before_activation, approximate=False))
    return residual_stream + jnp.einsum('rwj,ju->rwu', hidden_activation, down_weight, precision=FULL_PRECISION)

def reference(tokens, clusters, key_mask, query_key_value_weight, attention_output_weight, up_weight, down_weight, gain_one, shift_one, gain_two, shift_two, cotangent):
    total_seqs = TOKENS // LEN
    group_seqs = math.gcd(total_seqs, max(1, 4096 // LEN))
    groups = total_seqs // group_seqs
    inputs = tokens.astype(jnp.float32).reshape(groups, group_seqs, LEN, D)
    member = (clusters.reshape(groups, group_seqs, LEN, H, 1) == jnp.arange(C, dtype=jnp.int32)).astype(jnp.float32)
    keep_mask = key_mask.reshape(groups, group_seqs, LEN) == 1
    cot_rows = cotangent.astype(jnp.float32).reshape(groups, group_seqs, LEN, D)
    weights = (query_key_value_weight.astype(jnp.float32), attention_output_weight.astype(jnp.float32), up_weight.astype(jnp.float32), down_weight.astype(jnp.float32), gain_one.astype(jnp.float32), shift_one.astype(jnp.float32), gain_two.astype(jnp.float32), shift_two.astype(jnp.float32))

    def step_group(totals, block_data):
        block_inputs, block_member, block_keep, block_cot = block_data

        def apply_layer(layer_inputs, *params):
            return forward_pass(layer_inputs, *params, block_member, block_keep)
        outputs, pullback = jax.vjp(apply_layer, block_inputs, *weights)
        gradients = pullback(block_cot)
        totals = tuple((running + gradient for running, gradient in zip(totals, gradients[1:])))
        return (totals, (outputs.astype(jnp.bfloat16), gradients[0].astype(jnp.bfloat16)))
    initial = tuple((jnp.zeros_like(weight) for weight in weights))
    totals, (outputs, input_grads) = lax.scan(step_group, initial, (inputs, member, keep_mask, cot_rows))
    return (outputs.reshape(TOKENS, D), input_grads.reshape(TOKENS, D), totals[0], totals[1], totals[2], totals[3], totals[4], totals[5], totals[6], totals[7])
```

```python
import functools

import jax
import jax.numpy as jnp
from jax import lax
from jax.experimental import pallas as pl
from jax.experimental.pallas import tpu as pltpu
from jax.sharding import PartitionSpec as P

H = 12
DH = 64
C = 100
LEN = 1024
LANES = 128
GROUP = 4
WIDE = GROUP * DH

EPSILON = 1e-05
NEGATIVE = -1e30
MIB = 2**20
f32 = jnp.float32
bf16 = jnp.bfloat16

NN = (((1,), (0,)), ((), ()))
NT = (((1,), (1,)), ((), ()))
TN = (((0,), (0,)), ((), ()))
ANY = pl.BlockSpec(memory_space=pl.ANY)


def mm(a, b, dims=NN):
    return lax.dot_general(a, b, dims, preferred_element_type=f32)


def row_stats(x):
    mean = jnp.mean(x, axis=-1, keepdims=True)
    centered = x - mean
    var = jnp.mean(centered * centered, axis=-1, keepdims=True)
    r = lax.rsqrt(var + EPSILON)
    return centered * r, r


def norm_back(g, gain, xhat, r):
    gx = g * gain
    return r * (
        gx
        - jnp.mean(gx, axis=-1, keepdims=True)
        - xhat * jnp.mean(gx * xhat, axis=-1, keepdims=True)
    )


def member_pair(cl, p):
    rows = cl.shape[0]
    lane = lax.broadcasted_iota(jnp.int32, (rows, LANES), 1)
    halves = [(cl[:, 2 * p + i : 2 * p + i + 1] == lane).astype(f32) for i in (0, 1)]
    return jnp.concatenate(halves, axis=1)


def pair_mask():
    d = lax.broadcasted_iota(jnp.int32, (2 * DH, 2 * LANES), 0)
    c = lax.broadcasted_iota(jnp.int32, (2 * DH, 2 * LANES), 1)
    return ((d >= DH) == (c >= LANES)).astype(f32)


def forward_body(
    tok, cl, keep, wq, wk, wv, wo, g1, s1, g2, s2,
    n1, k_out, v_out, mixed, prob, cen, cnt, res, n2,
    acc,
):
    step = pl.program_id(0)
    tile = 256
    rows = tok.shape[0]

    @pl.when(step == 0)
    def _():
        def first_norm(i, _):
            at = pl.ds(pl.multiple_of(i * tile, tile), tile)
            xhat, _r = row_stats(tok[at, :].astype(f32))
            n1[at, :] = (xhat * g1[...] + s1[...]).astype(bf16)
            return 0

        lax.fori_loop(0, rows // tile, first_norm, 0)

    q = mm(n1[...], wq[...]).astype(bf16)
    k = mm(n1[...], wk[...]).astype(bf16)
    v = mm(n1[...], wv[...]).astype(bf16)
    k_out[...] = k
    v_out[...] = v
    same = pair_mask()
    kept = keep[...] == 1
    parts = []
    for p in range(GROUP // 2):
        cols = slice(2 * DH * p, 2 * DH * (p + 1))
        m32 = member_pair(cl[0], p)
        m = m32.astype(bf16)
        count = jnp.maximum(jnp.sum(m32, axis=0, keepdims=True), 1.0)
        centre = (mm(q[:, cols], m, TN) / count * same).astype(bf16)
        score = mm(k[:, cols], centre) * (DH**-0.5)
        score = jnp.where(kept, score, NEGATIVE)
        powered = jnp.exp(score - jnp.max(score, axis=0, keepdims=True))
        pr = (powered * (1.0 / jnp.sum(powered, axis=0, keepdims=True))).astype(bf16)
        centre_out = (mm(v[:, cols], pr, TN) * same).astype(bf16)
        parts.append(mm(m, centre_out, NT).astype(bf16))
        prob[:, 2 * LANES * p : 2 * LANES * (p + 1)] = pr
        cen[p] = centre
        cnt[p] = count
    mix = jnp.concatenate(parts, axis=1)
    mixed[...] = mix
    part = mm(mix, wo[...])

    @pl.when(step == 0)
    def _():
        acc[...] = part

    @pl.when(step > 0)
    def _():
        acc[...] += part

    @pl.when(step == pl.num_programs(0) - 1)
    def _():
        def second_norm(i, _):
            at = pl.ds(pl.multiple_of(i * tile, tile), tile)
            x = tok[at, :].astype(f32) + acc[at, :]
            res[at, :] = x
            xhat, _r = row_stats(x)
            n2[at, :] = (xhat * g2[...] + s2[...]).astype(bf16)
            return 0

        lax.fori_loop(0, rows // tile, second_norm, 0)


def whole(shape):
    return pl.BlockSpec(shape, lambda g: (0,) * len(shape))


def attention_forward(tokens, cl3, keep, wqkv, wo, g1, s1, g2, s2):
    rows, width = tokens.shape
    steps = H // GROUP
    pairs = GROUP // 2
    vec = whole((1, width))
    col = lambda off: pl.BlockSpec((width, WIDE), lambda g: (0, off + g))
    tall = pl.BlockSpec((rows, WIDE), lambda g: (0, g))
    sds = jax.ShapeDtypeStruct
    return pl.pallas_call(
        forward_body,
        grid=(steps,),
        in_specs=[
            whole((rows, width)),
            pl.BlockSpec((1, rows, GROUP), lambda g: (g, 0, 0)),
            whole((rows, 1)),
            col(0), col(steps), col(2 * steps),
            pl.BlockSpec((WIDE, width), lambda g: (g, 0)),
            vec, vec, vec, vec,
        ],
        out_specs=(
            whole((rows, width)),
            tall, tall, tall,
            pl.BlockSpec((rows, GROUP * LANES), lambda g: (0, g)),
            pl.BlockSpec((pairs, 2 * DH, 2 * LANES), lambda g: (g, 0, 0)),
            pl.BlockSpec((pairs, 1, 2 * LANES), lambda g: (g, 0, 0)),
            whole((rows, width)),
            whole((rows, width)),
        ),
        out_shape=(
            sds((rows, width), bf16),
            sds((rows, width), bf16),
            sds((rows, width), bf16),
            sds((rows, width), bf16),
            sds((rows, H * LANES), bf16),
            sds((H // 2, 2 * DH, 2 * LANES), bf16),
            sds((H // 2, 1, 2 * LANES), f32),
            sds((rows, width), f32),
            sds((rows, width), bf16),
        ),
        scratch_shapes=[pltpu.VMEM((rows, width), f32)],
        compiler_params=pltpu.CompilerParams(vmem_limit_bytes=56 * MIB),
        name="attention_forward",
    )(tokens, cl3, keep, wqkv, wqkv, wqkv, wo, g1, s1, g2, s2)


def backward_body(
    gn2, cot, res, tok, n1, k_in, v_in, mixed, prob, cen, cnt, cl, wq, wk, wv, wo, g1, g2,
    gq_w, gk_w, gv_w, go_w, dx, vecs,
    gres, ga, acc,
):
    step = pl.program_id(0)
    tile = 256
    rows, width = tok.shape

    @pl.when(step == 0)
    def _():
        def second_norm(i, carry):
            at = pl.ds(pl.multiple_of(i * tile, tile), tile)
            g = gn2[at, :]
            xhat, r = row_stats(res[at, :])
            out = cot[at, :].astype(f32) + norm_back(g, g2[...], xhat, r)
            gres[at, :] = out
            ga[at, :] = out.astype(bf16)
            return (
                carry[0] + jnp.sum(g * xhat, axis=0, keepdims=True),
                carry[1] + jnp.sum(g, axis=0, keepdims=True),
            )

        zero = jnp.zeros((1, width), f32)
        gain, shift = lax.fori_loop(0, rows // tile, second_norm, (zero, zero))
        vecs[2:3, :] = gain
        vecs[3:4, :] = shift
        vecs[4:8, :] = jnp.zeros((4, width), f32)

    go_w[...] = mm(mixed[...], ga[...], TN).astype(bf16)
    gm = mm(ga[...], wo[...], NT).astype(bf16)
    same = pair_mask()
    gqs, gks, gvs = [], [], []
    for p in range(GROUP // 2):
        cols = slice(2 * DH * p, 2 * DH * (p + 1))
        m = member_pair(cl[0], p).astype(bf16)
        centre = cen[p]
        gco = (mm(gm[:, cols], m, TN) * same).astype(bf16)
        pr = prob[:, 2 * LANES * p : 2 * LANES * (p + 1)]
        gvs.append(mm(pr, gco, NT).astype(bf16))
        pr32 = pr.astype(f32)
        weighted = pr32 * mm(v_in[:, cols], gco)
        gs = (weighted - pr32 * jnp.sum(weighted, axis=0, keepdims=True)).astype(bf16)
        gc = (mm(k_in[:, cols], gs, TN) * (same * DH**-0.5)).astype(bf16)
        gc = (gc.astype(f32) / cnt[p]).astype(bf16)
        gks.append((mm(gs, centre, NT) * (DH**-0.5)).astype(bf16))
        gqs.append(mm(m, gc, NT).astype(bf16))
    gq = jnp.concatenate(gqs, axis=1)
    gk = jnp.concatenate(gks, axis=1)
    gv = jnp.concatenate(gvs, axis=1)
    gq_w[...] = mm(n1[...], gq, TN).astype(bf16)
    gk_w[...] = mm(n1[...], gk, TN).astype(bf16)
    gv_w[...] = mm(n1[...], gv, TN).astype(bf16)
    part = mm(gq, wq[...], NT) + mm(gk, wk[...], NT) + mm(gv, wv[...], NT)

    @pl.when(step == 0)
    def _():
        acc[...] = part

    @pl.when(step > 0)
    def _():
        acc[...] += part

    @pl.when(step == pl.num_programs(0) - 1)
    def _():
        def first_norm(i, carry):
            at = pl.ds(pl.multiple_of(i * tile, tile), tile)
            g = acc[at, :]
            xhat, r = row_stats(tok[at, :].astype(f32))
            dx[at, :] = (gres[at, :] + norm_back(g, g1[...], xhat, r)).astype(bf16)
            return (
                carry[0] + jnp.sum(g * xhat, axis=0, keepdims=True),
                carry[1] + jnp.sum(g, axis=0, keepdims=True),
            )

        zero = jnp.zeros((1, width), f32)
        gain, shift = lax.fori_loop(0, rows // tile, first_norm, (zero, zero))
        vecs[0:1, :] = gain
        vecs[1:2, :] = shift


def attention_backward(gn2, cot, res, tok, n1, k, v, mixed, prob, cen, cnt, cl3, wqkv, wo, g1, g2):
    rows, width = tok.shape
    steps = H // GROUP
    pairs = GROUP // 2
    vec = whole((1, width))
    full = whole((rows, width))
    col = lambda off: pl.BlockSpec((width, WIDE), lambda g: (0, off + g))
    tall = pl.BlockSpec((rows, WIDE), lambda g: (0, g))
    sds = jax.ShapeDtypeStruct
    return pl.pallas_call(
        backward_body,
        grid=(steps,),
        in_specs=[
            full, full, full, full, full,
            tall, tall, tall,
            pl.BlockSpec((rows, GROUP * LANES), lambda g: (0, g)),
            pl.BlockSpec((pairs, 2 * DH, 2 * LANES), lambda g: (g, 0, 0)),
            pl.BlockSpec((pairs, 1, 2 * LANES), lambda g: (g, 0, 0)),
            pl.BlockSpec((1, rows, GROUP), lambda g: (g, 0, 0)),
            col(0), col(steps), col(2 * steps),
            pl.BlockSpec((WIDE, width), lambda g: (g, 0)),
            vec, vec,
        ],
        out_specs=(
            pl.BlockSpec((width, WIDE), lambda g: (0, g)),
            pl.BlockSpec((width, WIDE), lambda g: (0, g)),
            pl.BlockSpec((width, WIDE), lambda g: (0, g)),
            pl.BlockSpec((WIDE, width), lambda g: (g, 0)),
            full,
            whole((8, width)),
        ),
        out_shape=(
            sds((width, width), bf16),
            sds((width, width), bf16),
            sds((width, width), bf16),
            sds((width, width), bf16),
            sds((rows, width), bf16),
            sds((8, width), f32),
        ),
        scratch_shapes=[
            pltpu.VMEM((rows, width), f32),
            pltpu.VMEM((rows, width), bf16),
            pltpu.VMEM((rows, width), f32),
        ],
        compiler_params=pltpu.CompilerParams(vmem_limit_bytes=58 * MIB),
        name="attention_backward",
    )(gn2, cot, res, tok, n1, k, v, mixed, prob, cen, cnt, cl3, wqkv, wqkv, wqkv, wo, g1, g2)


def gelu_parts(x):
    t = 1.0 / (1.0 + (0.3275911 * 0.5**0.5) * jnp.abs(x))
    e = jnp.exp(-0.5 * x * x)
    poly = t * (
        0.254829592
        + t * (-0.284496736 + t * (1.421413741 + t * (-1.453152027 + t * 1.061405429)))
    )
    q = 0.5 * poly * e
    phi = jnp.where(x >= 0, 1.0 - q, q)
    return x * phi, phi + x * e * 0.3989422804014327


def forward_slot(first, places, *refs):
    n_w = len(places)
    n2, cot = refs[:2]
    weights = refs[2 : 2 + n_w]
    i = 2 + n_w
    if not first:
        br_in, gn_in = refs[i : i + 2]
        i += 2
    br, gn, own, other = refs[i : i + 4]
    i += 4
    (n2_s, cot_s, n2t_s, cott_s, up_s, down_s, act_s, gp_s, br_s, gn_s, g_s) = refs[i : i + 11]
    load_sem, weight_sem, acc_sem, out_sem = refs[i + 11 :]
    rows, width = n2_s.shape
    hidden = up_s.shape[1]
    half = width // 2
    tile = 512
    core = lax.axis_index("mod")
    spot = lax.rem(lax.axis_index("dp"), 4)

    acts = [
        pltpu.make_async_copy(n2, n2_s, load_sem.at[0]),
        pltpu.make_async_copy(cot, cot_s, load_sem.at[1]),
    ]
    loads = []
    for at, (ref, (is_up, core_rel, spot_rel)) in enumerate(zip(weights, places)):
        d0 = pl.multiple_of((core ^ core_rel) * half, half)
        if spot_rel is None:
            target = up_s.at[pl.ds(d0, half), :] if is_up else down_s.at[:, pl.ds(d0, half)]
        elif is_up:
            n = half // 4
            target = up_s.at[pl.ds(pl.multiple_of(d0 + (spot ^ spot_rel) * n, n), n), :]
        else:
            n = hidden // 4
            target = down_s.at[
                pl.ds(pl.multiple_of((spot ^ spot_rel) * n, n), n), pl.ds(d0, half)
            ]
        loads.append(pltpu.make_async_copy(ref, target, weight_sem.at[at]))
    for copy in acts + loads:
        copy.start()
    if not first:
        sums = [
            pltpu.make_async_copy(br_in, br_s, acc_sem.at[0]),
            pltpu.make_async_copy(gn_in, gn_s, acc_sem.at[1]),
        ]
        for copy in sums:
            copy.start()
    for copy in acts + loads:
        copy.wait()

    def hidden_rows(i, _):
        at = pl.ds(pl.multiple_of(i * tile, tile), tile)
        h = mm(n2_s[at, :], up_s[...])
        ga = mm(cot_s[at, :], down_s[...], NT)
        act, slope = gelu_parts(h)
        act_s[at, :] = act.astype(bf16)
        gp_s[at, :] = (ga * slope).astype(bf16)
        n2t_s[:, at] = n2_s[at, :].T
        cott_s[:, at] = cot_s[at, :].T
        return 0

    lax.fori_loop(0, rows // tile, hidden_rows, 0)
    dtile = half

    def weight_rows(i, _):
        at = pl.ds(pl.multiple_of(i * dtile, dtile), dtile)
        g_s[0, at, :] = mm(n2t_s[at, :], gp_s[...]).astype(bf16)
        g_s[1, at, :] = mm(cott_s[at, :], act_s[...]).astype(bf16)
        return 0

    lax.fori_loop(0, width // dtile, weight_rows, 0)
    outs = []
    for n, (out, rel) in enumerate(((own, 0), (other, 1))):
        at = pl.ds(pl.multiple_of((core ^ rel) * half, half), half)
        outs.append(pltpu.make_async_copy(g_s.at[:, at, :], out, out_sem.at[n]))
    for copy in outs:
        copy.start()
    if not first:
        for copy in sums:
            copy.wait()

    def token_rows(i, _):
        at = pl.ds(pl.multiple_of(i * tile, tile), tile)
        b = mm(act_s[at, :], down_s[...])
        g = mm(gp_s[at, :], up_s[...], NT)
        if first:
            br_s[at, :] = b
            gn_s[at, :] = g
        else:
            br_s[at, :] += b
            gn_s[at, :] += g
        return 0

    lax.fori_loop(0, rows // tile, token_rows, 0)
    outs.append(pltpu.make_async_copy(br_s, br, out_sem.at[2]))
    outs.append(pltpu.make_async_copy(gn_s, gn, out_sem.at[3]))
    for copy in outs[2:]:
        copy.start()
    for copy in outs:
        copy.wait()


def feed_forward_slot(n2, cot, pieces, sums, hidden):
    rows, width = n2.shape
    half = width // 2
    places = tuple(place for _, place in pieces)
    args = [n2, cot] + [a for a, _ in pieces] + list(sums or ())
    sds = jax.ShapeDtypeStruct
    V = pltpu.VMEM
    D = pltpu.SemaphoreType.DMA
    return pl.pallas_call(
        functools.partial(forward_slot, sums is None, places),
        in_specs=[ANY] * len(args),
        out_specs=(ANY,) * 4,
        out_shape=(
            sds((rows, width), f32),
            sds((rows, width), f32),
            sds((2, half, hidden), bf16),
            sds((2, half, hidden), bf16),
        ),
        scratch_shapes=[
            V((rows, width), bf16),
            V((rows, width), bf16),
            V((width, rows), bf16),
            V((width, rows), bf16),
            V((width, hidden), bf16),
            V((hidden, width), bf16),
            V((rows, hidden), bf16),
            V((rows, hidden), bf16),
            V((rows, width), f32),
            V((rows, width), f32),
            V((2, width, hidden), bf16),
            D((2,)),
            D((len(places),)),
            D((2,)),
            D((4,)),
        ],
        compiler_params=pltpu.CompilerParams(vmem_limit_bytes=56 * MIB),
        name="feed_forward",
    )(*args)


def flip(x, axis, bit):
    n = lax.axis_size(axis)
    return lax.ppermute(x, axis, [(i, i ^ (1 << bit)) for i in range(n)])


def turn(x, axis):
    n = lax.axis_size(axis)
    return lax.ppermute(x, axis, [(i, (i + 1) % n) for i in range(n)])


def take(x, index, n):
    return lax.dynamic_slice_in_dim(x, index * n, n, 0)


def halve(x, axis, bit, mine):
    n = x.shape[0] // 2
    return take(x, mine, n) + flip(take(x, 1 - mine, n), axis, bit)


def join(x, axis, bit, mine):
    y = flip(x, axis, bit)
    return jnp.where(mine == 0, jnp.concatenate([x, y]), jnp.concatenate([y, x]))


def bits(axis):
    return lax.axis_size(axis).bit_length() - 1


def plane_scatter(x, order, spot_bits):
    for b in order:
        x = halve(x, "dp", b, spot_bits[b])
    for b in range(2, bits("dp")):
        x = x + flip(x, "dp", b)
    return x


def plane_gather(x, order, spot_bits):
    for b in reversed(order):
        x = join(x, "dp", b, spot_bits[b])
    return x


def sum_everywhere(x, core, spot_bits):
    x = halve(x, "mod", 0, core)
    n = x.shape[0] // 2
    parts = [plane_scatter(x[:n], (0, 1), spot_bits), plane_scatter(x[n:], (1, 0), spot_bits)]
    x = jnp.concatenate(parts)
    for b in range(bits("hid")):
        x = x + flip(x, "hid", b)
    n = x.shape[0] // 2
    parts = [plane_gather(x[:n], (0, 1), spot_bits), plane_gather(x[n:], (1, 0), spot_bits)]
    return join(jnp.concatenate(parts), "mod", 0, core)


def per_device(
    tokens, clusters, key_mask, query_key_value_weight, attention_output_weight, up_weight,
    down_weight, gain_one, shift_one, gain_two, shift_two, cotangent,
):
    rows, width = tokens.shape
    half = width // 2
    hidden = up_weight.shape[1]
    ring = lax.axis_size("hid")
    core = lax.axis_index("mod")
    spot = lax.rem(lax.axis_index("dp"), 4)
    spot_bits = (spot & 1, spot >> 1)

    slots = [
        [
            (up_weight, (True, 0, None)),
            (down_weight, (False, 0, None)),
            (flip(up_weight, "mod", 0), (True, 1, None)),
            (flip(down_weight, "mod", 0), (False, 1, None)),
        ]
    ]
    a = take(up_weight, spot, half // 4)
    b = take(down_weight, spot, hidden // 4)
    for _ in range(1, ring):
        a, b = turn(a, "hid"), turn(b, "hid")
        ax, by = flip(a, "dp", 0), flip(b, "dp", 1)
        held = [
            (a, (True, 0, 0)),
            (ax, (True, 0, 1)),
            (flip(a, "dp", 1), (True, 0, 2)),
            (flip(ax, "dp", 1), (True, 0, 3)),
            (b, (False, 0, 0)),
            (by, (False, 0, 2)),
            (flip(b, "dp", 0), (False, 0, 1)),
            (flip(by, "dp", 0), (False, 0, 3)),
        ]
        held += [(flip(x, "mod", 0), (is_up, 1, s)) for x, (is_up, _, s) in held]
        slots.append(held)

    cl3 = clusters.reshape(rows, H // GROUP, GROUP).transpose(1, 0, 2)
    keep = key_mask.reshape(rows, 1)
    vec = lambda x: x.reshape(1, width)
    g1, s1, g2, s2 = vec(gain_one), vec(shift_one), vec(gain_two), vec(shift_two)
    n1, k, v, mixed, prob, cen, cnt, res, n2 = attention_forward(
        tokens, cl3, keep, query_key_value_weight, attention_output_weight, g1, s1, g2, s2
    )

    sums = None
    shares = []
    for pieces in slots:
        *sums, own, other = feed_forward_slot(n2, cotangent, pieces, sums, hidden)
        part = own + flip(other, "mod", 0)
        shares.append(
            jnp.stack(
                [
                    plane_scatter(part[0], (0, 1), spot_bits),
                    plane_scatter(part[1], (1, 0), spot_bits),
                ]
            )
        )
    branch, gn2 = sums
    output = (res + branch).astype(bf16)

    total = shares[1 % ring]
    for s in range(2, ring + 1):
        total = turn(total, "hid") + shares[s % ring]
    grad_in = plane_gather(total[0], (0, 1), spot_bits).astype(f32)
    grad_back = plane_gather(total[1], (1, 0), spot_bits).T.astype(f32)

    gq, gk, gv, go, input_grad, vecs = attention_backward(
        gn2, cotangent, res, tokens, n1, k, v, mixed, prob, cen, cnt, cl3,
        query_key_value_weight, attention_output_weight, g1, g2,
    )
    for axis in ("mod", "dp", "hid"):
        for bit in range(bits(axis)):
            vecs = vecs + flip(vecs, axis, bit)
    gqkv = jnp.concatenate([sum_everywhere(x, core, spot_bits) for x in (gq, gk, gv)], axis=1)
    grad_out = sum_everywhere(go, core, spot_bits)
    return (
        output,
        input_grad,
        gqkv.astype(f32),
        grad_out.astype(f32),
        grad_in,
        grad_back,
        vecs[0],
        vecs[1],
        vecs[2],
        vecs[3],
    )


def solution(mesh):
    every = P(("dp", "hid", "mod"), None)
    placed = (
        every, every, P(("dp", "hid", "mod")), P(), P(), P("mod", "hid"), P("hid", "mod"),
        P(), P(), P(), P(), every,
    )
    return jax.shard_map(
        per_device,
        mesh=mesh,
        in_specs=placed,
        out_specs=(every, every, P(), P(), P("mod", "hid"), P("hid", "mod"), P(), P(), P(), P()),
        check_vma=False,
    )
```

```python
import functools

import jax
import jax.numpy as jnp
from jax import lax
from jax.experimental import pallas as pl
from jax.experimental.pallas import tpu as pltpu
from jax.sharding import PartitionSpec as P

H = 12
DH = 64
C = 100
LEN = 1024
LANES = 128
GROUP = 4
WIDE = GROUP * DH

EPSILON = 1e-05
NEGATIVE = -1e30
MIB = 2**20
f32 = jnp.float32
bf16 = jnp.bfloat16

NN = (((1,), (0,)), ((), ()))
NT = (((1,), (1,)), ((), ()))
TN = (((0,), (0,)), ((), ()))
ANY = pl.BlockSpec(memory_space=pl.ANY)


def mm(a, b, dims=NN):
    return lax.dot_general(a, b, dims, preferred_element_type=f32)


def row_stats(x):
    mean = jnp.mean(x, axis=-1, keepdims=True)
    centered = x - mean
    var = jnp.mean(centered * centered, axis=-1, keepdims=True)
    r = lax.rsqrt(var + EPSILON)
    return centered * r, r


def norm_back(g, gain, xhat, r):
    gx = g * gain
    return r * (
        gx
        - jnp.mean(gx, axis=-1, keepdims=True)
        - xhat * jnp.mean(gx * xhat, axis=-1, keepdims=True)
    )


def member_pair(cl, p):
    rows = cl.shape[0]
    lane = lax.broadcasted_iota(jnp.int32, (rows, LANES), 1)
    halves = [(cl[:, 2 * p + i : 2 * p + i + 1] == lane).astype(f32) for i in (0, 1)]
    return jnp.concatenate(halves, axis=1)


def pair_mask():
    d = lax.broadcasted_iota(jnp.int32, (2 * DH, 2 * LANES), 0)
    c = lax.broadcasted_iota(jnp.int32, (2 * DH, 2 * LANES), 1)
    return ((d >= DH) == (c >= LANES)).astype(f32)


def hbm(x):
    return pltpu.with_memory_space_constraint(x, pltpu.HBM)


def cost(us):
    return pl.CostEstimate(flops=int(us * 1.15e9), bytes_accessed=int(us * 1e6), transcendentals=0)


def whole(shape):
    return pl.BlockSpec(shape, lambda i: (0,) * len(shape))


TOKEN = jax.ShapeDtypeStruct((1, 1), f32)
SCALAR = pl.BlockSpec(memory_space=pltpu.SMEM)


def call(body, after, *args, grid, in_specs, out_specs, out_shape, scratch=(), us, name, vmem=24):
    n_in, n_after = len(args), len(after)
    n_out = len(out_shape)

    def run(*refs):
        refs = refs[:n_in] + refs[n_in + n_after :]
        refs[n_in + n_out][0, 0] = 0.0
        body(*refs[: n_in + n_out], *refs[n_in + n_out + 1 :])

    return pl.pallas_call(
        run,
        grid=grid,
        in_specs=list(in_specs) + [ANY] * n_after,
        out_specs=tuple(out_specs) + (SCALAR,),
        out_shape=tuple(out_shape) + (TOKEN,),
        scratch_shapes=list(scratch),
        compiler_params=pltpu.CompilerParams(vmem_limit_bytes=vmem * MIB),
        cost_estimate=cost(us),
        name=name,
    )(*args, *after)


def fence(*arrays):
    def run(*refs):
        refs[-1][0, 0] = 0.0

    return pl.pallas_call(
        run,
        in_specs=[ANY] * len(arrays),
        out_specs=SCALAR,
        out_shape=TOKEN,
        cost_estimate=cost(0.3),
        name="fence",
    )(*arrays)


def tall(rows, width):
    return pl.BlockSpec((rows, width), lambda i: (i, 0))


def project_body(tok, w, g1, s1, qkv, n1t):
    xhat, _ = row_stats(tok[...].astype(f32))
    n1 = (xhat * g1[...] + s1[...]).astype(bf16)
    n1t[...] = n1.T
    qkv[...] = mm(n1, w[...]).astype(bf16)


def project(tokens, wqkv, g1, s1, after=()):
    rows, width = tokens.shape
    tile = 256
    sds = jax.ShapeDtypeStruct
    return call(
        project_body, after, hbm(tokens), hbm(wqkv), g1, s1,
        grid=(rows // tile,),
        in_specs=[tall(tile, width), whole(wqkv.shape), whole((1, width)), whole((1, width))],
        out_specs=(
            tall(tile, 3 * width),
            pl.BlockSpec((width, tile), lambda i: (0, i)),
        ),
        out_shape=(pltpu.HBM((rows, 3 * width), bf16), pltpu.HBM((width, rows), bf16)),
        us=6,
        name="project",
    )


def attend_body(
    tok, q, k, v, cl, keep, wo, g2, s2, mixed, prob, cen, cnt, res, n2, acc
):
    step = pl.program_id(0)
    tile = 256
    rows = tok.shape[0]
    same = pair_mask()
    kept = keep[...] == 1
    parts = []
    for p in range(GROUP // 2):
        cols = slice(2 * DH * p, 2 * DH * (p + 1))
        m32 = member_pair(cl[0], p)
        m = m32.astype(bf16)
        count = jnp.maximum(jnp.sum(m32, axis=0, keepdims=True), 1.0)
        centre = (mm(q[:, cols], m, TN) / count * same).astype(bf16)
        score = mm(k[:, cols], centre) * (DH**-0.5)
        score = jnp.where(kept, score, NEGATIVE)
        powered = jnp.exp(score - jnp.max(score, axis=0, keepdims=True))
        pr = (powered * (1.0 / jnp.sum(powered, axis=0, keepdims=True))).astype(bf16)
        centre_out = (mm(v[:, cols], pr, TN) * same).astype(bf16)
        parts.append(mm(m, centre_out, NT).astype(bf16))
        prob[:, 2 * LANES * p : 2 * LANES * (p + 1)] = pr
        cen[p] = centre
        cnt[p] = count
    mix = jnp.concatenate(parts, axis=1)
    mixed[...] = mix
    part = mm(mix, wo[...])

    @pl.when(step == 0)
    def _():
        acc[...] = part

    @pl.when(step > 0)
    def _():
        acc[...] += part

    @pl.when(step == pl.num_programs(0) - 1)
    def _():
        def second_norm(i, _):
            at = pl.ds(pl.multiple_of(i * tile, tile), tile)
            x = tok[at, :].astype(f32) + acc[at, :]
            res[at, :] = x
            xhat, _r = row_stats(x)
            n2[at, :] = (xhat * g2[...] + s2[...]).astype(bf16)
            return 0

        lax.fori_loop(0, rows // tile, second_norm, 0)


def group_cols(rows, off):
    return pl.BlockSpec((rows, WIDE), lambda g: (0, off + g))


PAIRS = GROUP // 2
STEPS = H // GROUP


def attend(tokens, qkv, cl3, keep, wo, g2, s2, after=()):
    rows, width = tokens.shape
    sds = jax.ShapeDtypeStruct
    vec = whole((1, width))
    return call(
        attend_body, after, hbm(tokens), hbm(qkv), hbm(qkv), hbm(qkv), cl3, keep, hbm(wo), g2, s2,
        grid=(STEPS,),
        in_specs=[
            whole((rows, width)),
            group_cols(rows, 0), group_cols(rows, STEPS), group_cols(rows, 2 * STEPS),
            pl.BlockSpec((1, rows, GROUP), lambda g: (g, 0, 0)),
            whole((rows, 1)),
            pl.BlockSpec((WIDE, width), lambda g: (g, 0)),
            vec, vec,
        ],
        out_specs=(
            group_cols(rows, 0),
            pl.BlockSpec((rows, GROUP * LANES), lambda g: (0, g)),
            pl.BlockSpec((PAIRS, 2 * DH, 2 * LANES), lambda g: (g, 0, 0)),
            pl.BlockSpec((PAIRS, 1, 2 * LANES), lambda g: (g, 0, 0)),
            whole((rows, width)),
            whole((rows, width)),
        ),
        out_shape=(
            pltpu.HBM((rows, width), bf16),
            pltpu.HBM((rows, H * LANES), bf16),
            pltpu.HBM((H // 2, 2 * DH, 2 * LANES), bf16),
            pltpu.HBM((H // 2, 1, 2 * LANES), f32),
            pltpu.HBM((rows, width), f32),
            sds((rows, width), bf16),
        ),
        scratch=[pltpu.VMEM((rows, width), f32)],
        us=16,
        name="attend",
        vmem=38,
    )


def residual_back_body(n_sums, *refs):
    gn2, refs = refs[:n_sums], refs[n_sums:]
    residual_back_rows(gn2, *refs)


def residual_back_rows(gn2, cot, res, mixed, wo, g2, gm, ga, go_w, vecs, acc):
    step = pl.program_id(0)
    g = gn2[0][...].astype(f32)
    for x in gn2[1:]:
        g = g + x[...].astype(f32)
    xhat, r = row_stats(res[...])
    out = (cot[...].astype(f32) + norm_back(g, g2[...], xhat, r)).astype(bf16)
    ga[...] = out
    gm[...] = mm(out, wo[...], NT).astype(bf16)
    part = mm(mixed[...], out, TN)
    gain = jnp.sum(g * xhat, axis=0, keepdims=True)
    shift_ = jnp.sum(g, axis=0, keepdims=True)

    @pl.when(step == 0)
    def _():
        acc[...] = part
        vecs[...] = jnp.zeros(vecs.shape, f32)

    @pl.when(step > 0)
    def _():
        acc[...] += part

    vecs[0:1, :] += gain
    vecs[1:2, :] += shift_

    @pl.when(step == pl.num_programs(0) - 1)
    def _():
        go_w[...] = acc[...].astype(bf16)


def residual_back(gn2, cot, res, mixed, wo, g2, after=()):
    rows, width = cot.shape
    tile = 256
    sds = jax.ShapeDtypeStruct
    t = tall(tile, width)
    return call(
        functools.partial(residual_back_body, len(gn2)), after, *gn2, hbm(cot), hbm(res), hbm(mixed), hbm(wo), g2,
        grid=(rows // tile,),
        in_specs=[t] * (len(gn2) + 3) + [whole(wo.shape), whole((1, width))],
        out_specs=(t, t, whole((width, width)), whole((8, width))),
        out_shape=(
            sds((rows, width), bf16),
            sds((rows, width), bf16),
            sds((width, width), bf16),
            sds((8, width), f32),
        ),
        scratch=[pltpu.VMEM((width, width), f32)],
        us=6,
        name="residual_back",
    )


def heads_back_body(n1t, gm, k, v, prob, cen, cnt, cl, gqkv, gw):
    same = pair_mask()
    gqs, gks, gvs = [], [], []
    for p in range(PAIRS):
        cols = slice(2 * DH * p, 2 * DH * (p + 1))
        m = member_pair(cl[0], p).astype(bf16)
        centre = cen[p]
        gco = (mm(gm[:, cols], m, TN) * same).astype(bf16)
        pr = prob[:, 2 * LANES * p : 2 * LANES * (p + 1)]
        gvs.append(mm(pr, gco, NT).astype(bf16))
        pr32 = pr.astype(f32)
        weighted = pr32 * mm(v[:, cols], gco)
        gs = (weighted - pr32 * jnp.sum(weighted, axis=0, keepdims=True)).astype(bf16)
        gc = (mm(k[:, cols], gs, TN) * (same * DH**-0.5)).astype(bf16)
        gc = (gc.astype(f32) / cnt[p]).astype(bf16)
        gks.append((mm(gs, centre, NT) * (DH**-0.5)).astype(bf16))
        gqs.append(mm(m, gc, NT).astype(bf16))
    out = jnp.concatenate(gqs + gks + gvs, axis=1)
    gqkv[...] = out
    gw[...] = mm(n1t[...], out).astype(bf16)


def heads_back(g, n1t, gm, qkv, prob, cen, cnt, cl3, after=()):
    rows, width = gm.shape
    sds = jax.ShapeDtypeStruct
    col = lambda off: pl.BlockSpec((rows, WIDE), lambda i: (0, off + g))
    return call(
        heads_back_body, after, hbm(n1t), gm, hbm(qkv), hbm(qkv), hbm(prob), hbm(cen), hbm(cnt), cl3,
        grid=(1,),
        in_specs=[
            whole((width, rows)),
            col(0), col(STEPS), col(2 * STEPS),
            pl.BlockSpec((rows, GROUP * LANES), lambda i: (0, g)),
            pl.BlockSpec((PAIRS, 2 * DH, 2 * LANES), lambda i: (g, 0, 0)),
            pl.BlockSpec((PAIRS, 1, 2 * LANES), lambda i: (g, 0, 0)),
            pl.BlockSpec((1, rows, GROUP), lambda i: (g, 0, 0)),
        ],
        out_specs=(whole((rows, 3 * WIDE)), whole((width, 3 * WIDE))),
        out_shape=(sds((rows, 3 * WIDE), bf16), sds((width, 3 * WIDE), bf16)),
        us=9,
        name="heads_back",
    )


def project_back_body(*refs):
    gs, (w, tok, ga, g1, dx, vecs) = refs[:STEPS], refs[STEPS:]
    step = pl.program_id(0)
    g = None
    for n in range(STEPS):
        for part in range(3):
            w0 = part * STEPS * WIDE + n * WIDE
            t = mm(gs[n][:, part * WIDE : (part + 1) * WIDE], w[:, w0 : w0 + WIDE], NT)
            g = t if g is None else g + t
    xhat, r = row_stats(tok[...].astype(f32))
    dx[...] = (ga[...].astype(f32) + norm_back(g, g1[...], xhat, r)).astype(bf16)

    @pl.when(step == 0)
    def _():
        vecs[...] = jnp.zeros(vecs.shape, f32)

    vecs[0:1, :] += jnp.sum(g * xhat, axis=0, keepdims=True)
    vecs[1:2, :] += jnp.sum(g, axis=0, keepdims=True)


def project_back(gs, wqkv, tok, ga, g1, after=()):
    rows, width = tok.shape
    tile = 256
    sds = jax.ShapeDtypeStruct
    t = tall(tile, width)
    return call(
        project_back_body, after, *gs, hbm(wqkv), hbm(tok), ga, g1,
        grid=(rows // tile,),
        in_specs=[tall(tile, 3 * WIDE)] * STEPS + [whole(wqkv.shape), t, t, whole((1, width))],
        out_specs=(t, whole((8, width))),
        out_shape=(sds((rows, width), bf16), sds((8, width), f32)),
        us=7,
        name="project_back",
    )


def gelu_parts(x):
    t = 1.0 / (1.0 + (0.3275911 * 0.5**0.5) * jnp.abs(x))
    e = jnp.exp(-0.5 * x * x)
    poly = t * (
        0.254829592
        + t * (-0.284496736 + t * (1.421413741 + t * (-1.453152027 + t * 1.061405429)))
    )
    q = 0.5 * poly * e
    phi = jnp.where(x >= 0, 1.0 - q, q)
    return x * phi, phi + x * e * 0.3989422804014327


def feed_forward_body(places, n_after, *refs):
    n_w = len(places)
    n2, cot = refs[:2]
    weights = refs[2 : 2 + n_w]
    i = 2 + n_w
    i += n_after
    br, gn, own, other, token = refs[i : i + 5]
    i += 5
    token[0, 0] = 0.0
    (n2_s, cot_s, n2t_s, cott_s, up_s, down_s, act_s, gp_s, br_s, gn_s, g_s) = refs[i : i + 11]
    load_sem, weight_sem, out_sem, g_sem = refs[i + 11 :]
    rows, width = n2_s.shape
    hidden = up_s.shape[1]
    half = width // 2
    tile = min(512, rows)
    tiles = rows // tile
    core = lax.axis_index("mod")
    spot = lax.rem(lax.axis_index("dp"), 4)

    tokens_in = pltpu.make_async_copy(n2, n2_s, load_sem.at[0])
    cot_in = pltpu.make_async_copy(cot, cot_s, load_sem.at[1])
    ups, downs = [], []

    def load(group, source, target):
        at = weight_sem.at[len(ups) + len(downs)]
        group.append(pltpu.make_async_copy(source, target, at))

    chunks = hidden // half
    n_up, n_down = half // 4, hidden // 4
    for ref, (kind, core_rel, spot_rel) in zip(weights, places):
        d0 = pl.multiple_of((core ^ core_rel) * half, half)
        if kind == "up":
            load(ups, ref, up_s.at[pl.ds(d0, half), :])
        elif kind == "down":
            load(downs, ref, down_s.at[:, pl.ds(d0, half)])
        else:
            rels = (spot_rel,) if kind == "piece" else range(4)
            for n, rel in enumerate(rels):
                r0 = n * (chunks * n_up + n_down)
                u0 = pl.multiple_of(d0 + (spot ^ rel) * n_up, n_up)
                for m in range(chunks):
                    load(
                        ups,
                        ref.at[pl.ds(r0 + m * n_up, n_up), :],
                        up_s.at[pl.ds(u0, n_up), pl.ds(m * half, half)],
                    )
                f0 = pl.multiple_of((spot ^ rel) * n_down, n_down)
                load(
                    downs,
                    ref.at[pl.ds(r0 + chunks * n_up, n_down), :],
                    down_s.at[pl.ds(f0, n_down), pl.ds(d0, half)],
                )
    for copy in [*ups, tokens_in, *downs, cot_in]:
        copy.start()

    def row_tile(i):
        return pl.ds(i * tile, tile)

    for copy in [*ups, tokens_in, *downs, cot_in]:
        copy.wait()

    def hidden_rows(i, _):
        at = pl.ds(pl.multiple_of(i * tile, tile), tile)
        h = mm(n2_s[at, :], up_s[...])
        ga = mm(cot_s[at, :], down_s[...], NT)
        act, slope = gelu_parts(h)
        act_s[at, :] = act.astype(bf16)
        gp_s[at, :] = (ga * slope).astype(bf16)
        n2t_s[:, at] = n2_s[at, :].T
        cott_s[:, at] = cot_s[at, :].T
        return 0

    lax.fori_loop(0, tiles, hidden_rows, 0)
    outs = []
    for i in range(tiles):
        at = row_tile(i)
        gn_s[at, :] = mm(gp_s[at, :], up_s[...], NT).astype(bf16)
        br_s[at, :] = mm(act_s[at, :], down_s[...]).astype(bf16)
        outs.append(pltpu.make_async_copy(gn_s.at[at, :], gn.at[at, :], out_sem.at[2 * i]))
        outs[-1].start()
        outs.append(pltpu.make_async_copy(br_s.at[at, :], br.at[at, :], out_sem.at[2 * i + 1]))
        outs[-1].start()

    for n, (left, right) in enumerate(((n2t_s, gp_s), (cott_s, act_s))):
        g_s[n] = mm(left[...], right[...]).astype(bf16)
        for m, (out, rel) in enumerate(((other, 1), (own, 0))):
            at = pl.ds(pl.multiple_of((core ^ rel) * half, half), half)
            outs.append(pltpu.make_async_copy(g_s.at[n, at, :], out.at[n], g_sem.at[2 * n + m]))
            outs[-1].start()
    for copy in outs:
        copy.wait()


def feed_forward(n2, cot, pieces, hidden, after=()):
    rows, width = n2.shape
    half = width // 2
    places = tuple(place for _, place in pieces)
    each = hidden // half + 1
    n_loads = sum({"piece": each, "pieces": 4 * each}.get(place[0], 1) for place in places)
    tiles = rows // min(512, rows)
    args = [n2, cot] + [a for a, _ in pieces] + list(after)
    sds = jax.ShapeDtypeStruct
    V = pltpu.VMEM
    D = pltpu.SemaphoreType.DMA
    return pl.pallas_call(
        functools.partial(feed_forward_body, places, len(after)),
        in_specs=[ANY] * len(args),
        out_specs=(ANY,) * 4 + (SCALAR,),
        out_shape=(
            sds((rows, width), bf16),
            sds((rows, width), bf16),
            sds((2, half, hidden), bf16),
            sds((2, half, hidden), bf16),
            TOKEN,
        ),
        scratch_shapes=[
            V((rows, width), bf16),
            V((rows, width), bf16),
            V((width, rows), bf16),
            V((width, rows), bf16),
            V((width, hidden), bf16),
            V((hidden, width), bf16),
            V((rows, hidden), bf16),
            V((rows, hidden), bf16),
            V((rows, width), bf16),
            V((rows, width), bf16),
            V((2, width, hidden), bf16),
            D((2,)),
            D((n_loads,)),
            D((2 * tiles,)),
            D((4,)),
        ],
        compiler_params=pltpu.CompilerParams(vmem_limit_bytes=28 * MIB),
        cost_estimate=cost(11),
        name="feed_forward",
    )(*args)


def behind(x, token):
    return x + token.reshape((1,) * x.ndim).astype(x.dtype)


def flip(x, axis, bit):
    n = lax.axis_size(axis)
    return lax.ppermute(x, axis, [(i, i ^ (1 << bit)) for i in range(n)])


def shift(x, axis, rel):
    n = lax.axis_size(axis)
    return lax.ppermute(x, axis, [(i, i ^ rel) for i in range(n)])


def turn(x, axis):
    n = lax.axis_size(axis)
    return lax.ppermute(x, axis, [(i, (i + 1) % n) for i in range(n)])


def take(x, index, n):
    return lax.dynamic_slice_in_dim(x, index * n, n, 0)


def halve(x, axis, bit, mine):
    n = x.shape[0] // 2
    return take(x, mine, n) + flip(take(x, 1 - mine, n), axis, bit)


def join(x, axis, bit, mine):
    y = flip(x, axis, bit)
    return jnp.where(mine == 0, jnp.concatenate([x, y]), jnp.concatenate([y, x]))


def bits(axis):
    return lax.axis_size(axis).bit_length() - 1


def group_sum(x):
    for b in range(2, bits("dp")):
        x = x + flip(x, "dp", b)
    return x


def plane_scatter(x, spot):
    n = x.shape[0] // 4
    got = [shift(take(x, spot ^ rel, n), "dp", rel) for rel in (1, 2, 3)]
    return group_sum(take(x, spot, n) + got[0] + got[1] + got[2])


def plane_gather(x, spot):
    n = x.shape[0]
    out = jnp.zeros((4 * n,) + x.shape[1:], x.dtype)
    for rel in range(4):
        y = shift(x, "dp", rel) if rel else x
        out = lax.dynamic_update_slice_in_dim(out, y, (spot ^ rel) * n, 0)
    return out


def along_scatter(x):
    z = lax.axis_index("hid")
    for b in range(bits("hid")):
        n = x.shape[1] // 2
        mine = (z >> b) & 1
        part = lambda i: lax.dynamic_slice_in_dim(x, i * n, n, 1)
        x = part(mine) + flip(part(1 - mine), "hid", b)
    return x


def along_gather(x):
    z = lax.axis_index("hid")
    for b in reversed(range(bits("hid"))):
        y = flip(x, "hid", b)
        x = jnp.where(
            (z >> b) & 1 == 0, jnp.concatenate([x, y], axis=1), jnp.concatenate([y, x], axis=1)
        )
    return x


def per_device(
    tokens, clusters, key_mask, query_key_value_weight, attention_output_weight, up_weight,
    down_weight, gain_one, shift_one, gain_two, shift_two, cotangent,
):
    rows, width = tokens.shape
    half = width // 2
    hidden = up_weight.shape[1]
    ring = lax.axis_size("hid")
    core = lax.axis_index("mod")
    spot = lax.rem(lax.axis_index("dp"), 4)
    spot_bits = (spot & 1, spot >> 1)

    quarter = take(up_weight, spot, half // 4)
    piece = jnp.concatenate(
        [quarter[:, m : m + half] for m in range(0, hidden, half)]
        + [take(down_weight, spot, hidden // 4)]
    )
    up_other, down_other = flip(up_weight, "mod", 0), flip(down_weight, "mod", 0)
    slots = [
        [
            (up_weight, ("up", 0, None)),
            (down_weight, ("down", 0, None)),
            (up_other, ("up", 1, None)),
            (down_other, ("down", 1, None)),
        ]
    ]

    cl3 = clusters.reshape(rows, H // GROUP, GROUP).transpose(1, 0, 2)
    keep = key_mask.reshape(rows, 1)
    vec = lambda x: x.reshape(1, width)
    g1, s1, g2, s2 = vec(gain_one), vec(shift_one), vec(gain_two), vec(shift_two)
    wqkv, wo = query_key_value_weight, attention_output_weight
    arrays = lambda slot: [x for x, _ in slot]

    qkv, n1t, token = project(tokens, wqkv, g1, s1, after=[piece])

    def spread(x):
        return [shift(x, "dp", rel) for rel in (1, 2, 3)]

    def held_slot(x, near, token):
        held = [x] + near
        both = behind(jnp.concatenate(held), token)
        return both, [(v, ("piece", 0, rel)) for rel, v in enumerate(held)] + [
            (flip(both, "mod", 0), ("pieces", 1, None))
        ]

    def plane(part, token):
        n = part.shape[1] // 2
        sends = [behind(take(part[i], 1 - spot_bits[i], n), token) for i in (0, 1)]
        keep = [take(part[i], spot_bits[i], n) for i in (0, 1)]
        return keep, [flip(sends[i], "dp", i) for i in (0, 1)], sends

    def finish(launched, token):
        keep, got, _ = launched
        return jnp.stack([a + behind(b, token) for a, b in zip(keep, got)])

    x = behind(turn(piece, "hid"), token)
    near = spread(x)
    far = turn(x, "hid")
    mixed, prob, cen, cnt, res, n2, token = attend(
        tokens, qkv, cl3, keep, wo, g2, s2, after=[x, up_other, down_other]
    )
    n_slots = ring
    branches, gn2s = [], []
    raw, part, share = [None] * n_slots, [None] * n_slots, [None] * n_slots
    for s in range(n_slots):
        first = gn2s[-1:]
        if s + 1 < n_slots:
            both, slot = held_slot(x, near, token)
            slots.append(slot)
            first += near + [both]
        if s + 2 < n_slots:
            x = behind(far, token)
            near = spread(x)
            first.append(x)
        if s + 3 < n_slots:
            far = turn(x, "hid")
        if s >= 1:
            got = flip(raw[s - 1][1], "mod", 0)
        if s >= 2:
            share[s - 2] = plane(part[s - 2], token)
            first += share[s - 2][2]
        if s >= 3:
            first += share[s - 3][1]
        br, gn, own, other, token = feed_forward(n2, cotangent, slots[s], hidden, after=first)
        branches.append(br)
        gn2s.append(gn)
        raw[s] = (own, other)
        if s >= 1:
            part[s - 1] = raw[s - 1][0] + behind(got, token)
    last = n_slots - 1
    got = flip(raw[last][1], "mod", 0)
    share[last - 1] = plane(part[last - 1], token)
    share = [finish(x, token) for x in share[: last - 1]] + share[last - 1 :]
    one = turn(share[1], "hid")
    output = res
    for x in branches:
        output = output + x.astype(f32)
    output = output.astype(bf16)

    gm, ga, go, vecs_two, token = residual_back(
        gn2s, cotangent, res, mixed, wo, g2, after=share[last - 2 : last - 1] + share[last - 1][2]
    )
    part[last] = raw[last][0] + behind(got, token)
    share[last] = plane(part[last], token)
    gs, ws = [None] * STEPS, [None] * STEPS
    heads = functools.partial(
        heads_back, n1t=n1t, gm=gm, qkv=qkv, prob=prob, cen=cen, cnt=cnt, cl3=cl3
    )
    gs[0], ws[0], after0 = heads(0, after=share[last - 1][1] + share[last][2])
    share[last - 1] = finish(share[last - 1], token)
    sides = jnp.concatenate([go, ws[0]], axis=1)
    n = width // 2
    early_send = take(sides, 1 - core, n)
    early_got = flip(early_send, "mod", 0)
    gs[1], ws[1], after1 = heads(1, after=[early_send] + share[last][1])
    share[last] = finish(share[last], after1)
    early = take(sides, core, n) + behind(early_got, after1)
    early_sends = [take(early, spot ^ rel, n // 4) for rel in (1, 2, 3)]
    early_near = [shift(x, "dp", rel) for rel, x in zip((1, 2, 3), early_sends)]
    total = behind(one, after1) + share[2 % ring]
    one = turn(total, "hid")
    gs[2], ws[2], after2 = heads(2, after=early_sends + [total])
    sides = jnp.concatenate(ws[1:], axis=1)
    late_send = take(sides, 1 - core, n)
    late_got = flip(late_send, "mod", 0)
    input_grad, vecs_one, token = project_back(
        gs, wqkv, tokens, ga, g1, after=[ws[2], late_send]
    )

    token = fence(token, late_got, *early_near, one)
    early = take(early, spot, n // 4) + behind(early_near[0], token) + early_near[1] + early_near[2]
    early = group_sum(early)
    late = take(sides, core, n) + behind(late_got, token)
    late = plane_scatter(late, spot)
    early = along_scatter(early)
    for s in range(3, ring):
        one = turn(behind(one, token) + share[s], "hid")
    vecs = jnp.concatenate([vecs_one[:2], vecs_two[:2], jnp.zeros((4, width), f32)])
    vecs = behind(vecs, token)
    vecs = vecs + flip(vecs, "mod", 0)
    token = fence(late, early, one)
    late, early, total = behind(late, token), behind(early, token), behind(one, token) + share[0]
    early = along_gather(early)
    late = along_scatter(late)
    mine = [halve(total[0], "dp", 1, spot_bits[1]), halve(total[1], "dp", 0, spot_bits[0])]
    mine = [group_sum(x) for x in mine]
    mine = [join(mine[0], "dp", 1, spot_bits[1]), join(mine[1], "dp", 0, spot_bits[0])]
    vecs = behind(vecs, token)
    for bit in range(bits("hid")):
        vecs = vecs + flip(vecs, "hid", bit)
    token = fence(early, late, *mine, vecs)
    early, late = behind(early, token), behind(late, token)
    mine, vecs = [behind(x, token) for x in mine], behind(vecs, token)
    early = plane_gather(early, spot)
    late = along_gather(late)
    for bit in range(bits("dp")):
        vecs = vecs + flip(vecs, "dp", bit)
    token = fence(early, late, vecs)
    early, late, mine = behind(early, token), behind(late, token), [behind(x, token) for x in mine]
    late = plane_gather(late, spot)
    early = join(early, "mod", 0, core)
    grad_in = join(mine[0], "dp", 0, spot_bits[0])
    grad_back = join(mine[1], "dp", 1, spot_bits[1])
    late = join(late, "mod", 0, core)
    grad_out = early[:, :width]
    blocks = [early[:, width:]] + [
        late[:, i * 3 * WIDE : (i + 1) * 3 * WIDE] for i in range(STEPS - 1)
    ]
    gqkv = jnp.concatenate(
        [x[:, i * WIDE : (i + 1) * WIDE] for i in range(3) for x in blocks], axis=1
    )
    return (
        output,
        input_grad,
        gqkv.astype(f32),
        grad_out.astype(f32),
        grad_in.astype(f32),
        grad_back.T.astype(f32),
        vecs[0],
        vecs[1],
        vecs[2],
        vecs[3],
    )


def solution(mesh):
    every = P(("dp", "hid", "mod"), None)
    placed = (
        every, every, P(("dp", "hid", "mod")), P(), P(), P("mod", "hid"), P("hid", "mod"),
        P(), P(), P(), P(), every,
    )
    return jax.shard_map(
        per_device,
        mesh=mesh,
        in_specs=placed,
        out_specs=(every, every, P(), P(), P("mod", "hid"), P("hid", "mod"), P(), P(), P(), P()),
        check_vma=False,
    )
```

```python
import functools

import jax
import jax.numpy as jnp
from jax import lax
from jax.experimental import pallas as pl
from jax.experimental.pallas import tpu as pltpu
from jax.sharding import PartitionSpec as P

H = 12
DH = 64
LEN = 1024
LANES = 128
GROUP = 4
PAIRS = GROUP // 2
STEPS = H // GROUP
WIDE = GROUP * DH

EPSILON = 1e-05
NEGATIVE = -1e30
MIB = 2**20
f32 = jnp.float32
bf16 = jnp.bfloat16

NN = (((1,), (0,)), ((), ()))
NT = (((1,), (1,)), ((), ()))
TN = (((0,), (0,)), ((), ()))
ANY = pl.BlockSpec(memory_space=pl.ANY)
SCALAR = pl.BlockSpec(memory_space=pltpu.SMEM)
TOKEN = jax.ShapeDtypeStruct((1, 1), f32)


def mm(a, b, dims=NN):
    return lax.dot_general(a, b, dims, preferred_element_type=f32)


def row_stats(x):
    mean = jnp.mean(x, axis=-1, keepdims=True)
    centered = x - mean
    var = jnp.mean(centered * centered, axis=-1, keepdims=True)
    r = lax.rsqrt(var + EPSILON)
    return centered * r, r


def norm_back(g, gain, xhat, r):
    gx = g * gain
    return r * (
        gx
        - jnp.mean(gx, axis=-1, keepdims=True)
        - xhat * jnp.mean(gx * xhat, axis=-1, keepdims=True)
    )


def member_pair(cl, p):
    rows = cl.shape[0]
    lane = lax.broadcasted_iota(jnp.int32, (rows, LANES), 1)
    halves = [(cl[:, 2 * p + i : 2 * p + i + 1] == lane).astype(f32) for i in (0, 1)]
    return jnp.concatenate(halves, axis=1)


def pair_mask():
    d = lax.broadcasted_iota(jnp.int32, (2 * DH, 2 * LANES), 0)
    c = lax.broadcasted_iota(jnp.int32, (2 * DH, 2 * LANES), 1)
    return ((d >= DH) == (c >= LANES)).astype(f32)


def hbm(x):
    return pltpu.with_memory_space_constraint(x, pltpu.HBM)


def cost(us):
    return pl.CostEstimate(flops=int(us * 1.15e9), bytes_accessed=int(us * 1e6), transcendentals=0)


def whole(shape):
    return pl.BlockSpec(shape, lambda i: (0,) * len(shape))


def tall(rows, width):
    return pl.BlockSpec((rows, width), lambda i: (i, 0))


def broad(width, rows):
    return pl.BlockSpec((width, rows), lambda i: (0, i))


def call(body, after, *args, grid, in_specs, out_specs, out_shape, scratch=(), us, name, vmem=24):
    n_in, n_after = len(args), len(after)
    n_out = len(out_shape)

    def run(*refs):
        refs = refs[:n_in] + refs[n_in + n_after :]
        refs[n_in + n_out][0, 0] = 0.0
        body(*refs[: n_in + n_out], *refs[n_in + n_out + 1 :])

    return pl.pallas_call(
        run,
        grid=grid,
        in_specs=list(in_specs) + [ANY] * n_after,
        out_specs=tuple(out_specs) + (SCALAR,),
        out_shape=tuple(out_shape) + (TOKEN,),
        scratch_shapes=list(scratch),
        compiler_params=pltpu.CompilerParams(vmem_limit_bytes=vmem * MIB),
        cost_estimate=cost(us),
        name=name,
    )(*args, *after)


def fence(*arrays):
    def run(*refs):
        refs[-1][0, 0] = 0.0

    return pl.pallas_call(
        run,
        in_specs=[ANY] * len(arrays),
        out_specs=SCALAR,
        out_shape=TOKEN,
        compiler_params=pltpu.CompilerParams(vmem_limit_bytes=MIB),
        cost_estimate=cost(0.3),
        name="fence",
    )(*arrays)


def project_body(tok, w, g1, s1, kv, qkvt, n1t):
    width = tok.shape[1]
    xhat, _ = row_stats(tok[...].astype(f32))
    n1 = (xhat * g1[...] + s1[...]).astype(bf16)
    n1t[...] = n1.T
    for part in range(3):
        cols = slice(part * width, (part + 1) * width)
        x = mm(n1, w[:, cols]).astype(bf16)
        qkvt[cols, :] = x.T
        if part:
            kv[:, (part - 1) * width : part * width] = x


def project(tokens, wqkv, g1, s1, after=()):
    rows, width = tokens.shape
    tile = 256
    return call(
        project_body, after, hbm(tokens), hbm(wqkv), g1, s1,
        grid=(rows // tile,),
        in_specs=[tall(tile, width), whole(wqkv.shape), whole((1, width)), whole((1, width))],
        out_specs=(tall(tile, 2 * width), broad(3 * width, tile), broad(width, tile)),
        out_shape=(
            pltpu.HBM((rows, 2 * width), bf16),
            pltpu.HBM((3 * width, rows), bf16),
            pltpu.HBM((width, rows), bf16),
        ),
        us=7,
        name="project",
    )


def attend_body(
    tok, qt, k, vt, cl, keep, wo, g2, s2, mixed, prob, cen, cnt, inv, res, n2,
    acc, bias, tok_s, sem,
):
    step = pl.program_id(0)
    tile = 256
    rows = tok_s.shape[0]
    same = pair_mask()

    @pl.when(step == 0)
    def _():
        pltpu.make_async_copy(tok, tok_s, sem.at[0]).start()
        column = jnp.where(keep[...] == 1, 0.0, NEGATIVE)
        bias[...] = jnp.broadcast_to(column, bias.shape)

    shut = jnp.concatenate([bias[...], bias[...]], axis=1)
    parts = []
    for p in range(PAIRS):
        cols = slice(2 * DH * p, 2 * DH * (p + 1))
        m32 = member_pair(cl[0], p)
        m = m32.astype(bf16)
        count = jnp.maximum(jnp.sum(m32, axis=0, keepdims=True), 1.0)
        centre = (mm(qt[cols, :], m) / count * same).astype(bf16) * bf16(DH**-0.5)
        score = mm(k[:, cols], centre) + shut
        powered = jnp.exp(score - jnp.max(score, axis=0, keepdims=True))
        over = 1.0 / jnp.sum(powered, axis=0, keepdims=True)
        powered = powered.astype(bf16)
        centre_out = (mm(vt[cols, :], powered) * (over * same)).astype(bf16)
        parts.append(mm(m, centre_out, NT).astype(bf16))
        prob[:, 2 * LANES * p : 2 * LANES * (p + 1)] = powered
        cen[p] = centre
        cnt[p] = count
        inv[p] = over
    mix = jnp.concatenate(parts, axis=1)
    mixed[...] = mix
    part = mm(mix, wo[...])

    @pl.when(step == 0)
    def _():
        acc[...] = part

    @pl.when(step > 0)
    def _():
        acc[...] += part

    @pl.when(step == pl.num_programs(0) - 1)
    def _():
        pltpu.make_async_copy(tok, tok_s, sem.at[0]).wait()

        def second_norm(i, _):
            at = pl.ds(pl.multiple_of(i * tile, tile), tile)
            x = tok_s[at, :].astype(f32) + acc[at, :]
            res[at, :] = x.astype(bf16)
            xhat, _r = row_stats(x)
            n2[at, :] = (xhat * g2[...] + s2[...]).astype(bf16)
            return 0

        lax.fori_loop(0, rows // tile, second_norm, 0)


def attend(tokens, kv, qkvt, cl3, keep, wo, g2, s2, after=()):
    rows, width = tokens.shape
    vec = whole((1, width))
    cols = pl.BlockSpec((rows, WIDE), lambda g: (0, g))
    row_block = lambda off: pl.BlockSpec((WIDE, rows), lambda g: (off + g, 0))
    small = lambda n: pl.BlockSpec((PAIRS, n, 2 * LANES), lambda g: (g, 0, 0))
    return call(
        attend_body, after, hbm(tokens), hbm(qkvt), hbm(kv), hbm(qkvt), cl3, keep, hbm(wo), g2, s2,
        grid=(STEPS,),
        in_specs=[
            ANY,
            row_block(0), cols, row_block(2 * STEPS),
            pl.BlockSpec((1, rows, GROUP), lambda g: (g, 0, 0)),
            whole((rows, 1)),
            pl.BlockSpec((WIDE, width), lambda g: (g, 0)),
            vec, vec,
        ],
        out_specs=(
            cols,
            pl.BlockSpec((rows, GROUP * LANES), lambda g: (0, g)),
            small(2 * DH), small(1), small(1),
            whole((rows, width)),
            whole((rows, width)),
        ),
        out_shape=(
            pltpu.HBM((rows, width), bf16),
            pltpu.HBM((rows, H * LANES), bf16),
            pltpu.HBM((H // 2, 2 * DH, 2 * LANES), bf16),
            pltpu.HBM((H // 2, 1, 2 * LANES), f32),
            pltpu.HBM((H // 2, 1, 2 * LANES), f32),
            pltpu.HBM((rows, width), bf16),
            jax.ShapeDtypeStruct((rows, width), bf16),
        ),
        scratch=[
            pltpu.VMEM((rows, width), f32),
            pltpu.VMEM((rows, LANES), f32),
            pltpu.VMEM((rows, width), bf16),
            pltpu.SemaphoreType.DMA((1,)),
        ],
        us=16,
        name="attend",
        vmem=36,
    )


def core_rows(ref, rel):
    n = ref.shape[0] // 2
    at = pl.multiple_of((lax.axis_index("mod") ^ rel) * n, n)
    return ref[pl.ds(at, n), :]


def residual_back_body(gn2, cot, res, mixed, wo, g2, gmt, ga, own, other, vecs, acc):
    step = pl.program_id(0)
    g = gn2[...].astype(f32)
    xhat, r = row_stats(res[...].astype(f32))
    out = (cot[...].astype(f32) + norm_back(g, g2[...], xhat, r)).astype(bf16)
    ga[...] = out
    gmt[...] = mm(wo[...], out, NT).astype(bf16)
    part = mm(mixed[...], out, TN)
    gain = jnp.sum(g * xhat, axis=0, keepdims=True)
    shift_ = jnp.sum(g, axis=0, keepdims=True)

    @pl.when(step == 0)
    def _():
        acc[...] = part
        vecs[...] = jnp.zeros(vecs.shape, f32)

    @pl.when(step > 0)
    def _():
        acc[...] += part

    vecs[0:1, :] += gain
    vecs[1:2, :] += shift_

    @pl.when(step == pl.num_programs(0) - 1)
    def _():
        own[...] = core_rows(acc, 0).astype(bf16)
        other[...] = core_rows(acc, 1).astype(bf16)


def residual_back(gn2, cot, res, mixed, wo, g2, after=()):
    rows, width = cot.shape
    tile = 256
    sds = jax.ShapeDtypeStruct
    t = tall(tile, width)
    side = (width // 2, width)
    return call(
        residual_back_body, after, gn2, hbm(cot), hbm(res), hbm(mixed), hbm(wo), g2,
        grid=(rows // tile,),
        in_specs=[t, t, t, t, whole(wo.shape), whole((1, width))],
        out_specs=(broad(width, tile), t, whole(side), whole(side), whole((8, width))),
        out_shape=(
            sds((width, rows), bf16),
            sds((rows, width), bf16),
            sds(side, bf16),
            sds(side, bf16),
            sds((8, width), f32),
        ),
        scratch=[pltpu.VMEM((width, width), f32)],
        us=6,
        name="residual_back",
    )


def heads_back_body(n1t, gmt, kt, v, prob, cen, cnt, inv, cl, gqkv, own, other, n1t_s, sem):
    copy = pltpu.make_async_copy(n1t, n1t_s, sem.at[0])
    copy.start()
    same = pair_mask()
    gqs, gks, gvs = [], [], []
    for p in range(PAIRS):
        cols = slice(2 * DH * p, 2 * DH * (p + 1))
        m = member_pair(cl[0], p).astype(bf16)
        over = inv[p]
        gco = (mm(gmt[cols, :], m) * same).astype(bf16)
        gco = (gco.astype(f32) * over).astype(bf16)
        pr = prob[:, 2 * LANES * p : 2 * LANES * (p + 1)]
        gvs.append(mm(pr, gco, NT).astype(bf16))
        pr32 = pr.astype(f32)
        weighted = pr32 * mm(v[:, cols], gco)
        inner = jnp.sum(weighted, axis=0, keepdims=True) * over
        gs = (weighted - pr32 * inner).astype(bf16)
        gc = (mm(kt[cols, :], gs) * (same * DH**-0.5)).astype(bf16)
        gc = (gc.astype(f32) / cnt[p]).astype(bf16)
        gks.append(mm(gs, cen[p], NT).astype(bf16))
        gqs.append(mm(m, gc, NT).astype(bf16))
    out = jnp.concatenate(gqs + gks + gvs, axis=1)
    gqkv[...] = out
    copy.wait()
    other[...] = mm(core_rows(n1t_s, 1), out).astype(bf16)
    own[...] = mm(core_rows(n1t_s, 0), out).astype(bf16)


def heads_back(g, n1t, gmt, qkvt, kv, prob, cen, cnt, inv, cl3, after=()):
    width, rows = n1t.shape
    sds = jax.ShapeDtypeStruct
    row_block = lambda off: pl.BlockSpec((WIDE, rows), lambda i: (off + g, 0))
    small = lambda n: pl.BlockSpec((PAIRS, n, 2 * LANES), lambda i: (g, 0, 0))
    side = (width // 2, 3 * WIDE)
    return call(
        heads_back_body, after,
        hbm(n1t), gmt, hbm(qkvt), hbm(kv), hbm(prob), hbm(cen), hbm(cnt), hbm(inv), cl3,
        grid=(1,),
        in_specs=[
            ANY,
            row_block(0),
            row_block(STEPS),
            pl.BlockSpec((rows, WIDE), lambda i: (0, STEPS + g)),
            pl.BlockSpec((rows, GROUP * LANES), lambda i: (0, g)),
            small(2 * DH), small(1), small(1),
            pl.BlockSpec((1, rows, GROUP), lambda i: (g, 0, 0)),
        ],
        out_specs=(whole((rows, 3 * WIDE)), whole(side), whole(side)),
        out_shape=(sds((rows, 3 * WIDE), bf16), sds(side, bf16), sds(side, bf16)),
        scratch=[pltpu.VMEM((width, rows), bf16), pltpu.SemaphoreType.DMA((1,))],
        us=6,
        name="heads_back",
    )


def project_back_body(*refs):
    gs, (w, tok, ga, g1, dx, vecs) = refs[:STEPS], refs[STEPS:]
    step = pl.program_id(0)
    g = None
    for n in range(STEPS):
        for part in range(3):
            w0 = part * STEPS * WIDE + n * WIDE
            t = mm(gs[n][:, part * WIDE : (part + 1) * WIDE], w[:, w0 : w0 + WIDE], NT)
            g = t if g is None else g + t
    xhat, r = row_stats(tok[...].astype(f32))
    dx[...] = (ga[...].astype(f32) + norm_back(g, g1[...], xhat, r)).astype(bf16)

    @pl.when(step == 0)
    def _():
        vecs[...] = jnp.zeros(vecs.shape, f32)

    vecs[0:1, :] += jnp.sum(g * xhat, axis=0, keepdims=True)
    vecs[1:2, :] += jnp.sum(g, axis=0, keepdims=True)


def project_back(gs, wqkv, tok, ga, g1, after=()):
    rows, width = tok.shape
    tile = 256
    sds = jax.ShapeDtypeStruct
    t = tall(tile, width)
    return call(
        project_back_body, after, *gs, hbm(wqkv), hbm(tok), ga, g1,
        grid=(rows // tile,),
        in_specs=[tall(tile, 3 * WIDE)] * STEPS + [whole(wqkv.shape), t, t, whole((1, width))],
        out_specs=(t, whole((8, width))),
        out_shape=(sds((rows, width), bf16), sds((8, width), f32)),
        us=7,
        name="project_back",
    )


def assemble_body(where, first, *refs):
    pieces, (out, vecs, held, sem) = refs[:8], refs[8:]
    step = pl.program_id(0)
    n = out.shape[0]
    width = out.shape[1] // 3
    wide = held.shape[2]

    @pl.when(step == 0)
    def _():
        for q, piece in enumerate(pieces):
            pltpu.make_async_copy(piece, held.at[q], sem.at[q]).start()

    for part in range(3):
        cols = slice(part * WIDE, (part + 1) * WIDE)
        out[:, part * width : part * width + WIDE] = first[:, cols].astype(f32)
    for q, piece in enumerate(pieces):

        @pl.when(step == q)
        def _(q=q, piece=piece):
            pltpu.make_async_copy(piece, held.at[q], sem.at[q]).wait()
            for part in range(3):
                for m in range(STEPS - 1):
                    at = part * width + (m + 1) * WIDE
                    col = (3 * m + part) * WIDE
                    out[:, at : at + WIDE] = held[q, :n, col : col + WIDE].astype(f32)

    @pl.when(step == 4)
    def _():
        parts = [held[q, n : n + 16, :].astype(f32) for q in range(4)]
        total = None
        for j in range(4):
            term = None
            for rel, x in enumerate(parts):
                x = jnp.where((where[1] ^ rel) == j, x, 0.0)
                term = x if term is None else term + x
            total = term if total is None else total + term
        per = wide // width
        vecs[...] = jnp.zeros(vecs.shape, f32)
        for r in range(4 // per):
            for m in range(per):
                vecs[r * per + m, :] = total[r, m * width : (m + 1) * width]


def assemble(core, spot, first, mine, got):
    width = first.shape[0]
    n = width // 8

    def place(i, where):
        return ((where[0] ^ (i // 4)) * 4 + (where[1] ^ lax.rem(i, 4)), 0)

    return pl.pallas_call(
        assemble_body,
        grid_spec=pltpu.PrefetchScalarGridSpec(
            num_scalar_prefetch=1,
            grid=(8,),
            in_specs=[pl.BlockSpec((n, 3 * WIDE), place)] + [ANY] * 8,
            out_specs=(
                pl.BlockSpec((n, 3 * width), place),
                pl.BlockSpec((8, width), lambda i, where: (0, 0)),
            ),
            scratch_shapes=[
                pltpu.VMEM((8,) + mine[0].shape, bf16),
                pltpu.SemaphoreType.DMA((8,)),
            ],
        ),
        out_shape=(pltpu.HBM((width, 3 * width), f32), jax.ShapeDtypeStruct((8, width), f32)),
        compiler_params=pltpu.CompilerParams(vmem_limit_bytes=16 * MIB),
        cost_estimate=cost(3),
        name="assemble",
    )(jnp.stack([core, spot]), first, *mine, *got)


def finish_body(where, *refs):
    early, early_got, a, a_got, b, b_got = (refs[:4], refs[4:8], *refs[8:12])
    grad_out, first, grad_in, grad_back, token = refs[12:]
    token[0, 0] = 0.0
    core, spot = where[0], where[1]
    n, wide = early[0].shape
    width = grad_out.shape[1]
    for side, group in enumerate((early, early_got)):
        for rel, x in enumerate(group):
            at = pl.multiple_of(((core ^ side) * 4 + (spot ^ rel)) * n, n)
            grad_out[pl.ds(at, n), :] = x[:, :width].astype(f32)
            first[pl.ds(at, n), :] = x[:, width:]
    n = a.shape[0]
    for side, x in enumerate((a, a_got)):
        at = pl.multiple_of(((spot & 1) ^ side) * n, n)
        grad_in[pl.ds(at, n), :] = x[...].astype(f32)
    lo = jnp.where((spot >> 1) == 0, b[...], b_got[...])
    hi = jnp.where((spot >> 1) == 0, b_got[...], b[...])
    grad_back[...] = jnp.concatenate([lo, hi], axis=0).astype(f32).T


def finish(core, spot, early, early_got, mine, gots, half, hidden):
    wide = early[0].shape[1]
    width = 2 * half
    V = pl.BlockSpec(memory_space=pltpu.VMEM)
    return pl.pallas_call(
        finish_body,
        in_specs=[SCALAR] + [V] * 12,
        out_specs=(V, V, V, V, SCALAR),
        out_shape=(
            jax.ShapeDtypeStruct((width, width), f32),
            jax.ShapeDtypeStruct((width, wide - width), bf16),
            jax.ShapeDtypeStruct((half, hidden), f32),
            jax.ShapeDtypeStruct((hidden, half), f32),
            TOKEN,
        ),
        compiler_params=pltpu.CompilerParams(vmem_limit_bytes=24 * MIB),
        cost_estimate=cost(4),
        name="finish",
    )(jnp.stack([core, spot]), *early, *early_got, mine[0], gots[0], mine[1], gots[1])


def gelu_parts(x):
    t = 1.0 / (1.0 + (0.3275911 * 0.5**0.5) * jnp.abs(x))
    e = jnp.exp(-0.5 * x * x)
    poly = t * (
        0.254829592
        + t * (-0.284496736 + t * (1.421413741 + t * (-1.453152027 + t * 1.061405429)))
    )
    q = 0.5 * poly * e
    phi = jnp.where(x >= 0, 1.0 - q, q)
    return x * phi, phi + x * e * 0.3989422804014327


def feed_forward_body(first, places, n_after, *refs):
    n_w = len(places)
    n2, cot = refs[:2]
    weights = refs[2 : 2 + n_w]
    i = 2 + n_w
    if not first:
        gn_in = refs[i]
        i += 1
    i += n_after
    br, gn, own, other, token = refs[i : i + 5]
    i += 5
    token[0, 0] = 0.0
    (n2_s, cot_s, n2t_s, cott_s, up_s, down_s, act_s, gp_s, br_s, gn_s, sum_s, g_s) = refs[
        i : i + 12
    ]
    load_sem, weight_sem, out_sem, g_sem = refs[i + 12 :]
    rows, width = n2_s.shape
    hidden = up_s.shape[1]
    half = width // 2
    tile = min(1024, rows)
    tiles = rows // tile
    core = lax.axis_index("mod")
    spot = lax.rem(lax.axis_index("dp"), 4)

    def rows_of(i):
        return pl.ds(i * tile, tile)

    def row_copies(source, target, at):
        return [
            pltpu.make_async_copy(
                source.at[rows_of(i), :], target.at[rows_of(i), :], load_sem.at[at * tiles + i]
            )
            for i in range(tiles)
        ]

    token_in = row_copies(n2, n2_s, 0)
    cot_in = row_copies(cot, cot_s, 1)
    sum_in = [] if first else row_copies(gn_in, sum_s, 2)
    ups, downs = [], []

    def load(group, source, target):
        at = weight_sem.at[len(ups) + len(downs)]
        group.append(pltpu.make_async_copy(source, target, at))

    chunks = hidden // half
    n_up, n_down = half // 4, hidden // 4
    for ref, (kind, core_rel, spot_rel) in zip(weights, places):
        d0 = pl.multiple_of((core ^ core_rel) * half, half)
        if kind == "up":
            load(ups, ref, up_s.at[pl.ds(d0, half), :])
        elif kind == "down":
            load(downs, ref, down_s.at[:, pl.ds(d0, half)])
        else:
            rels = (spot_rel,) if kind == "piece" else range(4)
            for n, rel in enumerate(rels):
                r0 = n * (chunks * n_up + n_down)
                u0 = pl.multiple_of(d0 + (spot ^ rel) * n_up, n_up)
                for m in range(chunks):
                    load(
                        ups,
                        ref.at[pl.ds(r0 + m * n_up, n_up), :],
                        up_s.at[pl.ds(u0, n_up), pl.ds(m * half, half)],
                    )
                f0 = pl.multiple_of((spot ^ rel) * n_down, n_down)
                load(
                    downs,
                    ref.at[pl.ds(r0 + chunks * n_up, n_down), :],
                    down_s.at[pl.ds(f0, n_down), pl.ds(d0, half)],
                )
    for copy in [*ups, token_in[0], *downs, cot_in[0], *token_in[1:], *cot_in[1:], *sum_in]:
        copy.start()
    for copy in [*ups, *token_in, *downs, *cot_in, *sum_in]:
        copy.wait()
    for i in range(tiles):
        at = rows_of(i)
        h = mm(n2_s[at, :], up_s[...])
        ga = mm(cot_s[at, :], down_s[...], NT)
        act, slope = gelu_parts(h)
        act_s[at, :] = act.astype(bf16)
        gp_s[at, :] = (ga * slope).astype(bf16)
        n2t_s[:, at] = n2_s[at, :].T
        cott_s[:, at] = cot_s[at, :].T

    outs = []
    wide, deep, wide_rows = width // 2, 256, min(512, tile)
    blocks = [(r0, c0) for r0 in range(0, tile, wide_rows) for c0 in range(0, width, deep)]
    for i in range(tiles):
        at = rows_of(i)
        for r0, c0 in blocks:
            sub, cols = pl.ds(i * tile + r0, wide_rows), slice(c0, c0 + deep)
            sums = mm(gp_s[sub, :], up_s[cols, :], NT)
            if not first:
                sums += sum_s[sub, cols].astype(f32)
            gn_s[sub, cols] = sums.astype(bf16)
        outs.append(pltpu.make_async_copy(gn_s.at[at, :], gn.at[at, :], out_sem.at[2 * i]))
        outs[-1].start()
        for r0, c0 in blocks:
            sub, cols = pl.ds(i * tile + r0, wide_rows), slice(c0, c0 + deep)
            br_s[sub, cols] = mm(act_s[sub, :], down_s[:, cols]).astype(bf16)
        outs.append(pltpu.make_async_copy(br_s.at[at, :], br.at[at, :], out_sem.at[2 * i + 1]))
        outs[-1].start()
    deep = min(256, hidden)
    for n, (left, right) in enumerate(((n2t_s, gp_s), (cott_s, act_s))):
        for r0 in range(0, width, wide):
            for c0 in range(0, hidden, deep):
                end = min(c0 + deep, hidden)
                g_s[n, r0 : r0 + wide, c0:end] = mm(
                    left[r0 : r0 + wide, :], right[:, c0:end]
                ).astype(bf16)
        for m, (out, rel) in enumerate(((other, 1), (own, 0))):
            at = pl.ds(pl.multiple_of((core ^ rel) * half, half), half)
            outs.append(pltpu.make_async_copy(g_s.at[n, at, :], out.at[n], g_sem.at[2 * n + m]))
            outs[-1].start()
    for copy in outs:
        copy.wait()


def feed_forward(n2, cot, pieces, gn, hidden, after=()):
    rows, width = n2.shape
    half = width // 2
    places = tuple(place for _, place in pieces)
    each = hidden // half + 1
    n_loads = sum({"piece": each, "pieces": 4 * each}.get(place[0], 1) for place in places)
    tiles = rows // min(1024, rows)
    args = [n2, cot] + [a for a, _ in pieces] + ([] if gn is None else [gn]) + list(after)
    sds = jax.ShapeDtypeStruct
    V = pltpu.VMEM
    D = pltpu.SemaphoreType.DMA
    return pl.pallas_call(
        functools.partial(feed_forward_body, gn is None, places, len(after)),
        in_specs=[ANY] * len(args),
        out_specs=(ANY,) * 4 + (SCALAR,),
        out_shape=(
            sds((rows, width), bf16),
            sds((rows, width), bf16),
            sds((2, half, hidden), bf16),
            sds((2, half, hidden), bf16),
            TOKEN,
        ),
        scratch_shapes=[
            V((rows, width), bf16),
            V((rows, width), bf16),
            V((width, rows), bf16),
            V((width, rows), bf16),
            V((width, hidden), bf16),
            V((hidden, width), bf16),
            V((rows, hidden), bf16),
            V((rows, hidden), bf16),
            V((rows, width), bf16),
            V((rows, width), bf16),
            V((rows, width), bf16),
            V((2, width, hidden), bf16),
            D((3 * tiles,)),
            D((n_loads,)),
            D((2 * tiles,)),
            D((4,)),
        ],
        compiler_params=pltpu.CompilerParams(vmem_limit_bytes=34 * MIB),
        cost_estimate=cost(11),
        name="feed_forward",
    )(*args)


def behind(x, token):
    return x + token.reshape((1,) * x.ndim).astype(x.dtype)


def zero_of(x):
    return x[(slice(0, 1),) * x.ndim].reshape(1, 1) * 0


def flip(x, axis, bit):
    n = lax.axis_size(axis)
    return lax.ppermute(x, axis, [(i, i ^ (1 << bit)) for i in range(n)])


def shift(x, axis, rel):
    n = lax.axis_size(axis)
    return lax.ppermute(x, axis, [(i, i ^ rel) for i in range(n)])


def turn(x, axis):
    n = lax.axis_size(axis)
    return lax.ppermute(x, axis, [(i, (i + 1) % n) for i in range(n)])


def take(x, index, n):
    return lax.dynamic_slice_in_dim(x, index * n, n, 0)


def bits(axis):
    return lax.axis_size(axis).bit_length() - 1


def group_sum(x):
    for b in range(2, bits("dp")):
        x = x + flip(x, "dp", b)
    return x


def column_half(x, index):
    n = x.shape[1] // 2
    return lax.dynamic_slice_in_dim(x, index * n, n, 1)


def column_block(x, index):
    n = x.shape[1] // lax.axis_size("hid")
    return lax.dynamic_slice_in_dim(x, index * n, n, 1)


def place_columns(parts, zed, reverse=False):
    n = parts[0].shape[1]
    out = jnp.zeros((parts[0].shape[0], n * len(parts)), parts[0].dtype)
    top = bits("hid") - 1
    for rel, x in enumerate(parts):
        index = zed ^ rel
        if reverse:
            index = sum(((index >> b) & 1) << (top - b) for b in range(top + 1))
        out = lax.dynamic_update_slice_in_dim(out, x, index * n, 1)
    return out


def in_order(parts, index):
    held = jnp.zeros((len(parts),) + parts[0].shape, parts[0].dtype)
    for rel, x in enumerate(parts):
        held = lax.dynamic_update_slice_in_dim(held, x[None], index ^ rel, 0)
    return jnp.sum(held.astype(f32), axis=0).astype(parts[0].dtype)


def sort_rows(x, y, mine):
    return jnp.where(mine == 0, jnp.concatenate([x, y]), jnp.concatenate([y, x]))


def add_rows(x, rider):
    rows = rider.reshape(-1, x.shape[1])
    pad = -rows.shape[0] % 16
    return jnp.concatenate([x, rows, jnp.zeros((pad, x.shape[1]), x.dtype)])


def cut_rows(x, n, shape):
    width = x.shape[1]
    return x[:n], x[n : n + shape[0] * shape[1] // width].reshape(shape)


def plane_sends(x, spot):
    n = x.shape[0] // 4
    return [take(x, spot ^ rel, n) for rel in (1, 2, 3)], take(x, spot, n)


def plane_near(sends):
    return [shift(x, "dp", rel) for rel, x in zip((1, 2, 3), sends)]


def per_device(
    tokens, clusters, key_mask, query_key_value_weight, attention_output_weight, up_weight,
    down_weight, gain_one, shift_one, gain_two, shift_two, cotangent,
):
    rows, width = tokens.shape
    half = width // 2
    hidden = up_weight.shape[1]
    ring = lax.axis_size("hid")
    core = lax.axis_index("mod")
    spot = lax.rem(lax.axis_index("dp"), 4)
    spot_bits = (spot & 1, spot >> 1)

    quarter = take(up_weight, spot, half // 4)
    piece = jnp.concatenate(
        [quarter[:, m : m + half] for m in range(0, hidden, half)]
        + [take(down_weight, spot, hidden // 4)]
    )
    up_other, down_other = flip(up_weight, "mod", 0), flip(down_weight, "mod", 0)
    slots = [
        [
            (up_weight, ("up", 0, None)),
            (down_weight, ("down", 0, None)),
            (up_other, ("up", 1, None)),
            (down_other, ("down", 1, None)),
        ]
    ]

    cl3 = clusters.reshape(rows, STEPS, GROUP).transpose(1, 0, 2)
    keep = key_mask.reshape(rows, 1)
    vec = lambda x: x.reshape(1, width)
    g1, s1, g2, s2 = vec(gain_one), vec(shift_one), vec(gain_two), vec(shift_two)
    wqkv, wo = query_key_value_weight, attention_output_weight

    kv, qkvt, n1t, token = project(tokens, wqkv, g1, s1, after=[piece])

    def spread(x):
        return [shift(x, "dp", rel) for rel in (1, 2, 3)]

    def held_slot(x, near, token):
        held = [x] + near
        both = behind(jnp.concatenate(held), token)
        return both, [(v, ("piece", 0, rel)) for rel, v in enumerate(held)] + [
            (flip(both, "mod", 0), ("pieces", 1, None))
        ]

    def plane(part, token):
        n = part.shape[1] // 2
        sends = [behind(take(part[i], 1 - spot_bits[i], n), token) for i in (0, 1)]
        keep = [take(part[i], spot_bits[i], n) for i in (0, 1)]
        return keep, [flip(sends[i], "dp", i) for i in (0, 1)], sends

    def finish_plane(launched, token):
        keep, got, _ = launched
        return jnp.stack([a + behind(b, token) for a, b in zip(keep, got)])

    x = behind(turn(piece, "hid"), token)
    near = spread(x)
    far = turn(x, "hid")
    mixed, prob, cen, cnt, inv, res, n2, token = attend(
        tokens, kv, qkvt, cl3, keep, wo, g2, s2, after=[x, up_other, down_other]
    )
    n_slots = ring
    gn2, branches = None, []
    raw, part, share = [None] * n_slots, [None] * n_slots, [None] * n_slots
    for s in range(n_slots):
        first = []
        if s + 1 < n_slots:
            both, slot = held_slot(x, near, token)
            slots.append(slot)
            first += near + [both]
        if s + 2 < n_slots:
            x = behind(far, token)
            near = spread(x)
            first.append(x)
        if s + 3 < n_slots:
            far = turn(x, "hid")
        if s >= 1:
            got = flip(raw[s - 1][1], "mod", 0)
        if s >= 2:
            share[s - 2] = plane(part[s - 2], token)
            first += share[s - 2][2]
        if s >= 3:
            first += share[s - 3][1]
        br, gn2, own, other, token = feed_forward(
            n2, cotangent, slots[s], gn2, hidden, after=first
        )
        branches.append(br)
        raw[s] = (own, other)
        if s >= 1:
            part[s - 1] = raw[s - 1][0] + behind(got, token)
    last = n_slots - 1
    got = flip(raw[last][1], "mod", 0)
    share[last - 1] = plane(part[last - 1], token)
    share = [finish_plane(x, token) for x in share[: last - 1]] + share[last - 1 :]
    one = turn(share[1], "hid")
    output = res.astype(f32)
    for x in branches:
        output = output + x.astype(f32)
    output = output.astype(bf16)

    gmt, ga, go_own, go_other, vecs_two, token = residual_back(
        gn2, cotangent, res, mixed, wo, g2,
        after=share[last - 2 : last - 1] + share[last - 1][2],
    )
    part[last] = raw[last][0] + behind(got, token)
    share[last] = plane(part[last], token)
    gs, ws = [None] * STEPS, [None] * STEPS
    heads = functools.partial(
        heads_back,
        n1t=n1t, gmt=gmt, qkvt=qkvt, kv=kv, prob=prob, cen=cen, cnt=cnt, inv=inv, cl3=cl3,
    )
    gs[0], own, other, after0 = heads(0, after=share[last - 1][1] + share[last][2])
    share[last - 1] = finish_plane(share[last - 1], token)
    early_send = jnp.concatenate([go_other, other], axis=1)
    early = jnp.concatenate([go_own, own], axis=1)
    early_got = flip(early_send, "mod", 0)
    total = behind(one, after0) + share[2 % ring]
    one = turn(total, "hid")
    gs[1], own1, other1, after1 = heads(1, after=[early_send, total] + share[last][1])
    share[last] = finish_plane(share[last], after1)
    early = early + behind(early_got, after1)
    n = half // 4
    zed = lax.axis_index("hid")
    z_bits = [(zed >> b) & 1 for b in range(bits("hid"))]
    early_sends, early = plane_sends(early, spot)
    early_near = plane_near(early_sends)
    late_got = flip(other1, "mod", 0)
    gs[2], own2, other2, after2 = heads(2, after=early_sends)

    for s in range(3, ring):
        total = behind(one, after2) + share[s]
        one = turn(total, "hid")
    token = fence(after2, total, late_got, *early_near)
    late_left = own1 + behind(late_got, token)
    late_right = own2 + flip(behind(other2, token), "mod", 0)
    late_sends, late = plane_sends(jnp.concatenate([late_left, late_right], axis=1), spot)
    late_near = plane_near(late_sends)
    early = group_sum(behind(early, token) + early_near[0] + early_near[1] + early_near[2])
    send = column_half(early, 1 - z_bits[0])
    got = flip(send, "hid", 0)
    input_grad, vecs_one, after3 = project_back(
        gs, wqkv, tokens, ga, g1, after=[*late_sends, send, one]
    )
    early = column_half(early, z_bits[0]) + behind(got, after3)
    for b in range(1, bits("hid")):
        send = column_half(early, 1 - z_bits[b])
        early = column_half(early, z_bits[b]) + flip(send, "hid", b)
    vecs = jnp.concatenate([vecs_one[:2], vecs_two[:2]]).astype(bf16)
    vecs = vecs + flip(vecs, "mod", 0)
    total = behind(one, zero_of(send)) + share[0]
    keeps = [take(x, spot_bits[i], x.shape[0] // 2) for x, i in zip(total, (1, 0))]
    gots = [
        flip(take(x, 1 - spot_bits[i], x.shape[0] // 2), "dp", i) for x, i in zip(total, (1, 0))
    ]
    token = fence(early, vecs, output, *late_near)
    late = group_sum(late + behind(late_near[0], token) + late_near[1] + late_near[2])
    late_z = [column_block(late, zed ^ rel) for rel in range(lax.axis_size("hid"))]
    sends = [add_rows(x, vecs) for x in late_z[1:]]
    got = [shift(x, "hid", rel + 1) for rel, x in enumerate(sends)]
    early = behind(early, token)
    early_z = [early] + [shift(early, "hid", rel) for rel in range(1, lax.axis_size("hid"))]
    got = [cut_rows(x, late.shape[0], vecs.shape) for x in got]
    late = late_z[0]
    for x, _ in got:
        late = late + x
    vecs = in_order([vecs] + [x for _, x in got], zed)
    early = place_columns(early_z, zed, reverse=True)
    mine = [group_sum(x + behind(y, token)) for x, y in zip(keeps, gots)]
    gots = [flip(x, "dp", i) for x, i in zip(mine, (1, 0))]
    token = fence(early, late)
    mine = [
        sort_rows(x, behind(y, token), spot_bits[i]) for x, y, i in zip(mine, gots, (1, 0))
    ]
    early = behind(early, token)
    early_near = plane_near([early] * 3)
    late = behind(late, token)
    late_z = [late] + [shift(late, "hid", rel) for rel in range(1, lax.axis_size("hid"))]
    gots = [flip(x, "dp", i) for x, i in zip(mine, (0, 1))]
    token = fence(*late_z, *early_near)
    loaded = add_rows(behind(place_columns(late_z, zed), token), group_sum(vecs))
    late_near = plane_near([loaded] * 3)
    early = [behind(x, token) for x in [early] + early_near]
    early_got = [flip(x, "mod", 0) for x in early]
    grad_out, first, grad_in, grad_back, token = finish(
        core, spot, early, early_got, mine, gots, half, hidden
    )
    pieces = [loaded] + [behind(x, token) for x in late_near]
    got = [flip(x, "mod", 0) for x in pieces]
    gqkv, vecs = assemble(core, spot, first, pieces, got)
    return (
        output,
        input_grad,
        gqkv,
        grad_out,
        grad_in,
        grad_back,
        vecs[0],
        vecs[1],
        vecs[2],
        vecs[3],
    )


def solution(mesh):
    every = P(("dp", "hid", "mod"), None)
    placed = (
        every, every, P(("dp", "hid", "mod")), P(), P(), P("mod", "hid"), P("hid", "mod"),
        P(), P(), P(), P(), every,
    )
    return jax.shard_map(
        per_device,
        mesh=mesh,
        in_specs=placed,
        out_specs=(every, every, P(), P(), P("mod", "hid"), P("hid", "mod"), P(), P(), P(), P()),
        check_vma=False,
    )
```

```python
import functools

import jax
import jax.numpy as jnp
from jax import lax
from jax.experimental import pallas as pl
from jax.experimental.pallas import tpu as pltpu
from jax.sharding import PartitionSpec as P

H = 12
DH = 64
LEN = 1024
LANES = 128
GROUP = 4
PAIRS = GROUP // 2
STEPS = H // GROUP
WIDE = GROUP * DH

EPSILON = 1e-05
NEGATIVE = -1e30
MIB = 2**20
f32 = jnp.float32
bf16 = jnp.bfloat16

NN = (((1,), (0,)), ((), ()))
NT = (((1,), (1,)), ((), ()))
TN = (((0,), (0,)), ((), ()))
ANY = pl.BlockSpec(memory_space=pl.ANY)
SCALAR = pl.BlockSpec(memory_space=pltpu.SMEM)
TOKEN = jax.ShapeDtypeStruct((1, 1), f32)


def mm(a, b, dims=NN):
    return lax.dot_general(a, b, dims, preferred_element_type=f32)


def row_stats(x):
    mean = jnp.mean(x, axis=-1, keepdims=True)
    centered = x - mean
    var = jnp.mean(centered * centered, axis=-1, keepdims=True)
    r = lax.rsqrt(var + EPSILON)
    return centered * r, r


def norm_back(g, gain, xhat, r):
    gx = g * gain
    return r * (
        gx
        - jnp.mean(gx, axis=-1, keepdims=True)
        - xhat * jnp.mean(gx * xhat, axis=-1, keepdims=True)
    )


def member_pair(cl, p):
    rows = cl.shape[0]
    lane = lax.broadcasted_iota(jnp.int32, (rows, LANES), 1)
    halves = [(cl[:, 2 * p + i : 2 * p + i + 1] == lane).astype(f32) for i in (0, 1)]
    return jnp.concatenate(halves, axis=1)


def pair_mask():
    d = lax.broadcasted_iota(jnp.int32, (2 * DH, 2 * LANES), 0)
    c = lax.broadcasted_iota(jnp.int32, (2 * DH, 2 * LANES), 1)
    return ((d >= DH) == (c >= LANES)).astype(f32)


def hbm(x):
    return pltpu.with_memory_space_constraint(x, pltpu.HBM)


def cost(us):
    return pl.CostEstimate(flops=int(us * 1.15e9), bytes_accessed=int(us * 1e6), transcendentals=0)


def whole(shape):
    return pl.BlockSpec(shape, lambda i: (0,) * len(shape))


def tall(rows, width):
    return pl.BlockSpec((rows, width), lambda i: (i, 0))


def broad(width, rows):
    return pl.BlockSpec((width, rows), lambda i: (0, i))


def call(body, after, *args, grid, in_specs, out_specs, out_shape, scratch=(), us, name, vmem=34):
    n_in, n_after = len(args), len(after)
    n_out = len(out_shape)

    def run(*refs):
        refs = refs[:n_in] + refs[n_in + n_after :]
        refs[n_in + n_out][0, 0] = 0.0
        body(*refs[: n_in + n_out], *refs[n_in + n_out + 1 :])

    return pl.pallas_call(
        run,
        grid=grid,
        in_specs=list(in_specs) + [ANY] * n_after,
        out_specs=tuple(out_specs) + (SCALAR,),
        out_shape=tuple(out_shape) + (TOKEN,),
        scratch_shapes=list(scratch),
        compiler_params=pltpu.CompilerParams(vmem_limit_bytes=vmem * MIB),
        cost_estimate=cost(us),
        name=name,
    )(*args, *after)


def fence(*arrays):
    def run(*refs):
        refs[-1][0, 0] = 0.0

    return pl.pallas_call(
        run,
        in_specs=[ANY] * len(arrays),
        out_specs=SCALAR,
        out_shape=TOKEN,
        compiler_params=pltpu.CompilerParams(vmem_limit_bytes=MIB),
        cost_estimate=cost(0.3),
        name="fence",
    )(*arrays)


def project_body(tok, w, g1, s1, kv, qkvt, n1t):
    width = tok.shape[1]
    xhat, _ = row_stats(tok[...].astype(f32))
    n1 = (xhat * g1[...] + s1[...]).astype(bf16)
    n1t[...] = n1.T
    for part in range(3):
        cols = slice(part * width, (part + 1) * width)
        x = mm(n1, w[:, cols]).astype(bf16)
        qkvt[cols, :] = x.T
        if part:
            kv[:, (part - 1) * width : part * width] = x


def project(tokens, wqkv, g1, s1, after=()):
    rows, width = tokens.shape
    tile = 512
    return call(
        project_body, after, hbm(tokens), hbm(wqkv), g1, s1,
        grid=(rows // tile,),
        in_specs=[tall(tile, width), whole(wqkv.shape), whole((1, width)), whole((1, width))],
        out_specs=(tall(tile, 2 * width), broad(3 * width, tile), broad(width, tile)),
        out_shape=(
            pltpu.HBM((rows, 2 * width), bf16),
            pltpu.HBM((3 * width, rows), bf16),
            pltpu.HBM((width, rows), bf16),
        ),
        us=7,
        name="project",
    )


def attend_body(
    tok, qt, k, vt, cl, keep, wo, g2, s2, mixed, prob, cen, cnt, inv, res, n2,
    acc, bias, tok_s, sem,
):
    step = pl.program_id(0)
    tile = 256
    rows = tok_s.shape[0]
    same = pair_mask()

    @pl.when(step == 0)
    def _():
        pltpu.make_async_copy(tok, tok_s, sem.at[0]).start()
        column = jnp.where(keep[...] == 1, 0.0, NEGATIVE)
        bias[...] = jnp.broadcast_to(column, bias.shape)

    shut = jnp.concatenate([bias[...], bias[...]], axis=1)
    parts = []
    for p in range(PAIRS):
        cols = slice(2 * DH * p, 2 * DH * (p + 1))
        m32 = member_pair(cl[0], p)
        m = m32.astype(bf16)
        count = jnp.maximum(jnp.sum(m32, axis=0, keepdims=True), 1.0)
        centre = (mm(qt[cols, :], m) / count * same).astype(bf16) * bf16(DH**-0.5)
        score = mm(k[:, cols], centre) + shut
        powered = jnp.exp(score - jnp.max(score, axis=0, keepdims=True))
        over = 1.0 / jnp.sum(powered, axis=0, keepdims=True)
        powered = powered.astype(bf16)
        centre_out = (mm(vt[cols, :], powered) * (over * same)).astype(bf16)
        parts.append(mm(m, centre_out, NT).astype(bf16))
        prob[:, 2 * LANES * p : 2 * LANES * (p + 1)] = powered
        cen[p] = centre
        cnt[p] = count
        inv[p] = over
    mix = jnp.concatenate(parts, axis=1)
    mixed[...] = mix
    part = mm(mix, wo[...])

    @pl.when(step == 0)
    def _():
        acc[...] = part

    @pl.when(step > 0)
    def _():
        acc[...] += part

    @pl.when(step == pl.num_programs(0) - 1)
    def _():
        pltpu.make_async_copy(tok, tok_s, sem.at[0]).wait()

        def second_norm(i, _):
            at = pl.ds(pl.multiple_of(i * tile, tile), tile)
            x = tok_s[at, :].astype(f32) + acc[at, :]
            res[at, :] = x.astype(bf16)
            xhat, _r = row_stats(x)
            n2[at, :] = (xhat * g2[...] + s2[...]).astype(bf16)
            return 0

        lax.fori_loop(0, rows // tile, second_norm, 0)


def attend(tokens, kv, qkvt, cl3, keep, wo, g2, s2, after=()):
    rows, width = tokens.shape
    vec = whole((1, width))
    cols = pl.BlockSpec((rows, WIDE), lambda g: (0, g))
    row_block = lambda off: pl.BlockSpec((WIDE, rows), lambda g: (off + g, 0))
    small = lambda n: pl.BlockSpec((PAIRS, n, 2 * LANES), lambda g: (g, 0, 0))
    return call(
        attend_body, after, hbm(tokens), hbm(qkvt), hbm(kv), hbm(qkvt), cl3, keep, hbm(wo), g2, s2,
        grid=(STEPS,),
        in_specs=[
            ANY,
            row_block(0), cols, row_block(2 * STEPS),
            pl.BlockSpec((1, rows, GROUP), lambda g: (g, 0, 0)),
            whole((rows, 1)),
            pl.BlockSpec((WIDE, width), lambda g: (g, 0)),
            vec, vec,
        ],
        out_specs=(
            cols,
            pl.BlockSpec((rows, GROUP * LANES), lambda g: (0, g)),
            small(2 * DH), small(1), small(1),
            whole((rows, width)),
            whole((rows, width)),
        ),
        out_shape=(
            pltpu.HBM((rows, width), bf16),
            pltpu.HBM((rows, H * LANES), bf16),
            pltpu.HBM((H // 2, 2 * DH, 2 * LANES), bf16),
            pltpu.HBM((H // 2, 1, 2 * LANES), f32),
            pltpu.HBM((H // 2, 1, 2 * LANES), f32),
            pltpu.HBM((rows, width), bf16),
            jax.ShapeDtypeStruct((rows, width), bf16),
        ),
        scratch=[
            pltpu.VMEM((rows, width), f32),
            pltpu.VMEM((rows, LANES), f32),
            pltpu.VMEM((rows, width), bf16),
            pltpu.SemaphoreType.DMA((1,)),
        ],
        us=16,
        name="attend",
        vmem=36,
    )


def core_rows(ref, rel):
    n = ref.shape[0] // 2
    at = pl.multiple_of((lax.axis_index("mod") ^ rel) * n, n)
    return ref[pl.ds(at, n), :]


def residual_back_body(gn2, cot, res, mixed, wo, g2, gmt, ga, own, other, vecs, acc):
    step = pl.program_id(0)
    g = gn2[...].astype(f32)
    xhat, r = row_stats(res[...].astype(f32))
    out = (cot[...].astype(f32) + norm_back(g, g2[...], xhat, r)).astype(bf16)
    ga[...] = out
    gmt[...] = mm(wo[...], out, NT).astype(bf16)
    part = mm(mixed[...], out, TN)
    gain = jnp.sum(g * xhat, axis=0, keepdims=True)
    shift_ = jnp.sum(g, axis=0, keepdims=True)

    @pl.when(step == 0)
    def _():
        acc[...] = part
        vecs[...] = jnp.zeros(vecs.shape, f32)

    @pl.when(step > 0)
    def _():
        acc[...] += part

    vecs[0:1, :] += gain
    vecs[1:2, :] += shift_

    @pl.when(step == pl.num_programs(0) - 1)
    def _():
        own[...] = core_rows(acc, 0).astype(bf16)
        other[...] = core_rows(acc, 1).astype(bf16)


def residual_back(gn2, cot, res, mixed, wo, g2, after=()):
    rows, width = cot.shape
    tile = 512
    sds = jax.ShapeDtypeStruct
    t = tall(tile, width)
    side = (width // 2, width)
    return call(
        residual_back_body, after, gn2, hbm(cot), hbm(res), hbm(mixed), hbm(wo), g2,
        grid=(rows // tile,),
        in_specs=[t, t, t, t, whole(wo.shape), whole((1, width))],
        out_specs=(broad(width, tile), t, whole(side), whole(side), whole((8, width))),
        out_shape=(
            sds((width, rows), bf16),
            sds((rows, width), bf16),
            sds(side, bf16),
            sds(side, bf16),
            sds((8, width), f32),
        ),
        scratch=[pltpu.VMEM((width, width), f32)],
        us=6,
        name="residual_back",
    )


def heads_back_body(n1t, gmt, kt, v, prob, cen, cnt, inv, cl, gqkv, own, other, n1t_s, sem):
    copy = pltpu.make_async_copy(n1t, n1t_s, sem.at[0])
    copy.start()
    same = pair_mask()
    gqs, gks, gvs = [], [], []
    for p in range(PAIRS):
        cols = slice(2 * DH * p, 2 * DH * (p + 1))
        m = member_pair(cl[0], p).astype(bf16)
        over = inv[p]
        gco = (mm(gmt[cols, :], m) * same).astype(bf16)
        gco = (gco.astype(f32) * over).astype(bf16)
        pr = prob[:, 2 * LANES * p : 2 * LANES * (p + 1)]
        gvs.append(mm(pr, gco, NT).astype(bf16))
        pr32 = pr.astype(f32)
        weighted = pr32 * mm(v[:, cols], gco)
        inner = jnp.sum(weighted, axis=0, keepdims=True) * over
        gs = (weighted - pr32 * inner).astype(bf16)
        gc = (mm(kt[cols, :], gs) * (same * DH**-0.5)).astype(bf16)
        gc = (gc.astype(f32) / cnt[p]).astype(bf16)
        gks.append(mm(gs, cen[p], NT).astype(bf16))
        gqs.append(mm(m, gc, NT).astype(bf16))
    out = jnp.concatenate(gqs + gks + gvs, axis=1)
    gqkv[...] = out
    copy.wait()
    other[...] = mm(core_rows(n1t_s, 1), out).astype(bf16)
    own[...] = mm(core_rows(n1t_s, 0), out).astype(bf16)


def heads_back(g, n1t, gmt, qkvt, kv, prob, cen, cnt, inv, cl3, after=()):
    width, rows = n1t.shape
    sds = jax.ShapeDtypeStruct
    row_block = lambda off: pl.BlockSpec((WIDE, rows), lambda i: (off + g, 0))
    small = lambda n: pl.BlockSpec((PAIRS, n, 2 * LANES), lambda i: (g, 0, 0))
    side = (width // 2, 3 * WIDE)
    return call(
        heads_back_body, after,
        hbm(n1t), gmt, hbm(qkvt), hbm(kv), hbm(prob), hbm(cen), hbm(cnt), hbm(inv), cl3,
        grid=(1,),
        in_specs=[
            ANY,
            row_block(0),
            row_block(STEPS),
            pl.BlockSpec((rows, WIDE), lambda i: (0, STEPS + g)),
            pl.BlockSpec((rows, GROUP * LANES), lambda i: (0, g)),
            small(2 * DH), small(1), small(1),
            pl.BlockSpec((1, rows, GROUP), lambda i: (g, 0, 0)),
        ],
        out_specs=(whole((rows, 3 * WIDE)), whole(side), whole(side)),
        out_shape=(sds((rows, 3 * WIDE), bf16), sds(side, bf16), sds(side, bf16)),
        scratch=[pltpu.VMEM((width, rows), bf16), pltpu.SemaphoreType.DMA((1,))],
        us=6,
        name="heads_back",
    )


def project_back_body(*refs):
    gs, (w, tok, ga, g1, dx, vecs) = refs[:STEPS], refs[STEPS:]
    step = pl.program_id(0)
    g = None
    for n in range(STEPS):
        for part in range(3):
            w0 = part * STEPS * WIDE + n * WIDE
            t = mm(gs[n][:, part * WIDE : (part + 1) * WIDE], w[:, w0 : w0 + WIDE], NT)
            g = t if g is None else g + t
    xhat, r = row_stats(tok[...].astype(f32))
    dx[...] = (ga[...].astype(f32) + norm_back(g, g1[...], xhat, r)).astype(bf16)

    @pl.when(step == 0)
    def _():
        vecs[...] = jnp.zeros(vecs.shape, f32)

    vecs[0:1, :] += jnp.sum(g * xhat, axis=0, keepdims=True)
    vecs[1:2, :] += jnp.sum(g, axis=0, keepdims=True)


def project_back(gs, wqkv, tok, ga, g1, after=()):
    rows, width = tok.shape
    tile = 512
    sds = jax.ShapeDtypeStruct
    t = tall(tile, width)
    return call(
        project_back_body, after, *gs, hbm(wqkv), hbm(tok), ga, g1,
        grid=(rows // tile,),
        in_specs=[tall(tile, 3 * WIDE)] * STEPS + [whole(wqkv.shape), t, t, whole((1, width))],
        out_specs=(t, whole((8, width))),
        out_shape=(sds((rows, width), bf16), sds((8, width), f32)),
        us=0.1,
        name="project_back",
    )


def assemble_body(where, first, *refs):
    pieces, (out, vecs, held, sem) = refs[:8], refs[8:]
    step = pl.program_id(0)
    n = out.shape[0] // 2
    width = out.shape[1] // 3
    wide = held.shape[2]

    @pl.when(step == 0)
    def _():
        for q, piece in enumerate(pieces):
            pltpu.make_async_copy(piece, held.at[q], sem.at[q]).start()

    for part in range(3):
        cols = slice(part * WIDE, (part + 1) * WIDE)
        out[:, part * width : part * width + WIDE] = first[:, cols].astype(f32)
    for q, piece in enumerate(pieces):

        @pl.when(step == q // 2)
        def _(q=q, piece=piece):
            rows = pl.ds(pl.multiple_of(((where[1] ^ q) & 1) * n, n), n)
            pltpu.make_async_copy(piece, held.at[q], sem.at[q]).wait()
            for part in range(3):
                for m in range(STEPS - 1):
                    at = part * width + (m + 1) * WIDE
                    col = (3 * m + part) * WIDE
                    out[rows, at : at + WIDE] = held[q, :n, col : col + WIDE].astype(f32)

    @pl.when(step == 2)
    def _():
        parts = [held[q, n : n + 16, :].astype(f32) for q in range(4)]
        total = None
        for j in range(4):
            term = None
            for rel, x in enumerate(parts):
                x = jnp.where((where[1] ^ rel) == j, x, 0.0)
                term = x if term is None else term + x
            total = term if total is None else total + term
        per = wide // width
        vecs[...] = jnp.zeros(vecs.shape, f32)
        for r in range(4 // per):
            for m in range(per):
                vecs[r * per + m, :] = total[r, m * width : (m + 1) * width]


def assemble(core, spot, first, mine, got):
    width = first.shape[0]
    n = width // 4

    def place(i, where):
        return ((where[0] ^ (i // 2)) * 2 + ((where[1] // 2) ^ lax.rem(i, 2)), 0)

    return pl.pallas_call(
        assemble_body,
        grid_spec=pltpu.PrefetchScalarGridSpec(
            num_scalar_prefetch=1,
            grid=(4,),
            in_specs=[pl.BlockSpec((n, 3 * WIDE), place)] + [ANY] * 8,
            out_specs=(
                pl.BlockSpec((n, 3 * width), place),
                pl.BlockSpec((8, width), lambda i, where: (0, 0)),
            ),
            scratch_shapes=[
                pltpu.VMEM((8,) + mine[0].shape, bf16),
                pltpu.SemaphoreType.DMA((8,)),
            ],
        ),
        out_shape=(pltpu.HBM((width, 3 * width), f32), jax.ShapeDtypeStruct((8, width), f32)),
        compiler_params=pltpu.CompilerParams(vmem_limit_bytes=16 * MIB),
        cost_estimate=cost(3),
        name="assemble",
    )(jnp.stack([core, spot]), first, *mine, *got)


def finish_body(where, *refs):
    early, early_got, a, a_got, b, b_got = (refs[:4], refs[4:8], *refs[8:12])
    grad_out, first, grad_in, grad_back, token = refs[12:]
    token[0, 0] = 0.0
    core, spot = where[0], where[1]
    n, wide = early[0].shape
    width = grad_out.shape[1]
    for side, group in enumerate((early, early_got)):
        for rel, x in enumerate(group):
            at = pl.multiple_of(((core ^ side) * 4 + (spot ^ rel)) * n, n)
            grad_out[pl.ds(at, n), :] = x[:, :width].astype(f32)
            first[pl.ds(at, n), :] = x[:, width:]
    n = a.shape[0]
    for side, x in enumerate((a, a_got)):
        at = pl.multiple_of(((spot & 1) ^ side) * n, n)
        grad_in[pl.ds(at, n), :] = x[...].astype(f32)
    lo = jnp.where((spot >> 1) == 0, b[...], b_got[...])
    hi = jnp.where((spot >> 1) == 0, b_got[...], b[...])
    grad_back[...] = jnp.concatenate([lo, hi], axis=0).astype(f32).T


def finish(core, spot, early, early_got, mine, gots, half, hidden):
    wide = early[0].shape[1]
    width = 2 * half
    V = pl.BlockSpec(memory_space=pltpu.VMEM)
    return pl.pallas_call(
        finish_body,
        in_specs=[SCALAR] + [V] * 12,
        out_specs=(V, V, V, V, SCALAR),
        out_shape=(
            jax.ShapeDtypeStruct((width, width), f32),
            jax.ShapeDtypeStruct((width, wide - width), bf16),
            jax.ShapeDtypeStruct((half, hidden), f32),
            jax.ShapeDtypeStruct((hidden, half), f32),
            TOKEN,
        ),
        compiler_params=pltpu.CompilerParams(vmem_limit_bytes=24 * MIB),
        cost_estimate=cost(4),
        name="finish",
    )(jnp.stack([core, spot]), *early, *early_got, mine[0], gots[0], mine[1], gots[1])


def gelu_parts(x):
    t = 1.0 / (1.0 + (0.3275911 * 0.5**0.5) * jnp.abs(x))
    e = jnp.exp(-0.5 * x * x)
    poly = t * (
        0.254829592
        + t * (-0.284496736 + t * (1.421413741 + t * (-1.453152027 + t * 1.061405429)))
    )
    q = 0.5 * poly * e
    phi = jnp.where(x >= 0, 1.0 - q, q)
    return x * phi, phi + x * e * 0.3989422804014327


def feed_forward_body(first, places, n_after, *refs):
    n_w = len(places)
    n2, cot = refs[:2]
    weights = refs[2 : 2 + n_w]
    i = 2 + n_w
    if not first:
        gn_in = refs[i]
        i += 1
    i += n_after
    br, gn, own, other, token = refs[i : i + 5]
    i += 5
    token[0, 0] = 0.0
    (n2_s, cot_s, n2t_s, cott_s, up_s, down_s, act_s, gp_s, br_s, gn_s, sum_s, g_s) = refs[
        i : i + 12
    ]
    load_sem, weight_sem, out_sem, g_sem = refs[i + 12 :]
    rows, width = n2_s.shape
    hidden = up_s.shape[1]
    half = width // 2
    tile = min(1024, rows)
    tiles = rows // tile
    core = lax.axis_index("mod")
    spot = lax.rem(lax.axis_index("dp"), 4)

    def rows_of(i):
        return pl.ds(i * tile, tile)

    def row_copies(source, target, at):
        return [
            pltpu.make_async_copy(
                source.at[rows_of(i), :], target.at[rows_of(i), :], load_sem.at[at * tiles + i]
            )
            for i in range(tiles)
        ]

    token_in = row_copies(n2, n2_s, 0)
    cot_in = row_copies(cot, cot_s, 1)
    sum_in = [] if first else row_copies(gn_in, sum_s, 2)
    ups, downs = [], []

    def load(group, source, target):
        at = weight_sem.at[len(ups) + len(downs)]
        group.append(pltpu.make_async_copy(source, target, at))

    chunks = hidden // half
    n_up, n_down = half // 4, hidden // 4
    for ref, (kind, core_rel, spot_rel) in zip(weights, places):
        d0 = pl.multiple_of((core ^ core_rel) * half, half)
        if kind == "up":
            load(ups, ref, up_s.at[pl.ds(d0, half), :])
        elif kind == "down":
            load(downs, ref, down_s.at[:, pl.ds(d0, half)])
        else:
            rels = (spot_rel,) if kind == "piece" else range(4)
            for n, rel in enumerate(rels):
                r0 = n * (chunks * n_up + n_down)
                u0 = pl.multiple_of(d0 + (spot ^ rel) * n_up, n_up)
                for m in range(chunks):
                    load(
                        ups,
                        ref.at[pl.ds(r0 + m * n_up, n_up), :],
                        up_s.at[pl.ds(u0, n_up), pl.ds(m * half, half)],
                    )
                f0 = pl.multiple_of((spot ^ rel) * n_down, n_down)
                load(
                    downs,
                    ref.at[pl.ds(r0 + chunks * n_up, n_down), :],
                    down_s.at[pl.ds(f0, n_down), pl.ds(d0, half)],
                )
    for copy in [*ups, token_in[0], *downs, cot_in[0], *token_in[1:], *cot_in[1:], *sum_in]:
        copy.start()
    for copy in [*ups, *token_in, *downs, *cot_in, *sum_in]:
        copy.wait()
    for i in range(tiles):
        at = rows_of(i)
        h = mm(n2_s[at, :], up_s[...])
        ga = mm(cot_s[at, :], down_s[...], NT)
        act, slope = gelu_parts(h)
        act_s[at, :] = act.astype(bf16)
        gp_s[at, :] = (ga * slope).astype(bf16)
        n2t_s[:, at] = n2_s[at, :].T
        cott_s[:, at] = cot_s[at, :].T

    outs = []
    wide, deep, wide_rows = width // 2, 256, min(512, tile)
    blocks = [(r0, c0) for r0 in range(0, tile, wide_rows) for c0 in range(0, width, deep)]
    for i in range(tiles):
        at = rows_of(i)
        for r0, c0 in blocks:
            sub, cols = pl.ds(i * tile + r0, wide_rows), slice(c0, c0 + deep)
            sums = mm(gp_s[sub, :], up_s[cols, :], NT)
            if not first:
                sums += sum_s[sub, cols].astype(f32)
            gn_s[sub, cols] = sums.astype(bf16)
        outs.append(pltpu.make_async_copy(gn_s.at[at, :], gn.at[at, :], out_sem.at[2 * i]))
        outs[-1].start()
        for r0, c0 in blocks:
            sub, cols = pl.ds(i * tile + r0, wide_rows), slice(c0, c0 + deep)
            br_s[sub, cols] = mm(act_s[sub, :], down_s[:, cols]).astype(bf16)
        outs.append(pltpu.make_async_copy(br_s.at[at, :], br.at[at, :], out_sem.at[2 * i + 1]))
        outs[-1].start()
    deep = min(256, hidden)
    for n, (left, right) in enumerate(((n2t_s, gp_s), (cott_s, act_s))):
        for r0 in range(0, width, wide):
            for c0 in range(0, hidden, deep):
                end = min(c0 + deep, hidden)
                g_s[n, r0 : r0 + wide, c0:end] = mm(
                    left[r0 : r0 + wide, :], right[:, c0:end]
                ).astype(bf16)
        for m, (out, rel) in enumerate(((other, 1), (own, 0))):
            at = pl.ds(pl.multiple_of((core ^ rel) * half, half), half)
            outs.append(pltpu.make_async_copy(g_s.at[n, at, :], out.at[n], g_sem.at[2 * n + m]))
            outs[-1].start()
    for copy in outs:
        copy.wait()


def feed_forward(n2, cot, pieces, gn, hidden, after=()):
    rows, width = n2.shape
    half = width // 2
    places = tuple(place for _, place in pieces)
    each = hidden // half + 1
    n_loads = sum({"piece": each, "pieces": 4 * each}.get(place[0], 1) for place in places)
    tiles = rows // min(1024, rows)
    args = [n2, cot] + [a for a, _ in pieces] + ([] if gn is None else [gn]) + list(after)
    sds = jax.ShapeDtypeStruct
    V = pltpu.VMEM
    D = pltpu.SemaphoreType.DMA
    return pl.pallas_call(
        functools.partial(feed_forward_body, gn is None, places, len(after)),
        in_specs=[ANY] * len(args),
        out_specs=(ANY,) * 4 + (SCALAR,),
        out_shape=(
            sds((rows, width), bf16),
            sds((rows, width), bf16),
            sds((2, half, hidden), bf16),
            sds((2, half, hidden), bf16),
            TOKEN,
        ),
        scratch_shapes=[
            V((rows, width), bf16),
            V((rows, width), bf16),
            V((width, rows), bf16),
            V((width, rows), bf16),
            V((width, hidden), bf16),
            V((hidden, width), bf16),
            V((rows, hidden), bf16),
            V((rows, hidden), bf16),
            V((rows, width), bf16),
            V((rows, width), bf16),
            V((rows, width), bf16),
            V((2, width, hidden), bf16),
            D((3 * tiles,)),
            D((n_loads,)),
            D((2 * tiles,)),
            D((4,)),
        ],
        compiler_params=pltpu.CompilerParams(vmem_limit_bytes=34 * MIB),
        cost_estimate=cost(11),
        name="feed_forward",
    )(*args)


def behind(x, token):
    return x + token.reshape((1,) * x.ndim).astype(x.dtype)


def zero_of(x):
    return x[(slice(0, 1),) * x.ndim].reshape(1, 1) * 0


def flip(x, axis, bit):
    n = lax.axis_size(axis)
    return lax.ppermute(x, axis, [(i, i ^ (1 << bit)) for i in range(n)])


def shift(x, axis, rel):
    n = lax.axis_size(axis)
    return lax.ppermute(x, axis, [(i, i ^ rel) for i in range(n)])


def turn(x, axis):
    n = lax.axis_size(axis)
    return lax.ppermute(x, axis, [(i, (i + 1) % n) for i in range(n)])


def take(x, index, n):
    return lax.dynamic_slice_in_dim(x, index * n, n, 0)


def bits(axis):
    return lax.axis_size(axis).bit_length() - 1


def group_sum(x):
    for b in range(2, bits("dp")):
        x = x + flip(x, "dp", b)
    return x


def column_half(x, index):
    n = x.shape[1] // 2
    return lax.dynamic_slice_in_dim(x, index * n, n, 1)


def column_block(x, index):
    n = x.shape[1] // lax.axis_size("hid")
    return lax.dynamic_slice_in_dim(x, index * n, n, 1)


def place_columns(parts, zed, reverse=False):
    n = parts[0].shape[1]
    out = jnp.zeros((parts[0].shape[0], n * len(parts)), parts[0].dtype)
    top = bits("hid") - 1
    for rel, x in enumerate(parts):
        index = zed ^ rel
        if reverse:
            index = sum(((index >> b) & 1) << (top - b) for b in range(top + 1))
        out = lax.dynamic_update_slice_in_dim(out, x, index * n, 1)
    return out


def in_order(parts, index):
    held = jnp.zeros((len(parts),) + parts[0].shape, parts[0].dtype)
    for rel, x in enumerate(parts):
        held = lax.dynamic_update_slice_in_dim(held, x[None], index ^ rel, 0)
    return jnp.sum(held.astype(f32), axis=0).astype(parts[0].dtype)


def sort_rows(x, y, mine):
    return jnp.where(mine == 0, jnp.concatenate([x, y]), jnp.concatenate([y, x]))


def add_rows(x, rider):
    rows = rider.reshape(-1, x.shape[1])
    pad = -rows.shape[0] % 16
    return jnp.concatenate([x, rows, jnp.zeros((pad, x.shape[1]), x.dtype)])


def cut_rows(x, n, shape):
    width = x.shape[1]
    return x[:n], x[n : n + shape[0] * shape[1] // width].reshape(shape)


def plane_sends(x, spot):
    n = x.shape[0] // 4
    return [take(x, spot ^ rel, n) for rel in (1, 2, 3)], take(x, spot, n)


def plane_near(sends):
    return [shift(x, "dp", rel) for rel, x in zip((1, 2, 3), sends)]


def per_device(
    tokens, clusters, key_mask, query_key_value_weight, attention_output_weight, up_weight,
    down_weight, gain_one, shift_one, gain_two, shift_two, cotangent,
):
    rows, width = tokens.shape
    half = width // 2
    hidden = up_weight.shape[1]
    ring = lax.axis_size("hid")
    core = lax.axis_index("mod")
    spot = lax.rem(lax.axis_index("dp"), 4)
    spot_bits = (spot & 1, spot >> 1)

    quarter = take(up_weight, spot, half // 4)
    piece = jnp.concatenate(
        [quarter[:, m : m + half] for m in range(0, hidden, half)]
        + [take(down_weight, spot, hidden // 4)]
    )
    up_other, down_other = flip(up_weight, "mod", 0), flip(down_weight, "mod", 0)
    slots = [
        [
            (up_weight, ("up", 0, None)),
            (down_weight, ("down", 0, None)),
            (up_other, ("up", 1, None)),
            (down_other, ("down", 1, None)),
        ]
    ]

    cl3 = clusters.reshape(rows, STEPS, GROUP).transpose(1, 0, 2)
    keep = key_mask.reshape(rows, 1)
    vec = lambda x: x.reshape(1, width)
    g1, s1, g2, s2 = vec(gain_one), vec(shift_one), vec(gain_two), vec(shift_two)
    wqkv, wo = query_key_value_weight, attention_output_weight

    kv, qkvt, n1t, token = project(tokens, wqkv, g1, s1, after=[piece])

    def spread(x):
        return [shift(x, "dp", rel) for rel in (1, 2, 3)]

    def held_slot(x, near, token):
        held = [x] + near
        both = behind(jnp.concatenate(held), token)
        return both, [(v, ("piece", 0, rel)) for rel, v in enumerate(held)] + [
            (flip(both, "mod", 0), ("pieces", 1, None))
        ]

    def plane(part, token):
        n = part.shape[1] // 2
        sends = [behind(take(part[i], 1 - spot_bits[i], n), token) for i in (0, 1)]
        keep = [take(part[i], spot_bits[i], n) for i in (0, 1)]
        return keep, [flip(sends[i], "dp", i) for i in (0, 1)], sends

    def finish_plane(launched, token):
        keep, got, _ = launched
        return jnp.stack([a + behind(b, token) for a, b in zip(keep, got)])

    x = behind(turn(piece, "hid"), token)
    near = spread(x)
    far = turn(x, "hid")
    mixed, prob, cen, cnt, inv, res, n2, token = attend(
        tokens, kv, qkvt, cl3, keep, wo, g2, s2, after=[x, up_other, down_other]
    )
    n_slots = ring
    gn2, branches = None, []
    raw, part, share = [None] * n_slots, [None] * n_slots, [None] * n_slots
    for s in range(n_slots):
        first = []
        if s + 1 < n_slots:
            both, slot = held_slot(x, near, token)
            slots.append(slot)
            first += near + [both]
        if s + 2 < n_slots:
            x = behind(far, token)
            near = spread(x)
            first.append(x)
        if s + 3 < n_slots:
            far = turn(x, "hid")
        if s >= 1:
            got = flip(raw[s - 1][1], "mod", 0)
        if s >= 2:
            share[s - 2] = plane(part[s - 2], token)
            first += share[s - 2][2]
        if s >= 3:
            first += share[s - 3][1]
        br, gn2, own, other, token = feed_forward(
            n2, cotangent, slots[s], gn2, hidden, after=first
        )
        branches.append(br)
        raw[s] = (own, other)
        if s >= 1:
            part[s - 1] = raw[s - 1][0] + behind(got, token)
    last = n_slots - 1
    got = flip(raw[last][1], "mod", 0)
    share[last - 1] = plane(part[last - 1], token)
    share = [finish_plane(x, token) for x in share[: last - 1]] + share[last - 1 :]
    one = turn(share[1], "hid")
    gmt, ga, go_own, go_other, vecs_two, token = residual_back(
        gn2, cotangent, res, mixed, wo, g2,
        after=share[last - 2 : last - 1] + share[last - 1][2],
    )
    part[last] = raw[last][0] + behind(got, token)
    share[last] = plane(part[last], token)
    gs, ws = [None] * STEPS, [None] * STEPS
    heads = functools.partial(
        heads_back,
        n1t=n1t, gmt=gmt, qkvt=qkvt, kv=kv, prob=prob, cen=cen, cnt=cnt, inv=inv, cl3=cl3,
    )
    gs[0], own, other, after0 = heads(0, after=share[last - 1][1] + share[last][2])
    share[last - 1] = finish_plane(share[last - 1], token)
    early_send = jnp.concatenate([go_other, other], axis=1)
    early = jnp.concatenate([go_own, own], axis=1)
    early_got = flip(early_send, "mod", 0)
    total = behind(one, after0) + share[2 % ring]
    one = turn(total, "hid")
    gs[1], own1, other1, after1 = heads(1, after=[early_send, total] + share[last][1])
    share[last] = finish_plane(share[last], after1)
    early = early + behind(early_got, after1)
    n = half // 4
    zed = lax.axis_index("hid")
    z_bits = [(zed >> b) & 1 for b in range(bits("hid"))]
    early_sends, early = plane_sends(early, spot)
    early_near = plane_near(early_sends)
    late_got = flip(other1, "mod", 0)
    gs[2], own2, other2, after2 = heads(2, after=early_sends)

    for s in range(3, ring):
        total = behind(one, after2) + share[s]
        one = turn(total, "hid")
    late_got2 = flip(other2, "mod", 0)
    output = behind(res, after2).astype(f32)
    for x in branches:
        output = output + x.astype(f32)
    output = output.astype(bf16)
    token = fence(after2, output, total, late_got, late_got2, *early_near)
    late_left = own1 + behind(late_got, token)
    late_right = own2 + behind(late_got2, token)
    late_sends, late = plane_sends(jnp.concatenate([late_left, late_right], axis=1), spot)
    late_near = plane_near(late_sends)
    early = group_sum(behind(early, token) + early_near[0] + early_near[1] + early_near[2])
    send = column_half(early, 1 - z_bits[0])
    got = flip(send, "hid", 0)
    input_grad, vecs_one, after3 = project_back(
        gs, wqkv, tokens, ga, g1, after=[*late_sends, send]
    )
    early = column_half(early, z_bits[0]) + behind(got, after3)
    for b in range(1, bits("hid")):
        send = column_half(early, 1 - z_bits[b])
        early = column_half(early, z_bits[b]) + flip(send, "hid", b)
    vecs = jnp.concatenate([vecs_one[:2], vecs_two[:2]]).astype(bf16)
    vecs = vecs + flip(vecs, "mod", 0)
    total = behind(one, zero_of(send)) + share[0]
    keeps = [take(x, spot_bits[i], x.shape[0] // 2) for x, i in zip(total, (1, 0))]
    gots = [
        flip(take(x, 1 - spot_bits[i], x.shape[0] // 2), "dp", i) for x, i in zip(total, (1, 0))
    ]
    token = fence(early, vecs, *late_near)
    late = group_sum(late + behind(late_near[0], token) + late_near[1] + late_near[2])
    late_z = [column_block(late, zed ^ rel) for rel in range(lax.axis_size("hid"))]
    sends = [add_rows(x, vecs) for x in late_z[1:]]
    got = [shift(x, "hid", rel + 1) for rel, x in enumerate(sends)]
    early = behind(early, token)
    early_z = [early] + [shift(early, "hid", rel) for rel in range(1, lax.axis_size("hid"))]
    early = place_columns(early_z, zed, reverse=True)
    mine = [group_sum(x + behind(y, token)) for x, y in zip(keeps, gots)]
    gots = [flip(x, "dp", i) for x, i in zip(mine, (1, 0))]
    token = fence(early)
    early = behind(early, token)
    early_near = plane_near([early] * 3)
    got = [cut_rows(x, late.shape[0], vecs.shape) for x in got]
    late = late_z[0]
    for x, _ in got:
        late = late + behind(x, token)
    vecs = in_order([vecs] + [x for _, x in got], zed)
    mine = [
        sort_rows(x, behind(y, token), spot_bits[i]) for x, y, i in zip(mine, gots, (1, 0))
    ]
    late_z = [late] + [shift(late, "hid", rel) for rel in range(1, lax.axis_size("hid"))]
    gots = [flip(x, "dp", i) for x, i in zip(mine, (0, 1))]
    token = fence(*early_near)
    token = fence(token, *late_z)
    loaded = add_rows(behind(place_columns(late_z, zed), token), group_sum(vecs))
    late_near = plane_near([loaded] * 3)
    early = [behind(x, token) for x in [early] + early_near]
    early_got = [flip(x, "mod", 0) for x in early]
    grad_out, first, grad_in, grad_back, token = finish(
        core, spot, early, early_got, mine, gots, half, hidden
    )
    pieces = [loaded] + [behind(x, token) for x in late_near]
    got = [flip(x, "mod", 0) for x in pieces]
    gqkv, vecs = assemble(core, spot, first, pieces, got)
    return (
        output,
        input_grad,
        gqkv,
        grad_out,
        grad_in,
        grad_back,
        vecs[0],
        vecs[1],
        vecs[2],
        vecs[3],
    )


def solution(mesh):
    every = P(("dp", "hid", "mod"), None)
    placed = (
        every, every, P(("dp", "hid", "mod")), P(), P(), P("mod", "hid"), P("hid", "mod"),
        P(), P(), P(), P(), every,
    )
    return jax.shard_map(
        per_device,
        mesh=mesh,
        in_specs=placed,
        out_specs=(every, every, P(), P(), P("mod", "hid"), P("hid", "mod"), P(), P(), P(), P()),
        check_vma=False,
    )
```

```python
import functools

import jax
import jax.numpy as jnp
from jax import lax
from jax.experimental import pallas as pl
from jax.experimental.pallas import tpu as pltpu
from jax.sharding import PartitionSpec as P

H = 12
DH = 64
LEN = 1024
LANES = 128
GROUP = 4
PAIRS = GROUP // 2
STEPS = H // GROUP
WIDE = GROUP * DH

EPSILON = 1e-05
NEGATIVE = -1e30
MIB = 2**20
f32 = jnp.float32
bf16 = jnp.bfloat16

NN = (((1,), (0,)), ((), ()))
NT = (((1,), (1,)), ((), ()))
TN = (((0,), (0,)), ((), ()))
ANY = pl.BlockSpec(memory_space=pl.ANY)
SCALAR = pl.BlockSpec(memory_space=pltpu.SMEM)
HERE = pl.BlockSpec(memory_space=pltpu.VMEM)
TOKEN = jax.ShapeDtypeStruct((1, 1), f32)


def mm(a, b, dims=NN):
    return lax.dot_general(a, b, dims, preferred_element_type=f32)


def row_stats(x):
    mean = jnp.mean(x, axis=-1, keepdims=True)
    centered = x - mean
    var = jnp.mean(centered * centered, axis=-1, keepdims=True)
    r = lax.rsqrt(var + EPSILON)
    return centered * r, r


def norm_back(g, gain, xhat, r):
    gx = g * gain
    return r * (
        gx
        - jnp.mean(gx, axis=-1, keepdims=True)
        - xhat * jnp.mean(gx * xhat, axis=-1, keepdims=True)
    )


def member_pair(cl, p):
    rows = cl.shape[0]
    lane = lax.broadcasted_iota(jnp.int32, (rows, LANES), 1)
    halves = [(cl[:, 2 * p + i : 2 * p + i + 1] == lane).astype(f32) for i in (0, 1)]
    return jnp.concatenate(halves, axis=1)


def pair_mask():
    d = lax.broadcasted_iota(jnp.int32, (2 * DH, 2 * LANES), 0)
    c = lax.broadcasted_iota(jnp.int32, (2 * DH, 2 * LANES), 1)
    return ((d >= DH) == (c >= LANES)).astype(f32)


def hbm(x):
    return pltpu.with_memory_space_constraint(x, pltpu.HBM)


def cost(us):
    return pl.CostEstimate(flops=int(us * 1.15e9), bytes_accessed=int(us * 1e6), transcendentals=0)


def whole(shape):
    return pl.BlockSpec(shape, lambda i: (0,) * len(shape))


def tall(rows, width):
    return pl.BlockSpec((rows, width), lambda i: (i, 0))


def broad(width, rows):
    return pl.BlockSpec((width, rows), lambda i: (0, i))


def call(body, after, *args, grid, in_specs, out_specs, out_shape, scratch=(), us, name, vmem=34):
    n_in, n_after = len(args), len(after)
    n_out = len(out_shape)

    def run(*refs):
        refs = refs[:n_in] + refs[n_in + n_after :]
        refs[n_in + n_out][0, 0] = 0.0
        body(*refs[: n_in + n_out], *refs[n_in + n_out + 1 :])

    return pl.pallas_call(
        run,
        grid=grid,
        in_specs=list(in_specs) + [ANY] * n_after,
        out_specs=tuple(out_specs) + (SCALAR,),
        out_shape=tuple(out_shape) + (TOKEN,),
        scratch_shapes=list(scratch),
        compiler_params=pltpu.CompilerParams(vmem_limit_bytes=vmem * MIB),
        cost_estimate=cost(us),
        name=name,
    )(*args, *after)


def fence(*arrays):
    def run(*refs):
        refs[-1][0, 0] = 0.0

    return pl.pallas_call(
        run,
        in_specs=[ANY] * len(arrays),
        out_specs=SCALAR,
        out_shape=TOKEN,
        compiler_params=pltpu.CompilerParams(vmem_limit_bytes=MIB),
        cost_estimate=cost(0.3),
        name="fence",
    )(*arrays)


def project_body(tok, w, g1, s1, kv, qkvt, n1t):
    width = tok.shape[1]
    xhat, _ = row_stats(tok[...].astype(f32))
    n1 = (xhat * g1[...] + s1[...]).astype(bf16)
    n1t[...] = n1.T
    for part in range(3):
        cols = slice(part * width, (part + 1) * width)
        x = mm(n1, w[:, cols]).astype(bf16)
        qkvt[cols, :] = x.T
        if part:
            kv[:, (part - 1) * width : part * width] = x


def project(tokens, wqkv, g1, s1, after=()):
    rows, width = tokens.shape
    tile = 512
    return call(
        project_body, after, hbm(tokens), hbm(wqkv), g1, s1,
        grid=(rows // tile,),
        in_specs=[tall(tile, width), whole(wqkv.shape), whole((1, width)), whole((1, width))],
        out_specs=(tall(tile, 2 * width), broad(3 * width, tile), broad(width, tile)),
        out_shape=(
            pltpu.HBM((rows, 2 * width), bf16),
            pltpu.HBM((3 * width, rows), bf16),
            pltpu.HBM((width, rows), bf16),
        ),
        us=7,
        name="project",
    )


def attend_body(
    tok, qt, k, vt, cl, keep, wo, g2, s2, mixed, prob, cen, cnt, inv, res, n2,
    acc, bias, tok_s, sem,
):
    step = pl.program_id(0)
    tile = 256
    rows = tok_s.shape[0]
    same = pair_mask()

    @pl.when(step == 0)
    def _():
        pltpu.make_async_copy(tok, tok_s, sem.at[0]).start()
        column = jnp.where(keep[...] == 1, 0.0, NEGATIVE)
        bias[...] = jnp.broadcast_to(column, bias.shape)

    shut = jnp.concatenate([bias[...], bias[...]], axis=1)
    parts = []
    for p in range(PAIRS):
        cols = slice(2 * DH * p, 2 * DH * (p + 1))
        m32 = member_pair(cl[0], p)
        m = m32.astype(bf16)
        count = jnp.maximum(jnp.sum(m32, axis=0, keepdims=True), 1.0)
        centre = (mm(qt[cols, :], m) / count * same).astype(bf16) * bf16(DH**-0.5)
        score = mm(k[:, cols], centre) + shut
        powered = jnp.exp(score - jnp.max(score, axis=0, keepdims=True))
        over = 1.0 / jnp.sum(powered, axis=0, keepdims=True)
        powered = powered.astype(bf16)
        centre_out = (mm(vt[cols, :], powered) * (over * same)).astype(bf16)
        parts.append(mm(m, centre_out, NT).astype(bf16))
        prob[:, 2 * LANES * p : 2 * LANES * (p + 1)] = powered
        cen[p] = centre
        cnt[p] = count
        inv[p] = over
    mix = jnp.concatenate(parts, axis=1)
    mixed[...] = mix
    part = mm(mix, wo[...])

    @pl.when(step == 0)
    def _():
        acc[...] = part

    @pl.when(step > 0)
    def _():
        acc[...] += part

    @pl.when(step == pl.num_programs(0) - 1)
    def _():
        pltpu.make_async_copy(tok, tok_s, sem.at[0]).wait()

        def second_norm(i, _):
            at = pl.ds(pl.multiple_of(i * tile, tile), tile)
            x = tok_s[at, :].astype(f32) + acc[at, :]
            res[at, :] = x.astype(bf16)
            xhat, _r = row_stats(x)
            n2[at, :] = (xhat * g2[...] + s2[...]).astype(bf16)
            return 0

        lax.fori_loop(0, rows // tile, second_norm, 0)


def attend(tokens, kv, qkvt, cl3, keep, wo, g2, s2, after=()):
    rows, width = tokens.shape
    vec = whole((1, width))
    cols = pl.BlockSpec((rows, WIDE), lambda g: (0, g))
    row_block = lambda off: pl.BlockSpec((WIDE, rows), lambda g: (off + g, 0))
    small = lambda n: pl.BlockSpec((PAIRS, n, 2 * LANES), lambda g: (g, 0, 0))
    return call(
        attend_body, after, hbm(tokens), hbm(qkvt), hbm(kv), hbm(qkvt), cl3, keep, hbm(wo), g2, s2,
        grid=(STEPS,),
        in_specs=[
            ANY,
            row_block(0), cols, row_block(2 * STEPS),
            pl.BlockSpec((1, rows, GROUP), lambda g: (g, 0, 0)),
            whole((rows, 1)),
            pl.BlockSpec((WIDE, width), lambda g: (g, 0)),
            vec, vec,
        ],
        out_specs=(
            cols,
            pl.BlockSpec((rows, GROUP * LANES), lambda g: (0, g)),
            small(2 * DH), small(1), small(1),
            whole((rows, width)),
            whole((rows, width)),
        ),
        out_shape=(
            pltpu.HBM((rows, width), bf16),
            pltpu.HBM((rows, H * LANES), bf16),
            pltpu.HBM((H // 2, 2 * DH, 2 * LANES), bf16),
            pltpu.HBM((H // 2, 1, 2 * LANES), f32),
            pltpu.HBM((H // 2, 1, 2 * LANES), f32),
            pltpu.HBM((rows, width), bf16),
            jax.ShapeDtypeStruct((rows, width), bf16),
        ),
        scratch=[
            pltpu.VMEM((rows, width), f32),
            pltpu.VMEM((rows, LANES), f32),
            pltpu.VMEM((rows, width), bf16),
            pltpu.SemaphoreType.DMA((1,)),
        ],
        us=16,
        name="attend",
        vmem=36,
    )


def core_rows(ref, rel):
    n = ref.shape[0] // 2
    at = pl.multiple_of((lax.axis_index("mod") ^ rel) * n, n)
    return ref[pl.ds(at, n), :]


def residual_back_body(gn2, cot, res, mixed, wo, g2, gmt, ga, own, other, vecs, acc):
    step = pl.program_id(0)
    g = gn2[...].astype(f32)
    xhat, r = row_stats(res[...].astype(f32))
    out = (cot[...].astype(f32) + norm_back(g, g2[...], xhat, r)).astype(bf16)
    ga[...] = out
    gmt[...] = mm(wo[...], out, NT).astype(bf16)
    part = mm(mixed[...], out, TN)
    gain = jnp.sum(g * xhat, axis=0, keepdims=True)
    shift_ = jnp.sum(g, axis=0, keepdims=True)

    @pl.when(step == 0)
    def _():
        acc[...] = part
        vecs[...] = jnp.zeros(vecs.shape, f32)

    @pl.when(step > 0)
    def _():
        acc[...] += part

    vecs[0:1, :] += gain
    vecs[1:2, :] += shift_

    @pl.when(step == pl.num_programs(0) - 1)
    def _():
        own[...] = core_rows(acc, 0).astype(bf16)
        other[...] = core_rows(acc, 1).astype(bf16)


def residual_back(gn2, cot, res, mixed, wo, g2, after=()):
    rows, width = cot.shape
    tile = 512
    sds = jax.ShapeDtypeStruct
    t = tall(tile, width)
    side = (width // 2, width)
    return call(
        residual_back_body, after, gn2, hbm(cot), hbm(res), hbm(mixed), hbm(wo), g2,
        grid=(rows // tile,),
        in_specs=[t, t, t, t, whole(wo.shape), whole((1, width))],
        out_specs=(broad(width, tile), t, whole(side), whole(side), whole((8, width))),
        out_shape=(
            sds((width, rows), bf16),
            sds((rows, width), bf16),
            sds(side, bf16),
            sds(side, bf16),
            sds((8, width), f32),
        ),
        scratch=[pltpu.VMEM((width, width), f32)],
        us=6,
        name="residual_back",
    )


def heads_back_body(n1t, gmt, kt, v, prob, cen, cnt, inv, cl, gqkv, own, other, n1t_s, sem):
    copy = pltpu.make_async_copy(n1t, n1t_s, sem.at[0])
    copy.start()
    same = pair_mask()
    gqs, gks, gvs = [], [], []
    for p in range(PAIRS):
        cols = slice(2 * DH * p, 2 * DH * (p + 1))
        m = member_pair(cl[0], p).astype(bf16)
        over = inv[p]
        gco = (mm(gmt[cols, :], m) * same).astype(bf16)
        gco = (gco.astype(f32) * over).astype(bf16)
        pr = prob[:, 2 * LANES * p : 2 * LANES * (p + 1)]
        gvs.append(mm(pr, gco, NT).astype(bf16))
        pr32 = pr.astype(f32)
        weighted = pr32 * mm(v[:, cols], gco)
        inner = jnp.sum(weighted, axis=0, keepdims=True) * over
        gs = (weighted - pr32 * inner).astype(bf16)
        gc = (mm(kt[cols, :], gs) * (same * DH**-0.5)).astype(bf16)
        gc = (gc.astype(f32) / cnt[p]).astype(bf16)
        gks.append(mm(gs, cen[p], NT).astype(bf16))
        gqs.append(mm(m, gc, NT).astype(bf16))
    out = jnp.concatenate(gqs + gks + gvs, axis=1)
    gqkv[...] = out
    copy.wait()
    other[...] = mm(core_rows(n1t_s, 1), out).astype(bf16)
    own[...] = mm(core_rows(n1t_s, 0), out).astype(bf16)


def heads_back(g, n1t, gmt, qkvt, kv, prob, cen, cnt, inv, cl3, after=()):
    width, rows = n1t.shape
    sds = jax.ShapeDtypeStruct
    row_block = lambda off: pl.BlockSpec((WIDE, rows), lambda i: (off + g, 0))
    small = lambda n: pl.BlockSpec((PAIRS, n, 2 * LANES), lambda i: (g, 0, 0))
    side = (width // 2, 3 * WIDE)
    return call(
        heads_back_body, after,
        hbm(n1t), gmt, hbm(qkvt), hbm(kv), hbm(prob), hbm(cen), hbm(cnt), hbm(inv), cl3,
        grid=(1,),
        in_specs=[
            ANY,
            row_block(0),
            row_block(STEPS),
            pl.BlockSpec((rows, WIDE), lambda i: (0, STEPS + g)),
            pl.BlockSpec((rows, GROUP * LANES), lambda i: (0, g)),
            small(2 * DH), small(1), small(1),
            pl.BlockSpec((1, rows, GROUP), lambda i: (g, 0, 0)),
        ],
        out_specs=(whole((rows, 3 * WIDE)), whole(side), whole(side)),
        out_shape=(sds((rows, 3 * WIDE), bf16), sds(side, bf16), sds(side, bf16)),
        scratch=[pltpu.VMEM((width, rows), bf16), pltpu.SemaphoreType.DMA((1,))],
        us=6,
        name="heads_back",
    )


def project_back_body(*refs):
    gs, (w, tok, ga, g1, dx, vecs) = refs[:STEPS], refs[STEPS:]
    step = pl.program_id(0)
    g = None
    for n in range(STEPS):
        for part in range(3):
            w0 = part * STEPS * WIDE + n * WIDE
            t = mm(gs[n][:, part * WIDE : (part + 1) * WIDE], w[:, w0 : w0 + WIDE], NT)
            g = t if g is None else g + t
    xhat, r = row_stats(tok[...].astype(f32))
    dx[...] = (ga[...].astype(f32) + norm_back(g, g1[...], xhat, r)).astype(bf16)

    @pl.when(step == 0)
    def _():
        vecs[...] = jnp.zeros(vecs.shape, f32)

    vecs[0:1, :] += jnp.sum(g * xhat, axis=0, keepdims=True)
    vecs[1:2, :] += jnp.sum(g, axis=0, keepdims=True)


def project_back(gs, wqkv, tok, ga, g1, after=()):
    rows, width = tok.shape
    tile = 512
    sds = jax.ShapeDtypeStruct
    t = tall(tile, width)
    return call(
        project_back_body, after, *gs, hbm(wqkv), hbm(tok), ga, g1,
        grid=(rows // tile,),
        in_specs=[tall(tile, 3 * WIDE)] * STEPS + [whole(wqkv.shape), t, t, whole((1, width))],
        out_specs=(t, whole((8, width))),
        out_shape=(sds((rows, width), bf16), sds((8, width), f32)),
        us=0.1,
        name="project_back",
    )


def assemble_body(where, first, *refs):
    pieces, (out, vecs, held, sem) = refs[:8], refs[8:]
    step = pl.program_id(0)
    n = out.shape[0] // 2
    width = out.shape[1] // 3
    wide = held.shape[2]

    @pl.when(step == 0)
    def _():
        for q, piece in enumerate(pieces):
            pltpu.make_async_copy(piece, held.at[q], sem.at[q]).start()

    for part in range(3):
        cols = slice(part * WIDE, (part + 1) * WIDE)
        out[:, part * width : part * width + WIDE] = first[:, cols].astype(f32)
    for q, piece in enumerate(pieces):

        @pl.when(step == q // 2)
        def _(q=q, piece=piece):
            rows = pl.ds(pl.multiple_of(((where[1] ^ q) & 1) * n, n), n)
            pltpu.make_async_copy(piece, held.at[q], sem.at[q]).wait()
            for part in range(3):
                for m in range(STEPS - 1):
                    at = part * width + (m + 1) * WIDE
                    col = (3 * m + part) * WIDE
                    out[rows, at : at + WIDE] = held[q, :n, col : col + WIDE].astype(f32)

    @pl.when(step == 2)
    def _():
        parts = [held[q, n : n + 16, :].astype(f32) for q in range(4)]
        total = None
        for j in range(4):
            term = None
            for rel, x in enumerate(parts):
                x = jnp.where((where[1] ^ rel) == j, x, 0.0)
                term = x if term is None else term + x
            total = term if total is None else total + term
        per = wide // width
        vecs[...] = jnp.zeros(vecs.shape, f32)
        for r in range(4 // per):
            for m in range(per):
                vecs[r * per + m, :] = total[r, m * width : (m + 1) * width]


def assemble(core, spot, first, mine, got):
    width = first.shape[0]
    n = width // 4

    def place(i, where):
        return ((where[0] ^ (i // 2)) * 2 + ((where[1] // 2) ^ lax.rem(i, 2)), 0)

    return pl.pallas_call(
        assemble_body,
        grid_spec=pltpu.PrefetchScalarGridSpec(
            num_scalar_prefetch=1,
            grid=(4,),
            in_specs=[pl.BlockSpec((n, 3 * WIDE), place)] + [ANY] * 8,
            out_specs=(
                pl.BlockSpec((n, 3 * width), place),
                pl.BlockSpec((8, width), lambda i, where: (0, 0)),
            ),
            scratch_shapes=[
                pltpu.VMEM((8,) + mine[0].shape, bf16),
                pltpu.SemaphoreType.DMA((8,)),
            ],
        ),
        out_shape=(pltpu.HBM((width, 3 * width), f32), jax.ShapeDtypeStruct((8, width), f32)),
        compiler_params=pltpu.CompilerParams(vmem_limit_bytes=16 * MIB),
        cost_estimate=cost(3),
        name="assemble",
    )(jnp.stack([core, spot]), first, *mine, *got)


def finish_body(where, *refs):
    early, early_got, a, a_got, b, b_got = (refs[:4], refs[4:8], *refs[8:12])
    grad_out, first, grad_in, grad_back, token = refs[12:]
    token[0, 0] = 0.0
    core, spot = where[0], where[1]
    n, wide = early[0].shape
    width = grad_out.shape[1]
    for side, group in enumerate((early, early_got)):
        for rel, x in enumerate(group):
            at = pl.multiple_of(((core ^ side) * 4 + (spot ^ rel)) * n, n)
            grad_out[pl.ds(at, n), :] = x[:, :width].astype(f32)
            first[pl.ds(at, n), :] = x[:, width:]
    n = a.shape[0]
    for side, x in enumerate((a, a_got)):
        at = pl.multiple_of(((spot & 1) ^ side) * n, n)
        grad_in[pl.ds(at, n), :] = x[...].astype(f32)
    lo = jnp.where((spot >> 1) == 0, b[...], b_got[...])
    hi = jnp.where((spot >> 1) == 0, b_got[...], b[...])
    grad_back[...] = jnp.concatenate([lo, hi], axis=0).astype(f32).T


def finish(core, spot, early, early_got, mine, gots, half, hidden):
    wide = early[0].shape[1]
    width = 2 * half
    V = pl.BlockSpec(memory_space=pltpu.VMEM)
    return pl.pallas_call(
        finish_body,
        in_specs=[SCALAR] + [V] * 12,
        out_specs=(V, V, V, V, SCALAR),
        out_shape=(
            jax.ShapeDtypeStruct((width, width), f32),
            jax.ShapeDtypeStruct((width, wide - width), bf16),
            jax.ShapeDtypeStruct((half, hidden), f32),
            jax.ShapeDtypeStruct((hidden, half), f32),
            TOKEN,
        ),
        compiler_params=pltpu.CompilerParams(vmem_limit_bytes=24 * MIB),
        cost_estimate=cost(4),
        name="finish",
    )(jnp.stack([core, spot]), *early, *early_got, mine[0], gots[0], mine[1], gots[1])


def gelu_parts(x):
    t = 1.0 / (1.0 + (0.3275911 * 0.5**0.5) * jnp.abs(x))
    e = jnp.exp(-0.5 * x * x)
    poly = t * (
        0.254829592
        + t * (-0.284496736 + t * (1.421413741 + t * (-1.453152027 + t * 1.061405429)))
    )
    q = 0.5 * poly * e
    phi = jnp.where(x >= 0, 1.0 - q, q)
    return x * phi, phi + x * e * 0.3989422804014327


def feed_forward_body(first, places, n_after, *refs):
    n_w = len(places)
    n2, cot = refs[:2]
    weights = refs[2 : 2 + n_w]
    i = 2 + n_w
    if not first:
        gn_in = refs[i]
        i += 1
    i += n_after
    br, gn, own, other, token = refs[i : i + 5]
    i += 5
    token[0, 0] = 0.0
    n2t_s, cott_s, up_s, down_s, act_s, gp_s, weight_sem = refs[i:]
    rows, width = n2.shape
    hidden = up_s.shape[1]
    half = width // 2
    core = lax.axis_index("mod")
    spot = lax.rem(lax.axis_index("dp"), 4)
    ups, downs = [], []

    def load(group, source, target):
        at = weight_sem.at[len(ups) + len(downs)]
        group.append(pltpu.make_async_copy(source, target, at))

    chunks = hidden // half
    n_up, n_down = half // 4, hidden // 4
    for ref, (kind, core_rel, spot_rel) in zip(weights, places):
        d0 = pl.multiple_of((core ^ core_rel) * half, half)
        if kind == "up":
            load(ups, ref, up_s.at[pl.ds(d0, half), :])
        elif kind == "down":
            load(downs, ref, down_s.at[:, pl.ds(d0, half)])
        else:
            rels = (spot_rel,) if kind == "piece" else range(4)
            for n, rel in enumerate(rels):
                r0 = n * (chunks * n_up + n_down)
                u0 = pl.multiple_of(d0 + (spot ^ rel) * n_up, n_up)
                for m in range(chunks):
                    load(
                        ups,
                        ref.at[pl.ds(r0 + m * n_up, n_up), :],
                        up_s.at[pl.ds(u0, n_up), pl.ds(m * half, half)],
                    )
                f0 = pl.multiple_of((spot ^ rel) * n_down, n_down)
                load(
                    downs,
                    ref.at[pl.ds(r0 + chunks * n_up, n_down), :],
                    down_s.at[pl.ds(f0, n_down), pl.ds(d0, half)],
                )
    for copy in [*ups, *downs]:
        copy.start()
    n2t_s[...] = n2[...].T
    cott_s[...] = cot[...].T
    for copy in [*ups, *downs]:
        copy.wait()
    h = mm(n2[...], up_s[...])
    ga = mm(cot[...], down_s[...], NT)
    act, slope = gelu_parts(h)
    act_s[...] = act.astype(bf16)
    gp_s[...] = (ga * slope).astype(bf16)

    tall_tile, deep = min(512, rows), 256
    for r0 in range(0, rows, tall_tile):
        for c0 in range(0, width, deep):
            sub, cols = slice(r0, r0 + tall_tile), slice(c0, c0 + deep)
            sums = mm(gp_s[sub, :], up_s[cols, :], NT)
            if not first:
                sums += gn_in[sub, cols].astype(f32)
            gn[sub, cols] = sums.astype(bf16)
            br[sub, cols] = mm(act_s[sub, :], down_s[:, cols]).astype(bf16)
    for n, (left, right) in enumerate(((n2t_s, gp_s), (cott_s, act_s))):
        for out, rel in ((other, 1), (own, 0)):
            at = pl.ds(pl.multiple_of((core ^ rel) * half, half), half)
            for c0 in range(0, hidden, deep):
                cols = slice(c0, min(c0 + deep, hidden))
                out[n, :, cols] = mm(left[at, :], right[:, cols]).astype(bf16)


def feed_forward(n2, cot, pieces, gn, hidden, after=()):
    rows, width = n2.shape
    half = width // 2
    places = tuple(place for _, place in pieces)
    each = hidden // half + 1
    n_loads = sum({"piece": each, "pieces": 4 * each}.get(place[0], 1) for place in places)
    args = [n2, cot] + [a for a, _ in pieces] + ([] if gn is None else [gn]) + list(after)
    specs = [HERE, HERE] + [ANY] * len(pieces) + ([] if gn is None else [HERE]) + [ANY] * len(after)
    sds = jax.ShapeDtypeStruct
    V = pltpu.VMEM
    return pl.pallas_call(
        functools.partial(feed_forward_body, gn is None, places, len(after)),
        in_specs=specs,
        out_specs=(HERE,) * 4 + (SCALAR,),
        out_shape=(
            sds((rows, width), bf16),
            sds((rows, width), bf16),
            sds((2, half, hidden), bf16),
            sds((2, half, hidden), bf16),
            TOKEN,
        ),
        scratch_shapes=[
            V((width, rows), bf16),
            V((width, rows), bf16),
            V((width, hidden), bf16),
            V((hidden, width), bf16),
            V((rows, hidden), bf16),
            V((rows, hidden), bf16),
            pltpu.SemaphoreType.DMA((n_loads,)),
        ],
        compiler_params=pltpu.CompilerParams(vmem_limit_bytes=34 * MIB),
        cost_estimate=cost(11),
        name="feed_forward",
    )(*args)


def behind(x, token):
    return x + token.reshape((1,) * x.ndim).astype(x.dtype)


def zero_of(x):
    return x[(slice(0, 1),) * x.ndim].reshape(1, 1) * 0


def flip(x, axis, bit):
    n = lax.axis_size(axis)
    return lax.ppermute(x, axis, [(i, i ^ (1 << bit)) for i in range(n)])


def shift(x, axis, rel):
    n = lax.axis_size(axis)
    return lax.ppermute(x, axis, [(i, i ^ rel) for i in range(n)])


def turn(x, axis):
    n = lax.axis_size(axis)
    return lax.ppermute(x, axis, [(i, (i + 1) % n) for i in range(n)])


def take(x, index, n):
    return lax.dynamic_slice_in_dim(x, index * n, n, 0)


def bits(axis):
    return lax.axis_size(axis).bit_length() - 1


def group_sum(x):
    for b in range(2, bits("dp")):
        x = x + flip(x, "dp", b)
    return x


def column_half(x, index):
    n = x.shape[1] // 2
    return lax.dynamic_slice_in_dim(x, index * n, n, 1)


def column_block(x, index):
    n = x.shape[1] // lax.axis_size("hid")
    return lax.dynamic_slice_in_dim(x, index * n, n, 1)


def place_columns(parts, zed, reverse=False):
    n = parts[0].shape[1]
    out = jnp.zeros((parts[0].shape[0], n * len(parts)), parts[0].dtype)
    top = bits("hid") - 1
    for rel, x in enumerate(parts):
        index = zed ^ rel
        if reverse:
            index = sum(((index >> b) & 1) << (top - b) for b in range(top + 1))
        out = lax.dynamic_update_slice_in_dim(out, x, index * n, 1)
    return out


def in_order(parts, index):
    held = jnp.zeros((len(parts),) + parts[0].shape, parts[0].dtype)
    for rel, x in enumerate(parts):
        held = lax.dynamic_update_slice_in_dim(held, x[None], index ^ rel, 0)
    return jnp.sum(held.astype(f32), axis=0).astype(parts[0].dtype)


def sort_rows(x, y, mine):
    return jnp.where(mine == 0, jnp.concatenate([x, y]), jnp.concatenate([y, x]))


def add_rows(x, rider):
    rows = rider.reshape(-1, x.shape[1])
    pad = -rows.shape[0] % 16
    return jnp.concatenate([x, rows, jnp.zeros((pad, x.shape[1]), x.dtype)])


def cut_rows(x, n, shape):
    width = x.shape[1]
    return x[:n], x[n : n + shape[0] * shape[1] // width].reshape(shape)


def plane_sends(x, spot):
    n = x.shape[0] // 4
    return [take(x, spot ^ rel, n) for rel in (1, 2, 3)], take(x, spot, n)


def plane_near(sends):
    return [shift(x, "dp", rel) for rel, x in zip((1, 2, 3), sends)]


def per_device(
    tokens, clusters, key_mask, query_key_value_weight, attention_output_weight, up_weight,
    down_weight, gain_one, shift_one, gain_two, shift_two, cotangent,
):
    rows, width = tokens.shape
    half = width // 2
    hidden = up_weight.shape[1]
    ring = lax.axis_size("hid")
    core = lax.axis_index("mod")
    spot = lax.rem(lax.axis_index("dp"), 4)
    spot_bits = (spot & 1, spot >> 1)

    quarter = take(up_weight, spot, half // 4)
    piece = jnp.concatenate(
        [quarter[:, m : m + half] for m in range(0, hidden, half)]
        + [take(down_weight, spot, hidden // 4)]
    )
    up_other, down_other = flip(up_weight, "mod", 0), flip(down_weight, "mod", 0)
    slots = [
        [
            (up_weight, ("up", 0, None)),
            (down_weight, ("down", 0, None)),
            (up_other, ("up", 1, None)),
            (down_other, ("down", 1, None)),
        ]
    ]

    cl3 = clusters.reshape(rows, STEPS, GROUP).transpose(1, 0, 2)
    keep = key_mask.reshape(rows, 1)
    vec = lambda x: x.reshape(1, width)
    g1, s1, g2, s2 = vec(gain_one), vec(shift_one), vec(gain_two), vec(shift_two)
    wqkv, wo = query_key_value_weight, attention_output_weight

    kv, qkvt, n1t, token = project(tokens, wqkv, g1, s1, after=[piece])

    def spread(x):
        return [shift(x, "dp", rel) for rel in (1, 2, 3)]

    def held_slot(x, near, token):
        held = [x] + near
        both = behind(jnp.concatenate(held), token)
        return both, [(v, ("piece", 0, rel)) for rel, v in enumerate(held)] + [
            (flip(both, "mod", 0), ("pieces", 1, None))
        ]

    def plane(part, token):
        n = part.shape[1] // 2
        sends = [behind(take(part[i], 1 - spot_bits[i], n), token) for i in (0, 1)]
        keep = [take(part[i], spot_bits[i], n) for i in (0, 1)]
        return keep, [flip(sends[i], "dp", i) for i in (0, 1)], sends

    def finish_plane(launched, token):
        keep, got, _ = launched
        return jnp.stack([a + behind(b, token) for a, b in zip(keep, got)])

    x = behind(turn(piece, "hid"), token)
    near = spread(x)
    far = turn(x, "hid")
    mixed, prob, cen, cnt, inv, res, n2, token = attend(
        tokens, kv, qkvt, cl3, keep, wo, g2, s2, after=[x, up_other, down_other]
    )
    n_slots = ring
    gn2, branches = None, []
    raw, part, share = [None] * n_slots, [None] * n_slots, [None] * n_slots
    for s in range(n_slots):
        first = []
        if s + 1 < n_slots:
            both, slot = held_slot(x, near, token)
            slots.append(slot)
            first += near + [both]
        if s + 2 < n_slots:
            x = behind(far, token)
            near = spread(x)
            first.append(x)
        if s + 3 < n_slots:
            far = turn(x, "hid")
        if s >= 1:
            got = flip(raw[s - 1][1], "mod", 0)
        if s >= 2:
            share[s - 2] = plane(part[s - 2], token)
            first += share[s - 2][2]
        if s >= 3:
            first += share[s - 3][1]
        br, gn2, own, other, token = feed_forward(
            n2, cotangent, slots[s], gn2, hidden, after=first
        )
        branches.append(br)
        raw[s] = (own, other)
        if s >= 1:
            part[s - 1] = raw[s - 1][0] + behind(got, token)
    last = n_slots - 1
    got = flip(raw[last][1], "mod", 0)
    share[last - 1] = plane(part[last - 1], token)
    share = [finish_plane(x, token) for x in share[: last - 1]] + share[last - 1 :]
    one = turn(share[1], "hid")
    gmt, ga, go_own, go_other, vecs_two, token = residual_back(
        gn2, cotangent, res, mixed, wo, g2,
        after=share[last - 2 : last - 1] + share[last - 1][2],
    )
    part[last] = raw[last][0] + behind(got, token)
    share[last] = plane(part[last], token)
    gs, ws = [None] * STEPS, [None] * STEPS
    heads = functools.partial(
        heads_back,
        n1t=n1t, gmt=gmt, qkvt=qkvt, kv=kv, prob=prob, cen=cen, cnt=cnt, inv=inv, cl3=cl3,
    )
    gs[0], own, other, after0 = heads(0, after=share[last - 1][1] + share[last][2])
    share[last - 1] = finish_plane(share[last - 1], token)
    early_send = jnp.concatenate([go_other, other], axis=1)
    early = jnp.concatenate([go_own, own], axis=1)
    early_got = flip(early_send, "mod", 0)
    total = behind(one, after0) + share[2 % ring]
    one = turn(total, "hid")
    gs[1], own1, other1, after1 = heads(1, after=[early_send, total] + share[last][1])
    share[last] = finish_plane(share[last], after1)
    early = early + behind(early_got, after1)
    n = half // 4
    zed = lax.axis_index("hid")
    z_bits = [(zed >> b) & 1 for b in range(bits("hid"))]
    early_sends, early = plane_sends(early, spot)
    early_near = plane_near(early_sends)
    late_got = flip(other1, "mod", 0)
    gs[2], own2, other2, after2 = heads(2, after=early_sends)

    for s in range(3, ring):
        total = behind(one, after2) + share[s]
        one = turn(total, "hid")
    late_got2 = flip(other2, "mod", 0)
    output = behind(res, after2).astype(f32)
    for x in branches:
        output = output + x.astype(f32)
    output = output.astype(bf16)
    token = fence(after2, output, total, late_got, late_got2, *early_near)
    late_left = own1 + behind(late_got, token)
    late_right = own2 + behind(late_got2, token)
    late_sends, late = plane_sends(jnp.concatenate([late_left, late_right], axis=1), spot)
    late_near = plane_near(late_sends)
    early = group_sum(behind(early, token) + early_near[0] + early_near[1] + early_near[2])
    send = column_half(early, 1 - z_bits[0])
    got = flip(send, "hid", 0)
    input_grad, vecs_one, after3 = project_back(
        gs, wqkv, tokens, ga, g1, after=[*late_sends, send]
    )
    early = column_half(early, z_bits[0]) + behind(got, after3)
    for b in range(1, bits("hid")):
        send = column_half(early, 1 - z_bits[b])
        early = column_half(early, z_bits[b]) + flip(send, "hid", b)
    vecs = jnp.concatenate([vecs_one[:2], vecs_two[:2]]).astype(bf16)
    vecs = vecs + flip(vecs, "mod", 0)
    total = behind(one, zero_of(send)) + share[0]
    keeps = [take(x, spot_bits[i], x.shape[0] // 2) for x, i in zip(total, (1, 0))]
    gots = [
        flip(take(x, 1 - spot_bits[i], x.shape[0] // 2), "dp", i) for x, i in zip(total, (1, 0))
    ]
    token = fence(early, vecs, *late_near)
    late = group_sum(late + behind(late_near[0], token) + late_near[1] + late_near[2])
    late_z = [column_block(late, zed ^ rel) for rel in range(lax.axis_size("hid"))]
    sends = [add_rows(x, vecs) for x in late_z[1:]]
    got = [shift(x, "hid", rel + 1) for rel, x in enumerate(sends)]
    early = behind(early, token)
    early_z = [early] + [shift(early, "hid", rel) for rel in range(1, lax.axis_size("hid"))]
    early = place_columns(early_z, zed, reverse=True)
    mine = [group_sum(x + behind(y, token)) for x, y in zip(keeps, gots)]
    gots = [flip(x, "dp", i) for x, i in zip(mine, (1, 0))]
    token = fence(early)
    early = behind(early, token)
    early_near = plane_near([early] * 3)
    got = [cut_rows(x, late.shape[0], vecs.shape) for x in got]
    late = late_z[0]
    for x, _ in got:
        late = late + behind(x, token)
    vecs = in_order([vecs] + [x for _, x in got], zed)
    mine = [
        sort_rows(x, behind(y, token), spot_bits[i]) for x, y, i in zip(mine, gots, (1, 0))
    ]
    late_z = [late] + [shift(late, "hid", rel) for rel in range(1, lax.axis_size("hid"))]
    gots = [flip(x, "dp", i) for x, i in zip(mine, (0, 1))]
    token = fence(*early_near)
    token = fence(token, *late_z)
    loaded = add_rows(behind(place_columns(late_z, zed), token), group_sum(vecs))
    late_near = plane_near([loaded] * 3)
    early = [behind(x, token) for x in [early] + early_near]
    early_got = [flip(x, "mod", 0) for x in early]
    grad_out, first, grad_in, grad_back, token = finish(
        core, spot, early, early_got, mine, gots, half, hidden
    )
    pieces = [loaded] + [behind(x, token) for x in late_near]
    got = [flip(x, "mod", 0) for x in pieces]
    gqkv, vecs = assemble(core, spot, first, pieces, got)
    return (
        output,
        input_grad,
        gqkv,
        grad_out,
        grad_in,
        grad_back,
        vecs[0],
        vecs[1],
        vecs[2],
        vecs[3],
    )


def solution(mesh):
    every = P(("dp", "hid", "mod"), None)
    placed = (
        every, every, P(("dp", "hid", "mod")), P(), P(), P("mod", "hid"), P("hid", "mod"),
        P(), P(), P(), P(), every,
    )
    return jax.shard_map(
        per_device,
        mesh=mesh,
        in_specs=placed,
        out_specs=(every, every, P(), P(), P("mod", "hid"), P("hid", "mod"), P(), P(), P(), P()),
        check_vma=False,
    )
```

```python
import functools

import jax
import jax.numpy as jnp
from jax import lax
from jax.experimental import pallas as pl
from jax.experimental.pallas import tpu as pltpu
from jax.sharding import PartitionSpec as P

H = 12
DH = 64
LEN = 1024
LANES = 128
GROUP = 4
PAIRS = GROUP // 2
STEPS = H // GROUP
WIDE = GROUP * DH

EPSILON = 1e-05
NEGATIVE = -1e30
MIB = 2**20
f32 = jnp.float32
bf16 = jnp.bfloat16

NN = (((1,), (0,)), ((), ()))
NT = (((1,), (1,)), ((), ()))
TN = (((0,), (0,)), ((), ()))
ANY = pl.BlockSpec(memory_space=pl.ANY)
SCALAR = pl.BlockSpec(memory_space=pltpu.SMEM)
HERE = pl.BlockSpec(memory_space=pltpu.VMEM)
TOKEN = jax.ShapeDtypeStruct((1, 1), f32)


def mm(a, b, dims=NN):
    return lax.dot_general(a, b, dims, preferred_element_type=f32)


def row_stats(x):
    mean = jnp.mean(x, axis=-1, keepdims=True)
    centered = x - mean
    var = jnp.mean(centered * centered, axis=-1, keepdims=True)
    r = lax.rsqrt(var + EPSILON)
    return centered * r, r


def norm_back(g, gain, xhat, r):
    gx = g * gain
    return r * (
        gx
        - jnp.mean(gx, axis=-1, keepdims=True)
        - xhat * jnp.mean(gx * xhat, axis=-1, keepdims=True)
    )


def member_pair(cl, p):
    rows = cl.shape[0]
    lane = lax.broadcasted_iota(jnp.int32, (rows, LANES), 1)
    halves = [(cl[:, 2 * p + i : 2 * p + i + 1] == lane).astype(f32) for i in (0, 1)]
    return jnp.concatenate(halves, axis=1)


def pair_mask():
    d = lax.broadcasted_iota(jnp.int32, (2 * DH, 2 * LANES), 0)
    c = lax.broadcasted_iota(jnp.int32, (2 * DH, 2 * LANES), 1)
    return ((d >= DH) == (c >= LANES)).astype(f32)


def hbm(x):
    return pltpu.with_memory_space_constraint(x, pltpu.HBM)


def cost(us):
    return pl.CostEstimate(flops=int(us * 1.15e9), bytes_accessed=int(us * 1e6), transcendentals=0)


def whole(shape):
    return pl.BlockSpec(shape, lambda i: (0,) * len(shape))


def tall(rows, width):
    return pl.BlockSpec((rows, width), lambda i: (i, 0))


def broad(width, rows):
    return pl.BlockSpec((width, rows), lambda i: (0, i))


def call(body, after, *args, grid, in_specs, out_specs, out_shape, scratch=(), us, name, vmem=34):
    n_in, n_after = len(args), len(after)
    n_out = len(out_shape)

    def run(*refs):
        refs = refs[:n_in] + refs[n_in + n_after :]
        refs[n_in + n_out][0, 0] = 0.0
        body(*refs[: n_in + n_out], *refs[n_in + n_out + 1 :])

    return pl.pallas_call(
        run,
        grid=grid,
        in_specs=list(in_specs) + [ANY] * n_after,
        out_specs=tuple(out_specs) + (SCALAR,),
        out_shape=tuple(out_shape) + (TOKEN,),
        scratch_shapes=list(scratch),
        compiler_params=pltpu.CompilerParams(vmem_limit_bytes=vmem * MIB),
        cost_estimate=cost(us),
        name=name,
    )(*args, *after)


def fence(*arrays):
    def run(*refs):
        refs[-1][0, 0] = 0.0

    return pl.pallas_call(
        run,
        in_specs=[ANY] * len(arrays),
        out_specs=SCALAR,
        out_shape=TOKEN,
        compiler_params=pltpu.CompilerParams(vmem_limit_bytes=MIB),
        cost_estimate=cost(0.3),
        name="fence",
    )(*arrays)


def project_body(tok, w, g1, s1, kv, qkvt, n1t):
    width = tok.shape[1]
    xhat, _ = row_stats(tok[...].astype(f32))
    n1 = (xhat * g1[...] + s1[...]).astype(bf16)
    n1t[...] = n1.T
    for part in range(3):
        cols = slice(part * width, (part + 1) * width)
        x = mm(n1, w[:, cols]).astype(bf16)
        qkvt[cols, :] = x.T
        if part:
            kv[:, (part - 1) * width : part * width] = x


def project(tokens, wqkv, g1, s1, after=()):
    rows, width = tokens.shape
    tile = 512
    return call(
        project_body, after, hbm(tokens), hbm(wqkv), g1, s1,
        grid=(rows // tile,),
        in_specs=[tall(tile, width), whole(wqkv.shape), whole((1, width)), whole((1, width))],
        out_specs=(tall(tile, 2 * width), broad(3 * width, tile), broad(width, tile)),
        out_shape=(
            pltpu.HBM((rows, 2 * width), bf16),
            pltpu.HBM((3 * width, rows), bf16),
            pltpu.HBM((width, rows), bf16),
        ),
        us=7,
        name="project",
    )


def attend_body(
    tok, qt, k, vt, cl, keep, wo, g2, s2, mixed, prob, cen, cnt, inv, res, n2,
    acc, bias, tok_s, sem,
):
    step = pl.program_id(0)
    tile = 256
    rows = tok_s.shape[0]
    same = pair_mask()

    @pl.when(step == 0)
    def _():
        pltpu.make_async_copy(tok, tok_s, sem.at[0]).start()
        column = jnp.where(keep[...] == 1, 0.0, NEGATIVE)
        bias[...] = jnp.broadcast_to(column, bias.shape)

    shut = jnp.concatenate([bias[...], bias[...]], axis=1)
    parts = []
    for p in range(PAIRS):
        cols = slice(2 * DH * p, 2 * DH * (p + 1))
        m32 = member_pair(cl[0], p)
        m = m32.astype(bf16)
        count = jnp.maximum(jnp.sum(m32, axis=0, keepdims=True), 1.0)
        centre = (mm(qt[cols, :], m) / count * same).astype(bf16) * bf16(DH**-0.5)
        score = mm(k[:, cols], centre) + shut
        powered = jnp.exp(score - jnp.max(score, axis=0, keepdims=True))
        over = 1.0 / jnp.sum(powered, axis=0, keepdims=True)
        powered = powered.astype(bf16)
        centre_out = (mm(vt[cols, :], powered) * (over * same)).astype(bf16)
        parts.append(mm(m, centre_out, NT).astype(bf16))
        prob[:, 2 * LANES * p : 2 * LANES * (p + 1)] = powered
        cen[p] = centre
        cnt[p] = count
        inv[p] = over
    mix = jnp.concatenate(parts, axis=1)
    mixed[...] = mix
    part = mm(mix, wo[...])

    @pl.when(step == 0)
    def _():
        acc[...] = part

    @pl.when(step > 0)
    def _():
        acc[...] += part

    @pl.when(step == pl.num_programs(0) - 1)
    def _():
        pltpu.make_async_copy(tok, tok_s, sem.at[0]).wait()

        def second_norm(i, _):
            at = pl.ds(pl.multiple_of(i * tile, tile), tile)
            x = tok_s[at, :].astype(f32) + acc[at, :]
            res[at, :] = x.astype(bf16)
            xhat, _r = row_stats(x)
            n2[at, :] = (xhat * g2[...] + s2[...]).astype(bf16)
            return 0

        lax.fori_loop(0, rows // tile, second_norm, 0)


def attend(tokens, kv, qkvt, cl3, keep, wo, g2, s2, after=()):
    rows, width = tokens.shape
    vec = whole((1, width))
    cols = pl.BlockSpec((rows, WIDE), lambda g: (0, g))
    row_block = lambda off: pl.BlockSpec((WIDE, rows), lambda g: (off + g, 0))
    small = lambda n: pl.BlockSpec((PAIRS, n, 2 * LANES), lambda g: (g, 0, 0))
    return call(
        attend_body, after, hbm(tokens), hbm(qkvt), hbm(kv), hbm(qkvt), cl3, keep, hbm(wo), g2, s2,
        grid=(STEPS,),
        in_specs=[
            ANY,
            row_block(0), cols, row_block(2 * STEPS),
            pl.BlockSpec((1, rows, GROUP), lambda g: (g, 0, 0)),
            whole((rows, 1)),
            pl.BlockSpec((WIDE, width), lambda g: (g, 0)),
            vec, vec,
        ],
        out_specs=(
            cols,
            pl.BlockSpec((rows, GROUP * LANES), lambda g: (0, g)),
            small(2 * DH), small(1), small(1),
            whole((rows, width)),
            whole((rows, width)),
        ),
        out_shape=(
            pltpu.HBM((rows, width), bf16),
            pltpu.HBM((rows, H * LANES), bf16),
            pltpu.HBM((H // 2, 2 * DH, 2 * LANES), bf16),
            pltpu.HBM((H // 2, 1, 2 * LANES), f32),
            pltpu.HBM((H // 2, 1, 2 * LANES), f32),
            pltpu.HBM((rows, width), bf16),
            jax.ShapeDtypeStruct((rows, width), bf16),
        ),
        scratch=[
            pltpu.VMEM((rows, width), f32),
            pltpu.VMEM((rows, LANES), f32),
            pltpu.VMEM((rows, width), bf16),
            pltpu.SemaphoreType.DMA((1,)),
        ],
        us=16,
        name="attend",
        vmem=36,
    )


def core_rows(ref, rel):
    n = ref.shape[0] // 2
    at = pl.multiple_of((lax.axis_index("mod") ^ rel) * n, n)
    return ref[pl.ds(at, n), :]


def residual_back_body(gn2, cot, res, mixed, wo, g2, gmt, ga, own, other, vecs, acc):
    step = pl.program_id(0)
    g = gn2[...].astype(f32)
    xhat, r = row_stats(res[...].astype(f32))
    out = (cot[...].astype(f32) + norm_back(g, g2[...], xhat, r)).astype(bf16)
    ga[...] = out
    gmt[...] = mm(wo[...], out, NT).astype(bf16)
    part = mm(mixed[...], out, TN)
    gain = jnp.sum(g * xhat, axis=0, keepdims=True)
    shift_ = jnp.sum(g, axis=0, keepdims=True)

    @pl.when(step == 0)
    def _():
        acc[...] = part
        vecs[...] = jnp.zeros(vecs.shape, f32)

    @pl.when(step > 0)
    def _():
        acc[...] += part

    vecs[0:1, :] += gain
    vecs[1:2, :] += shift_

    @pl.when(step == pl.num_programs(0) - 1)
    def _():
        own[...] = core_rows(acc, 0).astype(bf16)
        other[...] = core_rows(acc, 1).astype(bf16)


def residual_back(gn2, cot, res, mixed, wo, g2, after=()):
    rows, width = cot.shape
    tile = 512
    sds = jax.ShapeDtypeStruct
    t = tall(tile, width)
    side = (width // 2, width)
    return call(
        residual_back_body, after, gn2, hbm(cot), hbm(res), hbm(mixed), hbm(wo), g2,
        grid=(rows // tile,),
        in_specs=[t, t, t, t, whole(wo.shape), whole((1, width))],
        out_specs=(broad(width, tile), t, whole(side), whole(side), whole((8, width))),
        out_shape=(
            sds((width, rows), bf16),
            sds((rows, width), bf16),
            sds(side, bf16),
            sds(side, bf16),
            sds((8, width), f32),
        ),
        scratch=[pltpu.VMEM((width, width), f32)],
        us=6,
        name="residual_back",
    )


def heads_back_body(n1t, gmt, kt, v, prob, cen, cnt, inv, cl, gqkv, own, other, n1t_s, sem):
    copy = pltpu.make_async_copy(n1t, n1t_s, sem.at[0])
    copy.start()
    same = pair_mask()
    gqs, gks, gvs = [], [], []
    for p in range(PAIRS):
        cols = slice(2 * DH * p, 2 * DH * (p + 1))
        m = member_pair(cl[0], p).astype(bf16)
        over = inv[p]
        gco = (mm(gmt[cols, :], m) * same).astype(bf16)
        gco = (gco.astype(f32) * over).astype(bf16)
        pr = prob[:, 2 * LANES * p : 2 * LANES * (p + 1)]
        gvs.append(mm(pr, gco, NT).astype(bf16))
        pr32 = pr.astype(f32)
        weighted = pr32 * mm(v[:, cols], gco)
        inner = jnp.sum(weighted, axis=0, keepdims=True) * over
        gs = (weighted - pr32 * inner).astype(bf16)
        gc = (mm(kt[cols, :], gs) * (same * DH**-0.5)).astype(bf16)
        gc = (gc.astype(f32) / cnt[p]).astype(bf16)
        gks.append(mm(gs, cen[p], NT).astype(bf16))
        gqs.append(mm(m, gc, NT).astype(bf16))
    out = jnp.concatenate(gqs + gks + gvs, axis=1)
    gqkv[...] = out
    copy.wait()
    other[...] = mm(core_rows(n1t_s, 1), out).astype(bf16)
    own[...] = mm(core_rows(n1t_s, 0), out).astype(bf16)


def heads_back(g, n1t, gmt, qkvt, kv, prob, cen, cnt, inv, cl3, after=()):
    width, rows = n1t.shape
    sds = jax.ShapeDtypeStruct
    row_block = lambda off: pl.BlockSpec((WIDE, rows), lambda i: (off + g, 0))
    small = lambda n: pl.BlockSpec((PAIRS, n, 2 * LANES), lambda i: (g, 0, 0))
    side = (width // 2, 3 * WIDE)
    return call(
        heads_back_body, after,
        hbm(n1t), gmt, hbm(qkvt), hbm(kv), hbm(prob), hbm(cen), hbm(cnt), hbm(inv), cl3,
        grid=(1,),
        in_specs=[
            ANY,
            row_block(0),
            row_block(STEPS),
            pl.BlockSpec((rows, WIDE), lambda i: (0, STEPS + g)),
            pl.BlockSpec((rows, GROUP * LANES), lambda i: (0, g)),
            small(2 * DH), small(1), small(1),
            pl.BlockSpec((1, rows, GROUP), lambda i: (g, 0, 0)),
        ],
        out_specs=(whole((rows, 3 * WIDE)), whole(side), whole(side)),
        out_shape=(sds((rows, 3 * WIDE), bf16), sds(side, bf16), sds(side, bf16)),
        scratch=[pltpu.VMEM((width, rows), bf16), pltpu.SemaphoreType.DMA((1,))],
        us=6,
        name="heads_back",
    )


def project_back_body(*refs):
    gs, (w, tok, ga, g1, dx, vecs) = refs[:STEPS], refs[STEPS:]
    step = pl.program_id(0)
    g = None
    for n in range(STEPS):
        for part in range(3):
            w0 = part * STEPS * WIDE + n * WIDE
            t = mm(gs[n][:, part * WIDE : (part + 1) * WIDE], w[:, w0 : w0 + WIDE], NT)
            g = t if g is None else g + t
    xhat, r = row_stats(tok[...].astype(f32))
    dx[...] = (ga[...].astype(f32) + norm_back(g, g1[...], xhat, r)).astype(bf16)

    @pl.when(step == 0)
    def _():
        vecs[...] = jnp.zeros(vecs.shape, f32)

    vecs[0:1, :] += jnp.sum(g * xhat, axis=0, keepdims=True)
    vecs[1:2, :] += jnp.sum(g, axis=0, keepdims=True)


def project_back(gs, wqkv, tok, ga, g1, after=()):
    rows, width = tok.shape
    tile = 512
    sds = jax.ShapeDtypeStruct
    t = tall(tile, width)
    return call(
        project_back_body, after, *gs, hbm(wqkv), hbm(tok), ga, g1,
        grid=(rows // tile,),
        in_specs=[tall(tile, 3 * WIDE)] * STEPS + [whole(wqkv.shape), t, t, whole((1, width))],
        out_specs=(t, whole((8, width))),
        out_shape=(sds((rows, width), bf16), sds((8, width), f32)),
        us=0.1,
        name="project_back",
    )


def assemble_body(where, first, *refs):
    pieces, (out, vecs, held, sem) = refs[:8], refs[8:]
    step = pl.program_id(0)
    n = out.shape[0] // 2
    width = out.shape[1] // 3
    wide = held.shape[2]

    @pl.when(step == 0)
    def _():
        for q, piece in enumerate(pieces):
            pltpu.make_async_copy(piece, held.at[q], sem.at[q]).start()

    for part in range(3):
        cols = slice(part * WIDE, (part + 1) * WIDE)
        out[:, part * width : part * width + WIDE] = first[:, cols].astype(f32)
    for q, piece in enumerate(pieces):

        @pl.when(step == q // 2)
        def _(q=q, piece=piece):
            rows = pl.ds(pl.multiple_of(((where[1] ^ q) & 1) * n, n), n)
            pltpu.make_async_copy(piece, held.at[q], sem.at[q]).wait()
            for part in range(3):
                for m in range(STEPS - 1):
                    at = part * width + (m + 1) * WIDE
                    col = (3 * m + part) * WIDE
                    out[rows, at : at + WIDE] = held[q, :n, col : col + WIDE].astype(f32)

    @pl.when(step == 2)
    def _():
        parts = [held[q, n : n + 16, :].astype(f32) for q in range(4)]
        total = None
        for j in range(4):
            term = None
            for rel, x in enumerate(parts):
                x = jnp.where((where[1] ^ rel) == j, x, 0.0)
                term = x if term is None else term + x
            total = term if total is None else total + term
        per = wide // width
        vecs[...] = jnp.zeros(vecs.shape, f32)
        for r in range(4 // per):
            for m in range(per):
                vecs[r * per + m, :] = total[r, m * width : (m + 1) * width]


def assemble(core, spot, first, mine, got):
    width = first.shape[0]
    n = width // 4

    def place(i, where):
        return ((where[0] ^ (i // 2)) * 2 + ((where[1] // 2) ^ lax.rem(i, 2)), 0)

    return pl.pallas_call(
        assemble_body,
        grid_spec=pltpu.PrefetchScalarGridSpec(
            num_scalar_prefetch=1,
            grid=(4,),
            in_specs=[pl.BlockSpec((n, 3 * WIDE), place)] + [ANY] * 8,
            out_specs=(
                pl.BlockSpec((n, 3 * width), place),
                pl.BlockSpec((8, width), lambda i, where: (0, 0)),
            ),
            scratch_shapes=[
                pltpu.VMEM((8,) + mine[0].shape, bf16),
                pltpu.SemaphoreType.DMA((8,)),
            ],
        ),
        out_shape=(pltpu.HBM((width, 3 * width), f32), jax.ShapeDtypeStruct((8, width), f32)),
        compiler_params=pltpu.CompilerParams(vmem_limit_bytes=16 * MIB),
        cost_estimate=cost(3),
        name="assemble",
    )(jnp.stack([core, spot]), first, *mine, *got)


def finish_body(where, *refs):
    early, early_got, a, a_got, b, b_got = (refs[:4], refs[4:8], *refs[8:12])
    grad_out, first, grad_in, grad_back, token = refs[12:]
    token[0, 0] = 0.0
    core, spot = where[0], where[1]
    n, wide = early[0].shape
    width = grad_out.shape[1]
    for side, group in enumerate((early, early_got)):
        for rel, x in enumerate(group):
            at = pl.multiple_of(((core ^ side) * 4 + (spot ^ rel)) * n, n)
            grad_out[pl.ds(at, n), :] = x[:, :width].astype(f32)
            first[pl.ds(at, n), :] = x[:, width:]
    n = a.shape[0]
    for side, x in enumerate((a, a_got)):
        at = pl.multiple_of(((spot & 1) ^ side) * n, n)
        grad_in[pl.ds(at, n), :] = x[...].astype(f32)
    lo = jnp.where((spot >> 1) == 0, b[...], b_got[...])
    hi = jnp.where((spot >> 1) == 0, b_got[...], b[...])
    grad_back[...] = jnp.concatenate([lo, hi], axis=0).astype(f32).T


def finish(core, spot, early, early_got, mine, gots, half, hidden):
    wide = early[0].shape[1]
    width = 2 * half
    V = pl.BlockSpec(memory_space=pltpu.VMEM)
    return pl.pallas_call(
        finish_body,
        in_specs=[SCALAR] + [V] * 12,
        out_specs=(V, V, V, V, SCALAR),
        out_shape=(
            jax.ShapeDtypeStruct((width, width), f32),
            jax.ShapeDtypeStruct((width, wide - width), bf16),
            jax.ShapeDtypeStruct((half, hidden), f32),
            jax.ShapeDtypeStruct((hidden, half), f32),
            TOKEN,
        ),
        compiler_params=pltpu.CompilerParams(vmem_limit_bytes=24 * MIB),
        cost_estimate=cost(4),
        name="finish",
    )(jnp.stack([core, spot]), *early, *early_got, mine[0], gots[0], mine[1], gots[1])


def gelu_parts(x):
    t = 1.0 / (1.0 + (0.3275911 * 0.5**0.5) * jnp.abs(x))
    e = jnp.exp(-0.5 * x * x)
    poly = t * (
        0.254829592
        + t * (-0.284496736 + t * (1.421413741 + t * (-1.453152027 + t * 1.061405429)))
    )
    q = 0.5 * poly * e
    phi = jnp.where(x >= 0, 1.0 - q, q)
    return x * phi, phi + x * e * 0.3989422804014327


def feed_forward_body(first, places, n_after, *refs):
    n_w = len(places)
    n2, cot = refs[:2]
    weights = refs[2 : 2 + n_w]
    i = 2 + n_w
    if not first:
        gn_in = refs[i]
        i += 1
    i += n_after
    br, gn, own, other, token = refs[i : i + 5]
    i += 5
    token[0, 0] = 0.0
    n2t_s, cott_s, up_s, down_s, act_s, gp_s, weight_sem = refs[i:]
    rows, width = n2.shape
    hidden = up_s.shape[1]
    half = width // 2
    core = lax.axis_index("mod")
    spot = lax.rem(lax.axis_index("dp"), 4)
    ups, downs = [], []

    def load(group, source, target):
        at = weight_sem.at[len(ups) + len(downs)]
        group.append(pltpu.make_async_copy(source, target, at))

    chunks = hidden // half
    n_up, n_down = half // 4, hidden // 4
    for ref, (kind, core_rel, spot_rel) in zip(weights, places):
        d0 = pl.multiple_of((core ^ core_rel) * half, half)
        if kind == "up":
            load(ups, ref, up_s.at[pl.ds(d0, half), :])
        elif kind == "down":
            load(downs, ref, down_s.at[:, pl.ds(d0, half)])
        else:
            rels = (spot_rel,) if kind == "piece" else range(4)
            for n, rel in enumerate(rels):
                r0 = n * (chunks * n_up + n_down)
                u0 = pl.multiple_of(d0 + (spot ^ rel) * n_up, n_up)
                for m in range(chunks):
                    load(
                        ups,
                        ref.at[pl.ds(r0 + m * n_up, n_up), :],
                        up_s.at[pl.ds(u0, n_up), pl.ds(m * half, half)],
                    )
                f0 = pl.multiple_of((spot ^ rel) * n_down, n_down)
                load(
                    downs,
                    ref.at[pl.ds(r0 + chunks * n_up, n_down), :],
                    down_s.at[pl.ds(f0, n_down), pl.ds(d0, half)],
                )
    for copy in [*ups, *downs]:
        copy.start()
    n2t_s[...] = n2[...].T
    cott_s[...] = cot[...].T
    for copy in [*ups, *downs]:
        copy.wait()
    h = mm(n2[...], up_s[...])
    ga = mm(cot[...], down_s[...], NT)
    act, slope = gelu_parts(h)
    act_s[...] = act.astype(bf16)
    gp_s[...] = (ga * slope).astype(bf16)

    tall_tile, deep = min(512, rows), 256
    for r0 in range(0, rows, tall_tile):
        for c0 in range(0, width, deep):
            sub, cols = slice(r0, r0 + tall_tile), slice(c0, c0 + deep)
            sums = mm(gp_s[sub, :], up_s[cols, :], NT)
            if not first:
                sums += gn_in[sub, cols].astype(f32)
            gn[sub, cols] = sums.astype(bf16)
            br[sub, cols] = mm(act_s[sub, :], down_s[:, cols]).astype(bf16)
    for n, (left, right) in enumerate(((n2t_s, gp_s), (cott_s, act_s))):
        for out, rel in ((other, 1), (own, 0)):
            at = pl.ds(pl.multiple_of((core ^ rel) * half, half), half)
            for c0 in range(0, hidden, deep):
                cols = slice(c0, min(c0 + deep, hidden))
                out[n, :, cols] = mm(left[at, :], right[:, cols]).astype(bf16)


def feed_forward(n2, cot, pieces, gn, hidden, after=()):
    rows, width = n2.shape
    half = width // 2
    places = tuple(place for _, place in pieces)
    each = hidden // half + 1
    n_loads = sum({"piece": each, "pieces": 4 * each}.get(place[0], 1) for place in places)
    args = [n2, cot] + [a for a, _ in pieces] + ([] if gn is None else [gn]) + list(after)
    specs = [HERE, HERE] + [ANY] * len(pieces) + ([] if gn is None else [HERE]) + [ANY] * len(after)
    sds = jax.ShapeDtypeStruct
    V = pltpu.VMEM
    return pl.pallas_call(
        functools.partial(feed_forward_body, gn is None, places, len(after)),
        in_specs=specs,
        out_specs=(HERE,) * 4 + (SCALAR,),
        out_shape=(
            sds((rows, width), bf16),
            sds((rows, width), bf16),
            sds((2, half, hidden), bf16),
            sds((2, half, hidden), bf16),
            TOKEN,
        ),
        scratch_shapes=[
            V((width, rows), bf16),
            V((width, rows), bf16),
            V((width, hidden), bf16),
            V((hidden, width), bf16),
            V((rows, hidden), bf16),
            V((rows, hidden), bf16),
            pltpu.SemaphoreType.DMA((n_loads,)),
        ],
        compiler_params=pltpu.CompilerParams(vmem_limit_bytes=34 * MIB),
        cost_estimate=cost(11),
        name="feed_forward",
    )(*args)


def behind(x, token):
    return x + token.reshape((1,) * x.ndim).astype(x.dtype)


def zero_of(x):
    return x[(slice(0, 1),) * x.ndim].reshape(1, 1) * 0


def flip(x, axis, bit):
    n = lax.axis_size(axis)
    return lax.ppermute(x, axis, [(i, i ^ (1 << bit)) for i in range(n)])


def shift(x, axis, rel):
    n = lax.axis_size(axis)
    return lax.ppermute(x, axis, [(i, i ^ rel) for i in range(n)])


def turn(x, axis):
    n = lax.axis_size(axis)
    return lax.ppermute(x, axis, [(i, (i + 1) % n) for i in range(n)])


def take(x, index, n):
    return lax.dynamic_slice_in_dim(x, index * n, n, 0)


def bits(axis):
    return lax.axis_size(axis).bit_length() - 1


def group_sum(x):
    for b in range(2, bits("dp")):
        x = x + flip(x, "dp", b)
    return x


def column_half(x, index):
    n = x.shape[1] // 2
    return lax.dynamic_slice_in_dim(x, index * n, n, 1)


def column_block(x, index):
    n = x.shape[1] // lax.axis_size("hid")
    return lax.dynamic_slice_in_dim(x, index * n, n, 1)


def place_columns(parts, zed, reverse=False):
    n = parts[0].shape[1]
    out = jnp.zeros((parts[0].shape[0], n * len(parts)), parts[0].dtype)
    top = bits("hid") - 1
    for rel, x in enumerate(parts):
        index = zed ^ rel
        if reverse:
            index = sum(((index >> b) & 1) << (top - b) for b in range(top + 1))
        out = lax.dynamic_update_slice_in_dim(out, x, index * n, 1)
    return out


def in_order(parts, index):
    held = jnp.zeros((len(parts),) + parts[0].shape, parts[0].dtype)
    for rel, x in enumerate(parts):
        held = lax.dynamic_update_slice_in_dim(held, x[None], index ^ rel, 0)
    return jnp.sum(held.astype(f32), axis=0).astype(parts[0].dtype)


def sort_rows(x, y, mine):
    return jnp.where(mine == 0, jnp.concatenate([x, y]), jnp.concatenate([y, x]))


def add_rows(x, rider):
    rows = rider.reshape(-1, x.shape[1])
    pad = -rows.shape[0] % 16
    return jnp.concatenate([x, rows, jnp.zeros((pad, x.shape[1]), x.dtype)])


def cut_rows(x, n, shape):
    width = x.shape[1]
    return x[:n], x[n : n + shape[0] * shape[1] // width].reshape(shape)


def plane_sends(x, spot):
    n = x.shape[0] // 4
    return [take(x, spot ^ rel, n) for rel in (1, 2, 3)], take(x, spot, n)


def plane_near(sends):
    return [shift(x, "dp", rel) for rel, x in zip((1, 2, 3), sends)]


def per_device(
    tokens, clusters, key_mask, query_key_value_weight, attention_output_weight, up_weight,
    down_weight, gain_one, shift_one, gain_two, shift_two, cotangent,
):
    rows, width = tokens.shape
    half = width // 2
    hidden = up_weight.shape[1]
    ring = lax.axis_size("hid")
    core = lax.axis_index("mod")
    spot = lax.rem(lax.axis_index("dp"), 4)
    spot_bits = (spot & 1, spot >> 1)

    quarter = take(up_weight, spot, half // 4)
    piece = jnp.concatenate(
        [quarter[:, m : m + half] for m in range(0, hidden, half)]
        + [take(down_weight, spot, hidden // 4)]
    )
    up_other, down_other = flip(up_weight, "mod", 0), flip(down_weight, "mod", 0)
    slots = [
        [
            (up_weight, ("up", 0, None)),
            (down_weight, ("down", 0, None)),
            (up_other, ("up", 1, None)),
            (down_other, ("down", 1, None)),
        ]
    ]

    cl3 = clusters.reshape(rows, STEPS, GROUP).transpose(1, 0, 2)
    keep = key_mask.reshape(rows, 1)
    vec = lambda x: x.reshape(1, width)
    g1, s1, g2, s2 = vec(gain_one), vec(shift_one), vec(gain_two), vec(shift_two)
    wqkv, wo = query_key_value_weight, attention_output_weight

    kv, qkvt, n1t, token = project(tokens, wqkv, g1, s1, after=[piece])

    def spread(x):
        return [shift(x, "dp", rel) for rel in (1, 2, 3)]

    def held_slot(x, near, token):
        held = [x] + near
        both = behind(jnp.concatenate(held), token)
        return both, [(v, ("piece", 0, rel)) for rel, v in enumerate(held)] + [
            (flip(both, "mod", 0), ("pieces", 1, None))
        ]

    def plane(part, token):
        n = part.shape[1] // 2
        sends = [behind(take(part[i], 1 - spot_bits[i], n), token) for i in (0, 1)]
        keep = [take(part[i], spot_bits[i], n) for i in (0, 1)]
        return keep, [flip(sends[i], "dp", i) for i in (0, 1)], sends

    def finish_plane(launched, token):
        keep, got, _ = launched
        return jnp.stack([a + behind(b, token) for a, b in zip(keep, got)])

    x = behind(turn(piece, "hid"), token)
    near = spread(x)
    far = turn(x, "hid")
    mixed, prob, cen, cnt, inv, res, n2, token = attend(
        tokens, kv, qkvt, cl3, keep, wo, g2, s2, after=[x, up_other, down_other]
    )
    n_slots = ring
    gn2, branches = None, []
    raw, part, share = [None] * n_slots, [None] * n_slots, [None] * n_slots
    for s in range(n_slots):
        first = []
        if s + 1 < n_slots:
            both, slot = held_slot(x, near, token)
            slots.append(slot)
            first += near + [both]
        if s + 2 < n_slots:
            x = behind(far, token)
            near = spread(x)
            first.append(x)
        if s + 3 < n_slots:
            far = turn(x, "hid")
        if s >= 1:
            got = flip(raw[s - 1][1], "mod", 0)
        if s >= 2:
            share[s - 2] = plane(part[s - 2], token)
            first += share[s - 2][2]
        if s >= 3:
            first += share[s - 3][1]
        br, gn2, own, other, token = feed_forward(
            n2, cotangent, slots[s], gn2, hidden, after=first
        )
        branches.append(br)
        raw[s] = (own, other)
        if s >= 1:
            part[s - 1] = raw[s - 1][0] + behind(got, token)
    last = n_slots - 1
    got = flip(raw[last][1], "mod", 0)
    share[last - 1] = plane(part[last - 1], token)
    share = [finish_plane(x, token) for x in share[: last - 1]] + share[last - 1 :]
    one = turn(share[1], "hid")
    gmt, ga, go_own, go_other, vecs_two, token = residual_back(
        gn2, cotangent, res, mixed, wo, g2,
        after=share[last - 2 : last - 1] + share[last - 1][2],
    )
    part[last] = raw[last][0] + behind(got, token)
    share[last] = plane(part[last], token)
    gs, ws = [None] * STEPS, [None] * STEPS
    heads = functools.partial(
        heads_back,
        n1t=n1t, gmt=gmt, qkvt=qkvt, kv=kv, prob=prob, cen=cen, cnt=cnt, inv=inv, cl3=cl3,
    )
    gs[0], own, other, after0 = heads(0, after=share[last - 1][1] + share[last][2])
    share[last - 1] = finish_plane(share[last - 1], token)
    early_send = jnp.concatenate([go_other, other], axis=1)
    early = jnp.concatenate([go_own, own], axis=1)
    early_got = flip(early_send, "mod", 0)
    total = behind(one, after0) + share[2 % ring]
    one = turn(total, "hid")
    gs[1], own1, other1, after1 = heads(1, after=[early_send, total] + share[last][1])
    share[last] = finish_plane(share[last], after1)
    early = early + behind(early_got, after1)
    n = half // 4
    zed = lax.axis_index("hid")
    z_bits = [(zed >> b) & 1 for b in range(bits("hid"))]
    early_sends, early = plane_sends(early, spot)
    early_near = plane_near(early_sends)
    late_got = flip(other1, "mod", 0)
    gs[2], own2, other2, after2 = heads(2, after=early_sends)

    for s in range(3, ring):
        total = behind(one, after2) + share[s]
        one = turn(total, "hid")
    output = behind(res, after2).astype(f32)
    for x in branches:
        output = output + x.astype(f32)
    output = output.astype(bf16)
    token = fence(after2, output, total, late_got, *early_near)
    late_got2 = flip(behind(other2, token), "mod", 0)
    late_left = own1 + behind(late_got, token)
    late_right = own2 + late_got2
    late_sends, late = plane_sends(jnp.concatenate([late_left, late_right], axis=1), spot)
    late_near = plane_near(late_sends)
    early = group_sum(behind(early, token) + early_near[0] + early_near[1] + early_near[2])
    send = column_half(early, 1 - z_bits[0])
    got = flip(send, "hid", 0)
    input_grad, vecs_one, after3 = project_back(
        gs, wqkv, tokens, ga, g1, after=[*late_sends, send, late_got2]
    )
    early = column_half(early, z_bits[0]) + behind(got, after3)
    for b in range(1, bits("hid")):
        send = column_half(early, 1 - z_bits[b])
        early = column_half(early, z_bits[b]) + flip(send, "hid", b)
    vecs = jnp.concatenate([vecs_one[:2], vecs_two[:2]]).astype(bf16)
    vecs = vecs + flip(vecs, "mod", 0)
    total = behind(one, zero_of(send)) + share[0]
    keeps = [take(x, spot_bits[i], x.shape[0] // 2) for x, i in zip(total, (1, 0))]
    gots = [
        flip(take(x, 1 - spot_bits[i], x.shape[0] // 2), "dp", i) for x, i in zip(total, (1, 0))
    ]
    token = fence(early, vecs, *late_near)
    late = group_sum(late + behind(late_near[0], token) + late_near[1] + late_near[2])
    late_z = [column_block(late, zed ^ rel) for rel in range(lax.axis_size("hid"))]
    sends = [add_rows(x, vecs) for x in late_z[1:]]
    got = [shift(x, "hid", rel + 1) for rel, x in enumerate(sends)]
    early = behind(early, token)
    early_z = [early] + [shift(early, "hid", rel) for rel in range(1, lax.axis_size("hid"))]
    early = place_columns(early_z, zed, reverse=True)
    mine = [group_sum(x + behind(y, token)) for x, y in zip(keeps, gots)]
    gots = [flip(x, "dp", i) for x, i in zip(mine, (1, 0))]
    token = fence(early)
    early = behind(early, token)
    early_near = plane_near([early] * 3)
    got = [cut_rows(x, late.shape[0], vecs.shape) for x in got]
    late = late_z[0]
    for x, _ in got:
        late = late + behind(x, token)
    vecs = in_order([vecs] + [x for _, x in got], zed)
    mine = [
        sort_rows(x, behind(y, token), spot_bits[i]) for x, y, i in zip(mine, gots, (1, 0))
    ]
    late_z = [late] + [shift(late, "hid", rel) for rel in range(1, lax.axis_size("hid"))]
    gots = [flip(x, "dp", i) for x, i in zip(mine, (0, 1))]
    token = fence(*early_near)
    token = fence(token, *late_z)
    loaded = add_rows(behind(place_columns(late_z, zed), token), group_sum(vecs))
    late_near = plane_near([loaded] * 3)
    early = [behind(x, token) for x in [early] + early_near]
    early_got = [flip(x, "mod", 0) for x in early]
    grad_out, first, grad_in, grad_back, token = finish(
        core, spot, early, early_got, mine, gots, half, hidden
    )
    pieces = [loaded] + [behind(x, token) for x in late_near]
    got = [flip(x, "mod", 0) for x in pieces]
    gqkv, vecs = assemble(core, spot, first, pieces, got)
    return (
        output,
        input_grad,
        gqkv,
        grad_out,
        grad_in,
        grad_back,
        vecs[0],
        vecs[1],
        vecs[2],
        vecs[3],
    )


def solution(mesh):
    every = P(("dp", "hid", "mod"), None)
    placed = (
        every, every, P(("dp", "hid", "mod")), P(), P(), P("mod", "hid"), P("hid", "mod"),
        P(), P(), P(), P(), every,
    )
    return jax.shard_map(
        per_device,
        mesh=mesh,
        in_specs=placed,
        out_specs=(every, every, P(), P(), P("mod", "hid"), P("hid", "mod"), P(), P(), P(), P()),
        check_vma=False,
    )
```
